256 devices in a mesh: section: 4 (over z_hi, core), dp: 64 (over y, z_lo, x).
Axes of the slice: x: 4, y: 4, z: 8 (z_hi: 2, z_lo: 4; z = z_hi * 4 + z_lo), core: 2. Of those that a mesh axis runs over, the one named last changes fastest.
Arguments:
- stash: bfloat16 [4, 8192, 3072], P('section', 'dp'), may hold values from -16 to 16
- cotangent: bfloat16 [8192, 3072], P('dp'), may hold values from -6 to 6
- domain_ids: int32 [64], P('dp'), may hold values from 0 to 3, never falling along the last dimension, each value on 1 to 32 neighbouring positions
- shared_weight: bfloat16 [4, 3072, 256], P('section', 'dp'), may hold values from 0.5 to 2
- domain_weight: bfloat16 [4, 4, 3072, 256], P('section', None, 'dp'), may hold values from -0.375 to 0.375
- shared_bias: bfloat16 [4, 3072], P('section', 'dp'), may hold values from -3 to 3
- domain_bias: bfloat16 [4, 4, 3072], P('section', None, 'dp'), may hold values from -3 to 3
Outputs:
- d_inputs: bfloat16 [4, 8192, 3072], P('section', 'dp')
- d_shared: float32 [4, 3072, 256], P('section', 'dp')
- d_domain: float32 [4, 4, 3072, 256], P('section', None, 'dp')
- d_bias_shared: float32 [4, 3072], P('section', 'dp')
- d_bias_domain: float32 [4, 4, 3072], P('section', None, 'dp')
The draws below stay inside these ranges and needn't reach their ends.
Inputs may be any that keep to these rules, and one draw needn't show every extreme that they name: `domain_ids`: never falls from one micro-batch to the next; each of the 4 domains holds at least one micro-batch.
All inputs are finite; a program needn't handle non-finite values.
Results may differ from the reference program's by a relative error of at most 0.0077.
Values may be sent and summed in bfloat16 or wider, within the bound.
No kernel may reach another device: no remote copies, remote signals or barrier semaphores. Data moves between devices by JAX's collectives and lax.ppermute only.
A program may use at most 192 MiB of HBM per device.

```python
import math
import jax
import jax.numpy as jnp
import numpy as np
from jax import lax

D = 3072
GS = 256
DOMAINS = 4
ROWS = 128
MICRO = 64
TOKENS = 8192
N_SECTION = 4


def with_spikes(result, stream_key, source, target, shards_of, factor):
    def block_of(dim):
        return (jnp.arange(result.shape[dim]) // (result.shape[dim] // shards_of)).reshape((-1,) + (1,) * (result.ndim - 1 - dim))

    one_side = jax.random.permutation(stream_key, shards_of)[block_of(target)]
    far = (block_of(target) + shards_of // 2) % shards_of
    return jnp.where((block_of(source) == one_side) | (block_of(source) == far), factor * result, result)


def block_levels(rng, shape, cuts, least, largest):
    level = 1.0
    for dim, shards_of in cuts:
        heights = jax.random.uniform(jax.random.fold_in(jax.random.fold_in(rng, 6), dim), (shards_of,), jnp.float32, least / len(cuts), largest / len(cuts))
        level = level * jnp.repeat(jnp.exp(heights), shape[dim] // shards_of).reshape((-1,) + (1,) * (len(shape) - 1 - dim))
    return level


def profile(number_of, total, bound, skew):
    portions = [(1 << 20) // math.isqrt(rank ** skew) + 1 for rank in range(2, number_of + 1)]
    spare, holding = total - bound - (number_of - 1), [1] * (number_of - 1)
    while spare > 0:
        free = [i for i in range(number_of - 1) if holding[i] < bound]
        mass, left = sum([portions[i] for i in free]), spare
        for i in free:
            more = min(bound - holding[i], max(1, left * portions[i] // mass), spare)
            holding[i] = holding[i] + more
            spare = spare - more
    return np.array([bound] + holding)


def ragged_sizes(stream_key, amount, total, most, skew):
    if amount == 2:
        one = jax.random.randint(stream_key, (), max(1, total - most), min(most, total - 1) + 1)
        return jnp.stack([one, total - one])
    lengths = jnp.asarray(profile(amount, total, most, skew), jnp.int32)
    twos = (amount - 1) // 2
    donor, taker = lengths[1:1 + 2 * twos:2], lengths[2:2 + 2 * twos:2]
    margin = jnp.minimum(donor - 1, most - taker)
    shifted = jax.random.randint(jax.random.fold_in(stream_key, 1), (twos,), 0, 1 << 20) % (margin + 1)
    lengths = lengths.at[1:1 + 2 * twos:2].set(donor - shifted).at[2:2 + 2 * twos:2].set(taker + shifted)
    return lengths[jax.random.permutation(jax.random.fold_in(stream_key, 2), amount)]


def normal_values(own_key, dims, deviation, limit, pieces=(), dtype=jnp.bfloat16):
    result = jax.random.normal(own_key, dims, jnp.float32) * deviation
    if len(pieces) > 0:
        result = block_levels(own_key, dims, pieces, -0.22, 0.18) * result
    return jnp.clip(result, min=-limit, max=limit).astype(dtype)


def noise_with(rng, shape, spread, reach, pieces, heavy, kind=jnp.bfloat16):
    array = spread * jax.random.normal(rng, shape, jnp.float32)
    if pieces:
        array = array * block_levels(rng, shape, pieces, -0.22, 0.18)
    return jnp.clip(with_spikes(array, jax.random.fold_in(rng, 3), *heavy), -reach, reach).astype(kind)


def setup_inputs(seed: int = 0) -> dict:
    key_of = jax.random.split(jax.random.key(seed), 8)
    stash = noise_with(key_of[0], (N_SECTION, TOKENS, D), 1.0, 16.0, ((0, 4), (1, 64)), (1, 2, 64, 4.0))
    cotangent = normal_values(key_of[1], (TOKENS, D), 1.0, 6.0, ((0, 64),))
    domain_ids = jnp.searchsorted(jnp.cumsum(ragged_sizes(key_of[2], DOMAINS, MICRO, 2 * MICRO // DOMAINS, 0)), jnp.arange(MICRO), side="right").astype(jnp.int32)
    shared_weight = jnp.clip(jnp.exp(math.log(2.0) - 1.3862944 * jax.random.uniform(key_of[3], (N_SECTION, D, GS), jnp.float32) ** block_levels(key_of[3], (N_SECTION, D, GS), ((0, 4), (1, 64)), -0.2, 0.2)), 0.5, 2.0).astype(jnp.bfloat16)
    domain_weight = normal_values(key_of[4], (N_SECTION, DOMAINS, D, GS), GS ** -0.5, 0.375, ((0, 4), (2, 64)))
    shared_bias = normal_values(key_of[5], (N_SECTION, D), 0.5, 3.0, ((0, 4), (1, 64)))
    domain_bias = normal_values(key_of[6], (N_SECTION, DOMAINS, D), 0.5, 3.0, ((0, 4), (2, 64)))
    return {"stash": stash, "cotangent": cotangent, "domain_ids": domain_ids, "shared_weight": shared_weight, "domain_weight": domain_weight, "shared_bias": shared_bias, "domain_bias": domain_bias}


def grouped_forward(inputs, weights, groups):
    count = inputs.shape[0]
    split_in = inputs.reshape(count, groups, -1).astype(jnp.float32)
    return jnp.einsum("rgi,gio->rgo", split_in, weights.astype(jnp.float32)).reshape(count, -1)


def grouped_back(signal, weights, groups):
    count = signal.shape[0]
    split_sig = signal.reshape(count, groups, -1).astype(jnp.float32)
    return jnp.einsum("rgo,gio->rgi", split_sig, weights.astype(jnp.float32)).reshape(count, -1)


def grouped_outer(inputs, signal, groups):
    count = inputs.shape[0]
    split_in = inputs.reshape(count, groups, -1).astype(jnp.float32)
    split_sig = signal.reshape(count, groups, -1).astype(jnp.float32)
    return jnp.einsum("rgi,rgo->gio", split_in, split_sig)


def reference(stash, cotangent, domain_ids, shared_weight, domain_weight, shared_bias, domain_bias):
    groups = D // GS
    effective = (shared_weight[:, None].astype(jnp.float32) * domain_weight.astype(jnp.float32)).astype(jnp.bfloat16)
    offsets = shared_bias[:, None].astype(jnp.float32) + domain_bias.astype(jnp.float32)
    upstream = cotangent
    grads_in = []
    grads_shared = []
    grads_domain = []
    grads_bias_shared = []
    grads_bias_domain = []
    for layer in range(N_SECTION - 1, -1, -1):
        kernels = effective[layer].reshape(DOMAINS, groups, GS, GS)
        shifts = offsets[layer]

        def advance(carry, item, kernels=kernels, shifts=shifts):
            grad_kernel, grad_shift = carry
            inputs, incoming, domain = item
            kernel = kernels[domain]
            pre = grouped_forward(inputs, kernel, groups) + shifts[domain][None]
            sigma = jax.nn.sigmoid(pre)
            slope = sigma * (1.0 + pre * (1.0 - sigma))
            signal = (incoming.astype(jnp.float32) * slope).astype(jnp.bfloat16)
            outgoing = (incoming.astype(jnp.float32) + grouped_back(signal, kernel, groups)).astype(jnp.bfloat16)
            grad_kernel = grad_kernel.at[domain].add(grouped_outer(inputs, signal, groups))
            grad_shift = grad_shift.at[domain].add(jnp.sum(signal.astype(jnp.float32), axis=0))
            return (grad_kernel, grad_shift), outgoing

        start = (jnp.zeros((DOMAINS, groups, GS, GS), jnp.float32), jnp.zeros((DOMAINS, D), jnp.float32))
        items = (stash[layer].reshape(MICRO, ROWS, D), upstream.reshape(MICRO, ROWS, D), domain_ids)
        (grad_kernel, grad_shift), blocks = lax.scan(advance, start, items)
        upstream = blocks.reshape(TOKENS, D)
        flat_grad = grad_kernel.reshape(DOMAINS, D, GS)
        grads_in.append(upstream)
        grads_shared.append(jnp.sum(flat_grad * domain_weight[layer].astype(jnp.float32), axis=0))
        grads_domain.append(flat_grad * shared_weight[layer].astype(jnp.float32)[None])
        grads_bias_shared.append(jnp.sum(grad_shift, axis=0))
        grads_bias_domain.append(grad_shift)
    return (jnp.stack(grads_in[::-1]), jnp.stack(grads_shared[::-1]), jnp.stack(grads_domain[::-1]), jnp.stack(grads_bias_shared[::-1]), jnp.stack(grads_bias_domain[::-1]))
```

```python
import jax
import jax.numpy as jnp
from jax import lax
from jax.experimental import pallas as pl
from jax.experimental.pallas import tpu as pltpu
from jax.sharding import Mesh, PartitionSpec as P

D = 3072
GS = 256
DOMAINS = 4
ROWS = 128
NY, NZ, NX = 4, 4, 4
SHARD = 48
SLAB = D // NY
SG = SLAB // GS
PIECE = NZ * SHARD
TILE = 16
BLOCK = PIECE + TILE
VMEM = pl.BlockSpec(memory_space=pltpu.VMEM)
SMEM = pl.BlockSpec(memory_space=pltpu.SMEM)
BF = jnp.bfloat16
F32 = jnp.float32


def params():
    return pltpu.CompilerParams(vmem_limit_bytes=48 * 1024 * 1024)


def cost(flops, bytes_accessed):
    return pl.CostEstimate(flops=flops, bytes_accessed=bytes_accessed, transcendentals=0)


def prep_kernel(sw, dw, tile, out):
    shared = sw[...].astype(F32)
    for k in range(DOMAINS):
        product = (shared * dw[k].astype(F32)).astype(BF)
        for z in range(NZ):
            out[z, k * SHARD : (k + 1) * SHARD, :] = product
    for z in range(NZ):
        out[z, PIECE:, :] = tile[...]


def prep(sw, dw, tile):
    return pl.pallas_call(
        prep_kernel,
        out_shape=jax.ShapeDtypeStruct((NZ, BLOCK, GS), BF),
        in_specs=[VMEM, VMEM, VMEM],
        out_specs=VMEM,
        cost_estimate=cost(10**5, 10**6),
        name="prep",
    )(sw, dw, tile)


def pick_kernel(ids, held, out):
    step = pl.program_id(0)
    tile = held[0, PIECE:, :].astype(F32)
    for z in range(1, NZ):
        tile = tile + held[z, PIECE:, :].astype(F32)
    tile = tile.astype(BF)
    for i in range(NX):
        start = pl.multiple_of(ids[step * NX + i, 0] * SHARD, TILE)
        for z in range(NZ):
            out[i, z * SHARD : (z + 1) * SHARD, :] = held[z, pl.ds(start, SHARD), :]
        out[i, PIECE:, :] = tile


def pick(ids, held):
    return pl.pallas_call(
        pick_kernel,
        grid=(NY,),
        out_shape=jax.ShapeDtypeStruct((NY * NX, BLOCK, GS), BF),
        in_specs=[SMEM, pl.BlockSpec((NZ, BLOCK, GS), lambda i: (0, 0, 0))],
        out_specs=pl.BlockSpec((NX, BLOCK, GS), lambda i: (i, 0, 0)),
        cost_estimate=cost(10**5, 2 * 10**6),
        name="pick",
    )(ids, held)


def slope_kernel(own, got, x, slope, kernel, offsets):
    domain = own[0]
    tile = got[0, PIECE:, :].astype(F32)
    for i in range(1, NX):
        tile = tile + got[i, PIECE:, :].astype(F32)
    offsets[...] = tile
    for z in range(NZ):
        for i in range(NX):
            at = (z * NX + i) * SHARD
            kernel[at : at + SHARD, :] = got[i, z * SHARD : (z + 1) * SHARD, :]
    for q in range(SG):
        lanes = slice(q * GS, (q + 1) * GS)
        offset = offsets[q : q + 1, :] + offsets[pl.ds((1 + domain) * SG + q, 1), :]
        pre = jnp.dot(x[:, lanes], kernel[lanes, :], preferred_element_type=F32) + offset
        sigma = jax.nn.sigmoid(pre)
        slope[:, lanes] = sigma * (1.0 + pre * (1.0 - sigma))


def slopes(own, got, x):
    return pl.pallas_call(
        slope_kernel,
        grid=(NY,),
        out_shape=(
            jax.ShapeDtypeStruct((ROWS, D), F32),
            jax.ShapeDtypeStruct((D, GS), BF),
        ),
        in_specs=[
            SMEM,
            pl.BlockSpec((NX, BLOCK, GS), lambda i: (i, 0, 0)),
            pl.BlockSpec((ROWS, SLAB), lambda i: (0, i)),
        ],
        out_specs=(
            pl.BlockSpec((ROWS, SLAB), lambda i: (0, i)),
            pl.BlockSpec((SLAB, GS), lambda i: (i, 0)),
        ),
        scratch_shapes=[pltpu.VMEM((TILE, GS), F32)],
        compiler_params=params(),
        cost_estimate=cost(2 * 10**8, 6 * 10**6),
        name="slopes",
    )(own, got, x)


def back_product(signal, kernel):
    return lax.dot_general(
        signal, kernel, (((1,), (1,)), ((), ())), preferred_element_type=F32
    )


def chain_kernel(up, slope, kernel, out):
    for q in range(SG):
        lanes = slice(q * GS, (q + 1) * GS)
        above = up[:, lanes].astype(F32)
        signal = (above * slope[:, lanes]).astype(BF)
        out[:, lanes] = (above + back_product(signal, kernel[lanes, :])).astype(BF)


def chain(up, slope, kernel):
    wide = pl.BlockSpec((ROWS, SLAB), lambda i: (0, i))
    return pl.pallas_call(
        chain_kernel,
        grid=(NY,),
        out_shape=jax.ShapeDtypeStruct((ROWS, D), BF),
        in_specs=[wide, wide, pl.BlockSpec((SLAB, GS), lambda i: (i, 0))],
        out_specs=wide,
        compiler_params=params(),
        cost_estimate=cost(2 * 10**8, 5 * 10**6),
        name="chain",
    )(up, slope, kernel)


def grads_kernel(section, up3, up2, up1, up0, slope, kernel, x, out, send, tile):
    s = section[0]
    tile[...] = jnp.zeros_like(tile)
    for q in range(SG):
        lanes = slice(q * GS, (q + 1) * GS)
        up = jnp.where(
            s == 3,
            up3[:, lanes],
            jnp.where(s == 2, up2[:, lanes], jnp.where(s == 1, up1[:, lanes], up0[:, lanes])),
        )
        above = up.astype(F32)
        signal = (above * slope[:, lanes]).astype(BF)
        out[:, lanes] = (above + back_product(signal, kernel[lanes, :])).astype(BF)
        grad = lax.dot_general(
            x[:, lanes], signal, (((0,), (0,)), ((), ())), preferred_element_type=F32
        ).astype(BF)
        for u in range(GS // TILE):
            row = q * GS + u * TILE
            shard, inner = row // SHARD, row % SHARD
            z, i = shard // NX, shard % NX
            at = z * SHARD + inner
            send[i, at : at + TILE, :] = grad[u * TILE : (u + 1) * TILE, :]
        total = jnp.sum(signal.astype(F32), axis=0, keepdims=True)
        high = total.astype(BF).astype(F32)
        tile[q : q + 1, :] = high
        tile[SG + q : SG + q + 1, :] = total - high
    for i in range(NX):
        send[i, PIECE:, :] = tile[...].astype(BF)


def grads(section, ups, slope, kernel, x):
    wide = pl.BlockSpec((ROWS, SLAB), lambda i: (0, i))
    return pl.pallas_call(
        grads_kernel,
        grid=(NY,),
        out_shape=(
            jax.ShapeDtypeStruct((ROWS, D), BF),
            jax.ShapeDtypeStruct((NY * NX, BLOCK, GS), BF),
        ),
        in_specs=[SMEM] + [wide] * 5 + [pl.BlockSpec((SLAB, GS), lambda i: (i, 0)), wide],
        out_specs=(wide, pl.BlockSpec((NX, BLOCK, GS), lambda i: (i, 0, 0))),
        scratch_shapes=[pltpu.VMEM((TILE, GS), F32)],
        compiler_params=params(),
        cost_estimate=cost(4 * 10**8, 8 * 10**6),
        name="grads",
    )(section, *ups, slope, kernel, x)


def merge_kernel(ids, got, out, total, tile):
    step = pl.program_id(0)

    @pl.when(step == 0)
    def _():
        total[...] = jnp.zeros_like(total)

    for i in range(NX):
        domain = ids[step * NX + i, 0]
        total[domain] += got[i].astype(F32)

    @pl.when(step == NY - 1)
    def _():
        tile[...] = jnp.zeros_like(tile)
        for k in range(DOMAINS):
            for z in range(NZ):
                out[z, k * SHARD : (k + 1) * SHARD, :] = total[
                    k, z * SHARD : (z + 1) * SHARD, :
                ].astype(BF)
            tile[k * SG : (k + 1) * SG, :] = (
                total[k, PIECE : PIECE + SG, :] + total[k, PIECE + SG : PIECE + 2 * SG, :]
            )
        for z in range(NZ):
            out[z, PIECE:, :] = tile[...].astype(BF)


def merge(ids, got):
    return pl.pallas_call(
        merge_kernel,
        grid=(NY,),
        out_shape=jax.ShapeDtypeStruct((NZ, BLOCK, GS), BF),
        in_specs=[SMEM, pl.BlockSpec((NX, BLOCK, GS), lambda i: (i, 0, 0))],
        out_specs=pl.BlockSpec((NZ, BLOCK, GS), lambda i: (0, 0, 0)),
        scratch_shapes=[pltpu.VMEM((DOMAINS, BLOCK, GS), F32), pltpu.VMEM((TILE, GS), F32)],
        compiler_params=params(),
        cost_estimate=cost(10**6, 2 * 10**6),
        name="merge",
    )(ids, got)


def finish_kernel(got, sw, dw, d_shared, d_domain, bias):
    shared = sw[...].astype(F32)
    summed = jnp.zeros((SHARD, GS), F32)
    for k in range(DOMAINS):
        rows = slice(k * SHARD, (k + 1) * SHARD)
        share = got[0, rows, :].astype(F32)
        for z in range(1, NZ):
            share = share + got[z, rows, :].astype(F32)
        summed = summed + share * dw[k].astype(F32)
        d_domain[k] = share * shared
    d_shared[...] = summed
    tile = got[0, PIECE:, :].astype(F32)
    for z in range(1, NZ):
        tile = tile + got[z, PIECE:, :].astype(F32)
    bias[...] = tile


def finish(got, sw, dw):
    return pl.pallas_call(
        finish_kernel,
        out_shape=(
            jax.ShapeDtypeStruct((SHARD, GS), F32),
            jax.ShapeDtypeStruct((DOMAINS, SHARD, GS), F32),
            jax.ShapeDtypeStruct((TILE, GS), F32),
        ),
        in_specs=[VMEM, VMEM, VMEM],
        out_specs=(VMEM, VMEM, VMEM),
        cost_estimate=cost(10**6, 10**6),
        name="finish",
    )(got, sw, dw)


def exchange(block, axes):
    return lax.all_to_all(block, axes, 0, 0, tiled=True)


def body(stash, cotangent, domain_ids, shared_weight, domain_weight, shared_bias, domain_bias):
    x = stash[0]
    sw, dw = shared_weight[0], domain_weight[0]
    section = 2 * lax.axis_index("zhi") + lax.axis_index("core")
    place = PIECE * lax.axis_index("zlo") + SHARD * lax.axis_index("x")

    biases = jnp.concatenate([shared_bias, domain_bias[0]], axis=0)
    spread = lax.dynamic_update_slice(jnp.zeros((5, SLAB), BF), biases, (0, place))
    tile = jnp.pad(spread.reshape(5 * SG, GS), ((0, 1), (0, 0)))

    plane_ids = exchange(
        jnp.broadcast_to(domain_ids[0], (NY * NX, 1, 128)), ("y", "x")
    ).reshape(NY * NX, 128)
    held = exchange(prep(sw, dw, tile), "zlo")
    got = exchange(pick(plane_ids, held), ("y", "x"))
    slope, kernel = slopes(domain_ids, got, x)

    ups = [cotangent]
    for turn in range(3):
        out = chain(ups[-1], slope, kernel)
        ups.append(lax.ppermute(out, ("zhi", "core"), [(3 - turn, 2 - turn)]))

    d_inputs, send = grads(jnp.reshape(section, (1,)), ups, slope, kernel, x)
    merged = merge(plane_ids, exchange(send, ("y", "x")))
    d_shared, d_domain, bias = finish(exchange(merged, "zlo"), sw, dw)
    d_bias = lax.dynamic_slice(
        bias[: DOMAINS * SG].reshape(DOMAINS, SLAB), (0, place), (DOMAINS, SHARD)
    )
    return (
        d_inputs[None],
        d_shared[None],
        d_domain[None],
        jnp.sum(d_bias, axis=0)[None],
        d_bias[None],
    )


def solution(mesh):
    fine = Mesh(mesh.devices.reshape(2, 2, NY, NZ, NX), ("zhi", "core", "y", "zlo", "x"))
    section, dp = ("zhi", "core"), ("y", "zlo", "x")
    in_specs = (
        P(section, dp, None),
        P(dp, None),
        P(dp),
        P(section, dp, None),
        P(section, None, dp, None),
        P(section, dp),
        P(section, None, dp),
    )
    out_specs = (
        P(section, dp, None),
        P(section, dp, None),
        P(section, None, dp, None),
        P(section, dp),
        P(section, None, dp),
    )
    return jax.shard_map(
        body, mesh=fine, in_specs=in_specs, out_specs=out_specs, check_vma=False
    )
```

```python
import jax
import jax.numpy as jnp
from jax import lax
from jax.experimental import pallas as pl
from jax.experimental.pallas import tpu as pltpu
from jax.sharding import Mesh, PartitionSpec as P

D = 3072
GS = 256
DOMAINS = 4
ROWS = 128
NY, NZ, NX = 4, 4, 4
SHARD = 48
SLAB = D // NY
SG = SLAB // GS
PIECE = NZ * SHARD
TILE = 16
BLOCK = PIECE + TILE
HALF = PIECE // 2
PART = HALF + TILE
FIRST = (0, 1)
LAST = (2,)
VMEM = pl.BlockSpec(memory_space=pltpu.VMEM)
SMEM = pl.BlockSpec(memory_space=pltpu.SMEM)
BF = jnp.bfloat16
F32 = jnp.float32


def call(kernel, name, flops, moved, limit=48, **rest):
    return pl.pallas_call(
        kernel,
        name=name,
        compiler_params=pltpu.CompilerParams(vmem_limit_bytes=limit * 1024 * 1024),
        cost_estimate=pl.CostEstimate(flops=flops, bytes_accessed=moved, transcendentals=0),
        **rest,
    )


def prep_kernel(at, sw, dw, sb, db, out, wide, tile):
    shared = sw[...].astype(F32)
    for k in range(DOMAINS):
        out[k * SHARD : (k + 1) * SHARD, :] = (shared * dw[k].astype(F32)).astype(BF)
    wide[...] = jnp.zeros_like(wide)
    wide[0:1, :SHARD] = sb[...].astype(F32)
    wide[1 : 1 + DOMAINS, :SHARD] = db[...].astype(F32)
    placed = pltpu.roll(wide[...], at[0], 1)
    tile[...] = jnp.zeros_like(tile)
    for k in range(1 + DOMAINS):
        for q in range(SG):
            row = k * SG + q
            tile[row : row + 1, :] = placed[k : k + 1, q * GS : (q + 1) * GS]
    out[PIECE:, :] = tile[...].astype(BF)


def prep(at, sw, dw, sb, db):
    return call(
        prep_kernel,
        "prep",
        10**5,
        3 * 10**5,
        out_shape=jax.ShapeDtypeStruct((BLOCK, GS), BF),
        in_specs=[SMEM, VMEM, VMEM, VMEM, VMEM],
        out_specs=VMEM,
        scratch_shapes=[pltpu.VMEM((8, SLAB), F32), pltpu.VMEM((TILE, GS), F32)],
    )(at, sw, dw, sb, db)


def pick_kernel(ids, z, *refs):
    held, out = refs[:NZ], refs[NZ]
    step = pl.program_id(0)
    tile = held[0][PIECE:, :].astype(F32)
    for k in range(1, NZ):
        tile = tile + held[k][PIECE:, :].astype(F32)
    tile = tile.astype(BF)
    for i in range(NX):
        start = pl.multiple_of(ids[step * NX + i, 0] * SHARD, TILE)
        for k in range(NZ):
            to = pl.multiple_of(((z[0] + NZ - k) % NZ) * SHARD, TILE)
            out[i, pl.ds(to, SHARD), :] = held[k][pl.ds(start, SHARD), :]
        out[i, PIECE:, :] = tile


def pick(ids, z, held):
    return call(
        pick_kernel,
        "pick",
        10**5,
        2 * 10**6,
        grid=(NY,),
        out_shape=jax.ShapeDtypeStruct((NY * NX, BLOCK, GS), BF),
        in_specs=[SMEM, SMEM] + [pl.BlockSpec((BLOCK, GS), lambda i: (0, 0))] * NZ,
        out_specs=pl.BlockSpec((NX, BLOCK, GS), lambda i: (i, 0, 0)),
    )(ids, z, *held)


def slope_kernel(own, got, x, slope0, slope1, kernel0, kernel1, kernel, offsets):
    domain = own[0]
    tile = got[0, PIECE:, :].astype(F32)
    for i in range(1, NX):
        tile = tile + got[i, PIECE:, :].astype(F32)
    offsets[...] = tile
    for z in range(NZ):
        for i in range(NX):
            at = (z * NX + i) * SHARD
            kernel[at : at + SHARD, :] = got[i, z * SHARD : (z + 1) * SHARD, :]
    cut = len(FIRST) * GS
    kernel0[...] = kernel[:cut, :]
    kernel1[...] = kernel[cut:, :]
    for q in range(SG):
        lanes = slice(q * GS, (q + 1) * GS)
        offset = offsets[q : q + 1, :] + offsets[pl.ds((1 + domain) * SG + q, 1), :]
        pre = jnp.dot(x[:, lanes], kernel[lanes, :], preferred_element_type=F32) + offset
        sigma = jax.nn.sigmoid(pre)
        slope = sigma * (1.0 + pre * (1.0 - sigma))
        if q in FIRST:
            slope0[:, lanes] = slope
        else:
            slope1[...] = slope


def columns(width):
    return pl.BlockSpec((ROWS, width), lambda i: (0, i))


def rows(height):
    return pl.BlockSpec((height, GS), lambda i: (i, 0))


def slopes(own, got, x):
    w0, w1 = len(FIRST) * GS, len(LAST) * GS
    return call(
        slope_kernel,
        "slopes",
        2 * 10**8,
        6 * 10**6,
        grid=(NY,),
        out_shape=(
            jax.ShapeDtypeStruct((ROWS, NY * w0), F32),
            jax.ShapeDtypeStruct((ROWS, NY * w1), F32),
            jax.ShapeDtypeStruct((NY * w0, GS), BF),
            jax.ShapeDtypeStruct((NY * w1, GS), BF),
        ),
        in_specs=[SMEM, pl.BlockSpec((NX, BLOCK, GS), lambda i: (i, 0, 0)), columns(SLAB)],
        out_specs=(columns(w0), columns(w1), rows(w0), rows(w1)),
        scratch_shapes=[pltpu.VMEM((SLAB, GS), BF), pltpu.VMEM((TILE, GS), F32)],
    )(own, got, x)


def back_product(signal, kernel):
    return lax.dot_general(
        signal, kernel, (((1,), (1,)), ((), ())), preferred_element_type=F32
    )


def first_kernel(section, up, slope, kernel, out, kept):
    for q in range(slope.shape[1] // GS):
        lanes = slice(q * GS, (q + 1) * GS)
        above = jnp.where(section[0] == 3, up[:, lanes].astype(F32), 0.0)
        kept[:, lanes] = above.astype(BF)
        signal = (above * slope[:, lanes]).astype(BF)
        out[:, lanes] = (above + back_product(signal, kernel[lanes, :])).astype(BF)


def next_kernel(before, up, slope, kernel, out, kept):
    for q in range(slope.shape[1] // GS):
        lanes = slice(q * GS, (q + 1) * GS)
        above = before[:, lanes].astype(F32) + up[:, lanes].astype(F32)
        kept[:, lanes] = above.astype(BF)
        signal = (above * slope[:, lanes]).astype(BF)
        out[:, lanes] = (above + back_product(signal, kernel[lanes, :])).astype(BF)


def of_slab(groups):
    if groups == FIRST:
        return columns(SLAB)
    return pl.BlockSpec((ROWS, GS), lambda i: (0, SG * i + LAST[0]))


def chain(groups, head, up, slope, kernel, first=False):
    width = len(groups) * GS
    shape = jax.ShapeDtypeStruct((ROWS, NY * width), BF)
    return call(
        first_kernel if first else next_kernel,
        "chain",
        10**8,
        2 * 10**6,
        grid=(NY,),
        out_shape=(shape, shape),
        in_specs=([SMEM, of_slab(groups)] if first else [columns(width)] * 2)
        + [columns(width), rows(width)],
        out_specs=(columns(width), columns(width)),
    )(head, up, slope, kernel)


def local_grads(before, up, slope, kernel, x, q, tile, row):
    lanes = slice(q * GS, (q + 1) * GS)
    above = before[:, lanes].astype(F32) + up[:, lanes].astype(F32)
    signal = (above * slope[:, lanes]).astype(BF)
    outgoing = (above + back_product(signal, kernel[lanes, :])).astype(BF)
    grad = lax.dot_general(
        x[:, lanes], signal, (((0,), (0,)), ((), ())), preferred_element_type=F32
    ).astype(BF)
    total = jnp.sum(signal.astype(F32), axis=0, keepdims=True)
    high = total.astype(BF).astype(F32)
    tile[row : row + 1, :] = high
    tile[SG + row : SG + row + 1, :] = total - high
    return outgoing, grad


def place_of(row):
    shard, inner = row // SHARD, row % SHARD
    return shard // NX, shard % NX, inner


def grads0_kernel(before, up, slope, kernel, x, out, send, rest, tile):
    tile[...] = jnp.zeros_like(tile)
    for q in FIRST:
        outgoing, grad = local_grads(before, up, slope, kernel, x, q, tile, q)
        out[:, q * GS : (q + 1) * GS] = outgoing
        for u in range(GS // TILE):
            row = q * GS + u * TILE
            z, i, inner = place_of(row)
            if z < NZ // 2:
                at = z * SHARD + inner
                send[i, at : at + TILE, :] = grad[u * TILE : (u + 1) * TILE, :]
            else:
                at = row - 2 * PIECE
                rest[at : at + TILE, :] = grad[u * TILE : (u + 1) * TILE, :]
    for i in range(NX):
        send[i, HALF:, :] = tile[...].astype(BF)


REST = len(FIRST) * GS - 2 * PIECE


def grads0(before, up, slope, kernel, x):
    width = len(FIRST) * GS
    return call(
        grads0_kernel,
        "grads0",
        3 * 10**8,
        6 * 10**6,
        grid=(NY,),
        out_shape=(
            jax.ShapeDtypeStruct((ROWS, NY * width), BF),
            jax.ShapeDtypeStruct((NY * NX, PART, GS), BF),
            jax.ShapeDtypeStruct((NY * REST, GS), BF),
        ),
        in_specs=[columns(width)] * 3 + [rows(width), columns(SLAB)],
        out_specs=(
            columns(width),
            pl.BlockSpec((NX, PART, GS), lambda i: (i, 0, 0)),
            rows(REST),
        ),
        scratch_shapes=[pltpu.VMEM((TILE, GS), F32)],
    )(before, up, slope, kernel, x)


def grads1_kernel(before, up, slope, kernel, x, rest, out0, out, send, tile):
    tile[...] = jnp.zeros_like(tile)
    start = LAST[0] * GS
    out[:, :start] = out0[...]
    outgoing, grad = local_grads(before, up, slope, kernel, x, 0, tile, LAST[0])
    out[:, start:] = outgoing
    for u in range((SLAB - 2 * PIECE) // TILE):
        row = 2 * PIECE + u * TILE
        z, i, inner = place_of(row)
        at = (z - NZ // 2) * SHARD + inner
        if row < start:
            send[i, at : at + TILE, :] = rest[u * TILE : (u + 1) * TILE, :]
        else:
            send[i, at : at + TILE, :] = grad[row - start : row - start + TILE, :]
    for i in range(NX):
        send[i, HALF:, :] = tile[...].astype(BF)


def grads1(before, up, slope, kernel, x, rest, out0):
    width = len(LAST) * GS
    return call(
        grads1_kernel,
        "grads1",
        2 * 10**8,
        4 * 10**6,
        grid=(NY,),
        out_shape=(
            jax.ShapeDtypeStruct((ROWS, D), BF),
            jax.ShapeDtypeStruct((NY * NX, PART, GS), BF),
        ),
        in_specs=[columns(width)] * 3
        + [rows(width), of_slab(LAST), rows(REST), columns(len(FIRST) * GS)],
        out_specs=(columns(SLAB), pl.BlockSpec((NX, PART, GS), lambda i: (i, 0, 0))),
        scratch_shapes=[pltpu.VMEM((TILE, GS), F32)],
    )(before, up, slope, kernel, x, rest, out0)


def add_up(ids, got, total):
    step = pl.program_id(0)

    @pl.when(step == 0)
    def _():
        total[...] = jnp.zeros_like(total)

    for i in range(NX):
        domain = ids[step * NX + i, 0]
        total[domain] += got[i].astype(F32)


def merge0_kernel(ids, got, out, bias, total):
    add_up(ids, got, total)

    @pl.when(pl.program_id(0) == NY - 1)
    def _():
        for k in range(DOMAINS):
            for z in range(NZ // 2):
                out[z, k * SHARD : (k + 1) * SHARD, :] = total[
                    k, z * SHARD : (z + 1) * SHARD, :
                ].astype(BF)
            bias[k] = total[k, HALF:, :]


def merge0(ids, got):
    return call(
        merge0_kernel,
        "merge0",
        10**6,
        10**6,
        grid=(NY,),
        out_shape=(
            jax.ShapeDtypeStruct((NZ // 2, PIECE, GS), BF),
            jax.ShapeDtypeStruct((DOMAINS, TILE, GS), F32),
        ),
        in_specs=[SMEM, pl.BlockSpec((NX, PART, GS), lambda i: (i, 0, 0))],
        out_specs=(
            pl.BlockSpec((NZ // 2, PIECE, GS), lambda i: (0, 0, 0)),
            pl.BlockSpec((DOMAINS, TILE, GS), lambda i: (0, 0, 0)),
        ),
        scratch_shapes=[pltpu.VMEM((DOMAINS, PART, GS), F32)],
    )(ids, got)


def merge1_kernel(ids, z, got, sums, bias, *refs):
    outs, (total, parts, tile) = refs[:NZ], refs[NZ:]
    add_up(ids, got, total)

    @pl.when(pl.program_id(0) == NY - 1)
    def _():
        tile[...] = jnp.zeros_like(tile)
        parts[: NZ // 2] = sums[...]
        for k in range(DOMAINS):
            for half in range(NZ // 2):
                parts[NZ // 2 + half, k * SHARD : (k + 1) * SHARD, :] = total[
                    k, half * SHARD : (half + 1) * SHARD, :
                ].astype(BF)
            both = total[k, HALF:, :] + bias[k]
            tile[k * SG : (k + 1) * SG, :] = both[:SG, :] + both[SG : 2 * SG, :]
        for k in range(NZ):
            outs[k][:PIECE, :] = parts[(z[0] + k) % NZ]
            outs[k][PIECE:, :] = tile[...].astype(BF)


def merge1(ids, z, got, sums, bias):
    def whole(shape):
        return pl.BlockSpec(shape, lambda i: (0,) * len(shape))

    return call(
        merge1_kernel,
        "merge1",
        10**6,
        2 * 10**6,
        grid=(NY,),
        out_shape=(jax.ShapeDtypeStruct((BLOCK, GS), BF),) * NZ,
        in_specs=[
            SMEM,
            SMEM,
            pl.BlockSpec((NX, PART, GS), lambda i: (i, 0, 0)),
            whole((NZ // 2, PIECE, GS)),
            whole((DOMAINS, TILE, GS)),
        ],
        out_specs=(whole((BLOCK, GS)),) * NZ,
        scratch_shapes=[
            pltpu.VMEM((DOMAINS, PART, GS), F32),
            pltpu.VMEM((NZ, PIECE, GS), BF),
            pltpu.VMEM((TILE, GS), F32),
        ],
    )(ids, z, got, sums, bias)


def finish_kernel(at, *refs):
    got, (sw, dw, d_shared, d_domain, b_shared, b_domain, wide) = refs[:NZ], refs[NZ:]
    shared = sw[...].astype(F32)
    summed = jnp.zeros((SHARD, GS), F32)
    for k in range(DOMAINS):
        part = slice(k * SHARD, (k + 1) * SHARD)
        share = got[0][part, :].astype(F32)
        for z in range(1, NZ):
            share = share + got[z][part, :].astype(F32)
        summed = summed + share * dw[k].astype(F32)
        d_domain[k] = share * shared
    d_shared[...] = summed
    tile = got[0][PIECE:, :].astype(F32)
    for z in range(1, NZ):
        tile = tile + got[z][PIECE:, :].astype(F32)
    wide[...] = jnp.zeros_like(wide)
    for k in range(DOMAINS):
        for q in range(SG):
            row = k * SG + q
            wide[k : k + 1, q * GS : (q + 1) * GS] = tile[row : row + 1, :]
    placed = pltpu.roll(wide[...], SLAB - at[0], 1)
    b_domain[...] = placed[:DOMAINS, :SHARD]
    b_shared[...] = jnp.sum(placed[:DOMAINS, :SHARD], axis=0, keepdims=True)


def finish(at, got, sw, dw):
    return call(
        finish_kernel,
        "finish",
        10**6,
        10**6,
        out_shape=(
            jax.ShapeDtypeStruct((SHARD, GS), F32),
            jax.ShapeDtypeStruct((DOMAINS, SHARD, GS), F32),
            jax.ShapeDtypeStruct((1, SHARD), F32),
            jax.ShapeDtypeStruct((DOMAINS, SHARD), F32),
        ),
        in_specs=[SMEM] + [VMEM] * (NZ + 2),
        out_specs=(VMEM,) * 4,
        scratch_shapes=[pltpu.VMEM((8, SLAB), F32)],
    )(at, *got, sw, dw)


def exchange(block, axes):
    return lax.all_to_all(block, axes, 0, 0, tiled=True)


def turned(block, k):
    return lax.ppermute(block, "zlo", [(i, (i + k) % NZ) for i in range(NZ)])


def after(first, *then):
    return lax.optimization_barrier((first, *then))[1:]


def body(stash, cotangent, domain_ids, shared_weight, domain_weight, shared_bias, domain_bias):
    x = stash[0]
    sw, dw = shared_weight[0], domain_weight[0]
    section = jnp.reshape(2 * lax.axis_index("zhi") + lax.axis_index("core"), (1,))
    z = jnp.reshape(lax.axis_index("zlo"), (1,))
    at = PIECE * z + SHARD * lax.axis_index("x")

    own = prep(at, sw, dw, shared_bias, domain_bias[0])
    held = [own] + [turned(own, k) for k in range(1, NZ)]
    (ids,) = after(own, domain_ids)
    plane_ids = exchange(
        jnp.broadcast_to(ids[0], (NY * NX, 1, 128)), ("y", "x")
    ).reshape(NY * NX, 128)
    got = exchange(pick(plane_ids, z, held), ("y", "x"))
    slope0, slope1, kernel0, kernel1 = slopes(domain_ids, got, x)

    def hop(block, turn):
        return lax.ppermute(block, ("zhi", "core"), [(3 - turn, 2 - turn)])

    out0, kept0 = chain(FIRST, section, cotangent, slope0, kernel0, first=True)
    (slope1,) = after(out0, slope1)
    out1, kept1 = chain(LAST, section, cotangent, slope1, kernel1, first=True)
    for turn in range(2):
        up0 = hop(out0, turn)
        up1 = hop(out1, turn)
        (up0,) = after(out1, up0)
        out0, kept0 = chain(FIRST, kept0, up0, slope0, kernel0)
        (up1,) = after(out0, up1)
        out1, kept1 = chain(LAST, kept1, up1, slope1, kernel1)
    up0 = hop(out0, 2)
    up1 = hop(out1, 2)
    (up0,) = after(out1, up0)
    d_in0, send0, rest = grads0(kept0, up0, slope0, kernel0, x)
    got0 = exchange(send0, ("y", "x"))
    (up1,) = after(got0, up1)
    d_inputs, send1 = grads1(kept1, up1, slope1, kernel1, x, rest, d_in0)
    sums0, bias0 = merge0(plane_ids, got0)
    got1 = exchange(send1, ("y", "x"))
    merged = merge1(plane_ids, z, got1, sums0, bias0)
    final = [merged[0]] + [turned(merged[k], k) for k in range(1, NZ)]
    d_shared, d_domain, b_shared, b_domain = finish(at, final, sw, dw)
    return (d_inputs[None], d_shared[None], d_domain[None], b_shared, b_domain[None])


def solution(mesh):
    fine = Mesh(mesh.devices.reshape(2, 2, NY, NZ, NX), ("zhi", "core", "y", "zlo", "x"))
    section, dp = ("zhi", "core"), ("y", "zlo", "x")
    in_specs = (
        P(section, dp, None),
        P(dp, None),
        P(dp),
        P(section, dp, None),
        P(section, None, dp, None),
        P(section, dp),
        P(section, None, dp),
    )
    out_specs = (
        P(section, dp, None),
        P(section, dp, None),
        P(section, None, dp, None),
        P(section, dp),
        P(section, None, dp),
    )
    return jax.shard_map(
        body, mesh=fine, in_specs=in_specs, out_specs=out_specs, check_vma=False
    )
```

```python
import jax
import jax.numpy as jnp
from jax import lax
from jax.experimental import pallas as pl
from jax.experimental.pallas import tpu as pltpu
from jax.sharding import Mesh, PartitionSpec as P

D = 3072
GS = 256
DOMAINS = 4
ROWS = 128
NY, NZ, NX = 4, 4, 4
SHARD = 48
SLAB = D // NY
SG = SLAB // GS
PIECE = NZ * SHARD
TILE = 16
BLOCK = PIECE + TILE
HALF = PIECE // 2
PART = HALF + TILE
FIRST = (0, 1)
LAST = (2,)
VMEM = pl.BlockSpec(memory_space=pltpu.VMEM)
SMEM = pl.BlockSpec(memory_space=pltpu.SMEM)
BF = jnp.bfloat16
F32 = jnp.float32


def call(kernel, name, flops, moved, limit=48, **rest):
    return pl.pallas_call(
        kernel,
        name=name,
        compiler_params=pltpu.CompilerParams(vmem_limit_bytes=limit * 1024 * 1024),
        cost_estimate=pl.CostEstimate(flops=10**11, bytes_accessed=10**9, transcendentals=0),
        **rest,
    )


def prep_kernel(at, sw, dw, sb, db, out, wide, tile):
    shared = sw[...].astype(F32)
    for k in range(DOMAINS):
        out[k * SHARD : (k + 1) * SHARD, :] = (shared * dw[k].astype(F32)).astype(BF)
    wide[...] = jnp.zeros_like(wide)
    wide[0:1, :SHARD] = sb[...].astype(F32)
    wide[1 : 1 + DOMAINS, :SHARD] = db[...].astype(F32)
    placed = pltpu.roll(wide[...], at[0], 1)
    tile[...] = jnp.zeros_like(tile)
    for k in range(1 + DOMAINS):
        for q in range(SG):
            row = k * SG + q
            tile[row : row + 1, :] = placed[k : k + 1, q * GS : (q + 1) * GS]
    out[PIECE:, :] = tile[...].astype(BF)


def prep(at, sw, dw, sb, db):
    return call(
        prep_kernel,
        "prep",
        10**5,
        3 * 10**5,
        out_shape=jax.ShapeDtypeStruct((BLOCK, GS), BF),
        in_specs=[SMEM, VMEM, VMEM, VMEM, VMEM],
        out_specs=VMEM,
        scratch_shapes=[pltpu.VMEM((8, SLAB), F32), pltpu.VMEM((TILE, GS), F32)],
    )(at, sw, dw, sb, db)


def pick_kernel(ids, z, *refs):
    held, out = refs[:NZ], refs[NZ]
    step = pl.program_id(0)
    tile = held[0][PIECE:, :].astype(F32)
    for k in range(1, NZ):
        tile = tile + held[k][PIECE:, :].astype(F32)
    tile = tile.astype(BF)
    for i in range(NX):
        start = pl.multiple_of(ids[step * NX + i, 0] * SHARD, TILE)
        for k in range(NZ):
            to = pl.multiple_of(((z[0] + NZ - k) % NZ) * SHARD, TILE)
            out[i, pl.ds(to, SHARD), :] = held[k][pl.ds(start, SHARD), :]
        out[i, PIECE:, :] = tile


def pick(ids, z, held):
    return call(
        pick_kernel,
        "pick",
        10**5,
        2 * 10**6,
        grid=(NY,),
        out_shape=jax.ShapeDtypeStruct((NY * NX, BLOCK, GS), BF),
        in_specs=[SMEM, SMEM] + [pl.BlockSpec((BLOCK, GS), lambda i: (0, 0))] * NZ,
        out_specs=pl.BlockSpec((NX, BLOCK, GS), lambda i: (i, 0, 0)),
    )(ids, z, *held)


def slope_kernel(own, got, x, slope0, slope1, kernel0, kernel1, kernel, offsets):
    domain = own[0]
    tile = got[0, PIECE:, :].astype(F32)
    for i in range(1, NX):
        tile = tile + got[i, PIECE:, :].astype(F32)
    offsets[...] = tile
    for z in range(NZ):
        for i in range(NX):
            at = (z * NX + i) * SHARD
            kernel[at : at + SHARD, :] = got[i, z * SHARD : (z + 1) * SHARD, :]
    cut = len(FIRST) * GS
    kernel0[...] = kernel[:cut, :]
    kernel1[...] = kernel[cut:, :]
    for q in range(SG):
        lanes = slice(q * GS, (q + 1) * GS)
        offset = offsets[q : q + 1, :] + offsets[pl.ds((1 + domain) * SG + q, 1), :]
        pre = jnp.dot(x[:, lanes], kernel[lanes, :], preferred_element_type=F32) + offset
        sigma = jax.nn.sigmoid(pre)
        slope = sigma * (1.0 + pre * (1.0 - sigma))
        if q in FIRST:
            slope0[:, lanes] = slope
        else:
            slope1[...] = slope


def columns(width):
    return pl.BlockSpec((ROWS, width), lambda i: (0, i))


def rows(height):
    return pl.BlockSpec((height, GS), lambda i: (i, 0))


def slopes(own, got, x):
    w0, w1 = len(FIRST) * GS, len(LAST) * GS
    return call(
        slope_kernel,
        "slopes",
        2 * 10**8,
        6 * 10**6,
        grid=(NY,),
        out_shape=(
            jax.ShapeDtypeStruct((ROWS, NY * w0), F32),
            jax.ShapeDtypeStruct((ROWS, NY * w1), F32),
            jax.ShapeDtypeStruct((NY * w0, GS), BF),
            jax.ShapeDtypeStruct((NY * w1, GS), BF),
        ),
        in_specs=[SMEM, pl.BlockSpec((NX, BLOCK, GS), lambda i: (i, 0, 0)), columns(SLAB)],
        out_specs=(columns(w0), columns(w1), rows(w0), rows(w1)),
        scratch_shapes=[pltpu.VMEM((SLAB, GS), BF), pltpu.VMEM((TILE, GS), F32)],
    )(own, got, x)


def back_product(signal, kernel):
    return lax.dot_general(
        signal, kernel, (((1,), (1,)), ((), ())), preferred_element_type=F32
    )


def first_kernel(section, up, slope, kernel, out, kept):
    for q in range(slope.shape[1] // GS):
        lanes = slice(q * GS, (q + 1) * GS)
        above = jnp.where(section[0] == 3, up[:, lanes].astype(F32), 0.0)
        kept[:, lanes] = above.astype(BF)
        signal = (above * slope[:, lanes]).astype(BF)
        out[:, lanes] = (above + back_product(signal, kernel[lanes, :])).astype(BF)


def next_kernel(before, up, slope, kernel, out, kept):
    for q in range(slope.shape[1] // GS):
        lanes = slice(q * GS, (q + 1) * GS)
        above = before[:, lanes].astype(F32) + up[:, lanes].astype(F32)
        kept[:, lanes] = above.astype(BF)
        signal = (above * slope[:, lanes]).astype(BF)
        out[:, lanes] = (above + back_product(signal, kernel[lanes, :])).astype(BF)


def of_slab(groups):
    if groups == FIRST:
        return columns(SLAB)
    return pl.BlockSpec((ROWS, GS), lambda i: (0, SG * i + LAST[0]))


def chain(groups, head, up, slope, kernel, first=False):
    width = len(groups) * GS
    shape = jax.ShapeDtypeStruct((ROWS, NY * width), BF)
    return call(
        first_kernel if first else next_kernel,
        "chain",
        10**8,
        2 * 10**6,
        grid=(NY,),
        out_shape=(shape, shape),
        in_specs=([SMEM, of_slab(groups)] if first else [columns(width)] * 2)
        + [columns(width), rows(width)],
        out_specs=(columns(width), columns(width)),
    )(head, up, slope, kernel)


def local_grads(before, up, slope, kernel, x, q, tile, row):
    lanes = slice(q * GS, (q + 1) * GS)
    above = before[:, lanes].astype(F32) + up[:, lanes].astype(F32)
    signal = (above * slope[:, lanes]).astype(BF)
    outgoing = (above + back_product(signal, kernel[lanes, :])).astype(BF)
    grad = lax.dot_general(
        x[:, lanes], signal, (((0,), (0,)), ((), ())), preferred_element_type=F32
    ).astype(BF)
    total = jnp.sum(signal.astype(F32), axis=0, keepdims=True)
    high = total.astype(BF).astype(F32)
    tile[row : row + 1, :] = high
    tile[SG + row : SG + row + 1, :] = total - high
    return outgoing, grad


def place_of(row):
    shard, inner = row // SHARD, row % SHARD
    return shard // NX, shard % NX, inner


def grads0_kernel(before, up, slope, kernel, x, out, send, rest, tile):
    tile[...] = jnp.zeros_like(tile)
    for q in FIRST:
        outgoing, grad = local_grads(before, up, slope, kernel, x, q, tile, q)
        out[:, q * GS : (q + 1) * GS] = outgoing
        for u in range(GS // TILE):
            row = q * GS + u * TILE
            z, i, inner = place_of(row)
            if z < NZ // 2:
                at = z * SHARD + inner
                send[i, at : at + TILE, :] = grad[u * TILE : (u + 1) * TILE, :]
            else:
                at = row - 2 * PIECE
                rest[at : at + TILE, :] = grad[u * TILE : (u + 1) * TILE, :]
    for i in range(NX):
        send[i, HALF:, :] = tile[...].astype(BF)


REST = len(FIRST) * GS - 2 * PIECE


def grads0(before, up, slope, kernel, x):
    width = len(FIRST) * GS
    return call(
        grads0_kernel,
        "grads0",
        3 * 10**8,
        6 * 10**6,
        grid=(NY,),
        out_shape=(
            jax.ShapeDtypeStruct((ROWS, NY * width), BF),
            jax.ShapeDtypeStruct((NY * NX, PART, GS), BF),
            jax.ShapeDtypeStruct((NY * REST, GS), BF),
        ),
        in_specs=[columns(width)] * 3 + [rows(width), columns(SLAB)],
        out_specs=(
            columns(width),
            pl.BlockSpec((NX, PART, GS), lambda i: (i, 0, 0)),
            rows(REST),
        ),
        scratch_shapes=[pltpu.VMEM((TILE, GS), F32)],
    )(before, up, slope, kernel, x)


def grads1_kernel(before, up, slope, kernel, x, rest, out0, out, send, tile):
    tile[...] = jnp.zeros_like(tile)
    start = LAST[0] * GS
    out[:, :start] = out0[...]
    outgoing, grad = local_grads(before, up, slope, kernel, x, 0, tile, LAST[0])
    out[:, start:] = outgoing
    for u in range((SLAB - 2 * PIECE) // TILE):
        row = 2 * PIECE + u * TILE
        z, i, inner = place_of(row)
        at = (z - NZ // 2) * SHARD + inner
        if row < start:
            send[i, at : at + TILE, :] = rest[u * TILE : (u + 1) * TILE, :]
        else:
            send[i, at : at + TILE, :] = grad[row - start : row - start + TILE, :]
    for i in range(NX):
        send[i, HALF:, :] = tile[...].astype(BF)


def grads1(before, up, slope, kernel, x, rest, out0):
    width = len(LAST) * GS
    return call(
        grads1_kernel,
        "grads1",
        2 * 10**8,
        4 * 10**6,
        grid=(NY,),
        out_shape=(
            jax.ShapeDtypeStruct((ROWS, D), BF),
            jax.ShapeDtypeStruct((NY * NX, PART, GS), BF),
        ),
        in_specs=[columns(width)] * 3
        + [rows(width), of_slab(LAST), rows(REST), columns(len(FIRST) * GS)],
        out_specs=(columns(SLAB), pl.BlockSpec((NX, PART, GS), lambda i: (i, 0, 0))),
        scratch_shapes=[pltpu.VMEM((TILE, GS), F32)],
    )(before, up, slope, kernel, x, rest, out0)


def add_up(ids, got, total):
    step = pl.program_id(0)

    @pl.when(step == 0)
    def _():
        total[...] = jnp.zeros_like(total)

    for i in range(NX):
        domain = ids[step * NX + i, 0]
        total[domain] += got[i].astype(F32)


def merge0_kernel(ids, got, out, bias, total):
    add_up(ids, got, total)

    @pl.when(pl.program_id(0) == NY - 1)
    def _():
        for k in range(DOMAINS):
            for z in range(NZ // 2):
                out[z, k * SHARD : (k + 1) * SHARD, :] = total[
                    k, z * SHARD : (z + 1) * SHARD, :
                ].astype(BF)
            bias[k] = total[k, HALF:, :]


def merge0(ids, got):
    return call(
        merge0_kernel,
        "merge0",
        10**6,
        10**6,
        grid=(NY,),
        out_shape=(
            jax.ShapeDtypeStruct((NZ // 2, PIECE, GS), BF),
            jax.ShapeDtypeStruct((DOMAINS, TILE, GS), F32),
        ),
        in_specs=[SMEM, pl.BlockSpec((NX, PART, GS), lambda i: (i, 0, 0))],
        out_specs=(
            pl.BlockSpec((NZ // 2, PIECE, GS), lambda i: (0, 0, 0)),
            pl.BlockSpec((DOMAINS, TILE, GS), lambda i: (0, 0, 0)),
        ),
        scratch_shapes=[pltpu.VMEM((DOMAINS, PART, GS), F32)],
    )(ids, got)


def merge1_kernel(ids, z, got, sums, bias, *refs):
    outs, (total, parts, tile) = refs[:NZ], refs[NZ:]
    add_up(ids, got, total)

    @pl.when(pl.program_id(0) == NY - 1)
    def _():
        tile[...] = jnp.zeros_like(tile)
        parts[: NZ // 2] = sums[...]
        for k in range(DOMAINS):
            for half in range(NZ // 2):
                parts[NZ // 2 + half, k * SHARD : (k + 1) * SHARD, :] = total[
                    k, half * SHARD : (half + 1) * SHARD, :
                ].astype(BF)
            both = total[k, HALF:, :] + bias[k]
            tile[k * SG : (k + 1) * SG, :] = both[:SG, :] + both[SG : 2 * SG, :]
        for k in range(NZ):
            outs[k][:PIECE, :] = parts[(z[0] + k) % NZ]
            outs[k][PIECE:, :] = tile[...].astype(BF)


def merge1(ids, z, got, sums, bias):
    def whole(shape):
        return pl.BlockSpec(shape, lambda i: (0,) * len(shape))

    return call(
        merge1_kernel,
        "merge1",
        10**6,
        2 * 10**6,
        grid=(NY,),
        out_shape=(jax.ShapeDtypeStruct((BLOCK, GS), BF),) * NZ,
        in_specs=[
            SMEM,
            SMEM,
            pl.BlockSpec((NX, PART, GS), lambda i: (i, 0, 0)),
            whole((NZ // 2, PIECE, GS)),
            whole((DOMAINS, TILE, GS)),
        ],
        out_specs=(whole((BLOCK, GS)),) * NZ,
        scratch_shapes=[
            pltpu.VMEM((DOMAINS, PART, GS), F32),
            pltpu.VMEM((NZ, PIECE, GS), BF),
            pltpu.VMEM((TILE, GS), F32),
        ],
    )(ids, z, got, sums, bias)


def finish_kernel(at, *refs):
    got, (sw, dw, d_shared, d_domain, b_shared, b_domain, wide) = refs[:NZ], refs[NZ:]
    shared = sw[...].astype(F32)
    summed = jnp.zeros((SHARD, GS), F32)
    for k in range(DOMAINS):
        part = slice(k * SHARD, (k + 1) * SHARD)
        share = got[0][part, :].astype(F32)
        for z in range(1, NZ):
            share = share + got[z][part, :].astype(F32)
        summed = summed + share * dw[k].astype(F32)
        d_domain[k] = share * shared
    d_shared[...] = summed
    tile = got[0][PIECE:, :].astype(F32)
    for z in range(1, NZ):
        tile = tile + got[z][PIECE:, :].astype(F32)
    wide[...] = jnp.zeros_like(wide)
    for k in range(DOMAINS):
        for q in range(SG):
            row = k * SG + q
            wide[k : k + 1, q * GS : (q + 1) * GS] = tile[row : row + 1, :]
    placed = pltpu.roll(wide[...], SLAB - at[0], 1)
    b_domain[...] = placed[:DOMAINS, :SHARD]
    b_shared[...] = jnp.sum(placed[:DOMAINS, :SHARD], axis=0, keepdims=True)


def finish(at, got, sw, dw):
    return call(
        finish_kernel,
        "finish",
        10**6,
        10**6,
        out_shape=(
            jax.ShapeDtypeStruct((SHARD, GS), F32),
            jax.ShapeDtypeStruct((DOMAINS, SHARD, GS), F32),
            jax.ShapeDtypeStruct((1, SHARD), F32),
            jax.ShapeDtypeStruct((DOMAINS, SHARD), F32),
        ),
        in_specs=[SMEM] + [VMEM] * (NZ + 2),
        out_specs=(VMEM,) * 4,
        scratch_shapes=[pltpu.VMEM((8, SLAB), F32)],
    )(at, *got, sw, dw)


def exchange(block, axes):
    return lax.all_to_all(block, axes, 0, 0, tiled=True)


def turned(block, k):
    return lax.ppermute(block, "zlo", [(i, (i + k) % NZ) for i in range(NZ)])


def after(first, *then):
    return lax.optimization_barrier((first, *then))[1:]


def body(stash, cotangent, domain_ids, shared_weight, domain_weight, shared_bias, domain_bias):
    x = stash[0]
    sw, dw = shared_weight[0], domain_weight[0]
    section = jnp.reshape(2 * lax.axis_index("zhi") + lax.axis_index("core"), (1,))
    z = jnp.reshape(lax.axis_index("zlo"), (1,))
    at = PIECE * z + SHARD * lax.axis_index("x")

    own = prep(at, sw, dw, shared_bias, domain_bias[0])
    held = [own] + [turned(own, k) for k in range(1, NZ)]
    (ids,) = after(own, domain_ids)
    plane_ids = exchange(
        jnp.broadcast_to(ids[0], (NY * NX, 1, 128)), ("y", "x")
    ).reshape(NY * NX, 128)
    got = exchange(pick(plane_ids, z, held), ("y", "x"))
    slope0, slope1, kernel0, kernel1 = slopes(domain_ids, got, x)

    def hop(block, turn):
        return lax.ppermute(block, ("zhi", "core"), [(3 - turn, 2 - turn)])

    out0, kept0 = chain(FIRST, section, cotangent, slope0, kernel0, first=True)
    (slope1,) = after(out0, slope1)
    out1, kept1 = chain(LAST, section, cotangent, slope1, kernel1, first=True)
    for turn in range(2):
        up0 = hop(out0, turn)
        up1 = hop(out1, turn)
        (up0,) = after(out1, up0)
        out0, kept0 = chain(FIRST, kept0, up0, slope0, kernel0)
        (up1,) = after(out0, up1)
        out1, kept1 = chain(LAST, kept1, up1, slope1, kernel1)
    up0 = hop(out0, 2)
    up1 = hop(out1, 2)
    (up0,) = after(out1, up0)
    d_in0, send0, rest = grads0(kept0, up0, slope0, kernel0, x)
    got0 = exchange(send0, ("y", "x"))
    d_inputs, send1 = grads1(kept1, up1, slope1, kernel1, x, rest, d_in0)
    sums0, bias0 = merge0(plane_ids, got0)
    (send1,) = after(got0, send1)
    got1 = exchange(send1, ("y", "x"))
    merged = merge1(plane_ids, z, got1, sums0, bias0)
    final = [merged[0]] + [turned(merged[k], k) for k in range(1, NZ)]
    d_shared, d_domain, b_shared, b_domain = finish(at, final, sw, dw)
    return (d_inputs[None], d_shared[None], d_domain[None], b_shared, b_domain[None])


def solution(mesh):
    fine = Mesh(mesh.devices.reshape(2, 2, NY, NZ, NX), ("zhi", "core", "y", "zlo", "x"))
    section, dp = ("zhi", "core"), ("y", "zlo", "x")
    in_specs = (
        P(section, dp, None),
        P(dp, None),
        P(dp),
        P(section, dp, None),
        P(section, None, dp, None),
        P(section, dp),
        P(section, None, dp),
    )
    out_specs = (
        P(section, dp, None),
        P(section, dp, None),
        P(section, None, dp, None),
        P(section, dp),
        P(section, None, dp),
    )
    return jax.shard_map(
        body, mesh=fine, in_specs=in_specs, out_specs=out_specs, check_vma=False
    )
```

```python
import functools

import jax
import jax.numpy as jnp
from jax import lax
from jax.experimental import pallas as pl
from jax.experimental.pallas import tpu as pltpu
from jax.sharding import Mesh, PartitionSpec as P

D = 3072
GS = 256
DOMAINS = 4
ROWS = 128
NY, NZ, NX = 4, 4, 4
SHARD = 48
SLAB = D // NY
SG = SLAB // GS
PIECE = NZ * SHARD
TILE = 16
BLOCK = PIECE + TILE
FIRST = (0,)
LAST = (1, 2)
EARLY = 1
ROWS0 = EARLY * SHARD
ROWS1 = PIECE - ROWS0
REST = len(FIRST) * GS - EARLY * PIECE
VMEM = pl.BlockSpec(memory_space=pltpu.VMEM)
SMEM = pl.BlockSpec(memory_space=pltpu.SMEM)
BF = jnp.bfloat16
F32 = jnp.float32


def call(kernel, name, flops, moved, limit=48, **rest):
    return pl.pallas_call(
        kernel,
        name=name,
        compiler_params=pltpu.CompilerParams(vmem_limit_bytes=limit * 1024 * 1024),
        cost_estimate=pl.CostEstimate(flops=10**11, bytes_accessed=10**9, transcendentals=0),
        **rest,
    )


def prep_kernel(at, sw, dw, sb, db, out, wide, tile):
    shared = sw[...].astype(F32)
    for k in range(DOMAINS):
        out[k * SHARD : (k + 1) * SHARD, :] = (shared * dw[k].astype(F32)).astype(BF)
    wide[...] = jnp.zeros_like(wide)
    wide[0:1, :SHARD] = sb[...].astype(F32)
    wide[1 : 1 + DOMAINS, :SHARD] = db[...].astype(F32)
    placed = pltpu.roll(wide[...], at[0], 1)
    tile[...] = jnp.zeros_like(tile)
    for k in range(1 + DOMAINS):
        for q in range(SG):
            row = k * SG + q
            tile[row : row + 1, :] = placed[k : k + 1, q * GS : (q + 1) * GS]
    out[PIECE:, :] = tile[...].astype(BF)


def prep(at, sw, dw, sb, db):
    return call(
        prep_kernel,
        "prep",
        10**5,
        3 * 10**5,
        out_shape=jax.ShapeDtypeStruct((BLOCK, GS), BF),
        in_specs=[SMEM, VMEM, VMEM, VMEM, VMEM],
        out_specs=VMEM,
        scratch_shapes=[pltpu.VMEM((8, SLAB), F32), pltpu.VMEM((TILE, GS), F32)],
    )(at, sw, dw, sb, db)


def pick_kernel(ids, z, *refs):
    held, out = refs[:NZ], refs[NZ]
    step = pl.program_id(0)
    tile = held[0][PIECE:, :].astype(F32)
    for k in range(1, NZ):
        tile = tile + held[k][PIECE:, :].astype(F32)
    tile = tile.astype(BF)
    for i in range(NX):
        start = pl.multiple_of(ids[step * NX + i, 0] * SHARD, TILE)
        for k in range(NZ):
            to = pl.multiple_of(((z[0] + NZ - k) % NZ) * SHARD, TILE)
            out[i, pl.ds(to, SHARD), :] = held[k][pl.ds(start, SHARD), :]
        out[i, PIECE:, :] = tile


def pick(ids, z, held):
    return call(
        pick_kernel,
        "pick",
        10**5,
        2 * 10**6,
        grid=(NY,),
        out_shape=jax.ShapeDtypeStruct((NY * NX, BLOCK, GS), BF),
        in_specs=[SMEM, SMEM] + [pl.BlockSpec((BLOCK, GS), lambda i: (0, 0))] * NZ,
        out_specs=pl.BlockSpec((NX, BLOCK, GS), lambda i: (i, 0, 0)),
    )(ids, z, *held)


def slope_kernel(own, got, x, slope0, slope1, kernel0, kernel1, kernel, offsets):
    domain = own[0]
    tile = got[0, PIECE:, :].astype(F32)
    for i in range(1, NX):
        tile = tile + got[i, PIECE:, :].astype(F32)
    offsets[...] = tile
    for z in range(NZ):
        for i in range(NX):
            at = (z * NX + i) * SHARD
            kernel[at : at + SHARD, :] = got[i, z * SHARD : (z + 1) * SHARD, :]
    cut = len(FIRST) * GS
    kernel0[...] = kernel[:cut, :]
    kernel1[...] = kernel[cut:, :]
    for q in range(SG):
        lanes = slice(q * GS, (q + 1) * GS)
        offset = offsets[q : q + 1, :] + offsets[pl.ds((1 + domain) * SG + q, 1), :]
        pre = jnp.dot(x[:, lanes], kernel[lanes, :], preferred_element_type=F32) + offset
        sigma = jax.nn.sigmoid(pre)
        slope = sigma * (1.0 + pre * (1.0 - sigma))
        if q in FIRST:
            slope0[:, lanes] = slope
        else:
            slope1[:, q * GS - cut : (q + 1) * GS - cut] = slope


def columns(width):
    return pl.BlockSpec((ROWS, width), lambda i: (0, i))


def rows(height):
    return pl.BlockSpec((height, GS), lambda i: (i, 0))


def slopes(own, got, x):
    w0, w1 = len(FIRST) * GS, len(LAST) * GS
    return call(
        slope_kernel,
        "slopes",
        2 * 10**8,
        6 * 10**6,
        grid=(NY,),
        out_shape=(
            jax.ShapeDtypeStruct((ROWS, NY * w0), F32),
            jax.ShapeDtypeStruct((ROWS, NY * w1), F32),
            jax.ShapeDtypeStruct((NY * w0, GS), BF),
            jax.ShapeDtypeStruct((NY * w1, GS), BF),
        ),
        in_specs=[SMEM, pl.BlockSpec((NX, BLOCK, GS), lambda i: (i, 0, 0)), columns(SLAB)],
        out_specs=(columns(w0), columns(w1), rows(w0), rows(w1)),
        scratch_shapes=[pltpu.VMEM((SLAB, GS), BF), pltpu.VMEM((TILE, GS), F32)],
    )(own, got, x)


def back_product(signal, kernel):
    return lax.dot_general(
        signal, kernel, (((1,), (1,)), ((), ())), preferred_element_type=F32
    )


def first_kernel(base, section, up, slope, kernel, out, kept):
    for q in range(slope.shape[1] // GS):
        lanes = slice(q * GS, (q + 1) * GS)
        above = up[:, base + q * GS : base + (q + 1) * GS].astype(F32)
        above = jnp.where(section[0] == 3, above, 0.0)
        kept[:, lanes] = above.astype(BF)
        signal = (above * slope[:, lanes]).astype(BF)
        out[:, lanes] = (above + back_product(signal, kernel[lanes, :])).astype(BF)


def next_kernel(before, up, slope, kernel, out, kept):
    for q in range(slope.shape[1] // GS):
        lanes = slice(q * GS, (q + 1) * GS)
        above = before[:, lanes].astype(F32) + up[:, lanes].astype(F32)
        kept[:, lanes] = above.astype(BF)
        signal = (above * slope[:, lanes]).astype(BF)
        out[:, lanes] = (above + back_product(signal, kernel[lanes, :])).astype(BF)


def chain(groups, head, up, slope, kernel, first=False):
    width = len(groups) * GS
    shape = jax.ShapeDtypeStruct((ROWS, NY * width), BF)
    return call(
        functools.partial(first_kernel, groups[0] * GS) if first else next_kernel,
        "chain",
        10**8,
        2 * 10**6,
        grid=(NY,),
        out_shape=(shape, shape),
        in_specs=([SMEM, columns(SLAB)] if first else [columns(width)] * 2)
        + [columns(width), rows(width)],
        out_specs=(columns(width), columns(width)),
    )(head, up, slope, kernel)


def local_grads(groups, before, up, slope, kernel, x, out, tile):
    found = []
    tile[...] = jnp.zeros_like(tile)
    for j, q in enumerate(groups):
        lanes = slice(j * GS, (j + 1) * GS)
        above = before[:, lanes].astype(F32) + up[:, lanes].astype(F32)
        signal = (above * slope[:, lanes]).astype(BF)
        outgoing = (above + back_product(signal, kernel[lanes, :])).astype(BF)
        here = slice(q * GS, (q + 1) * GS)
        out[:, here] = outgoing
        grad = lax.dot_general(
            x[:, here], signal, (((0,), (0,)), ((), ())), preferred_element_type=F32
        )
        found.append(grad.astype(BF))
        total = jnp.sum(signal.astype(F32), axis=0, keepdims=True)
        high = total.astype(BF).astype(F32)
        tile[q : q + 1, :] = high
        tile[SG + q : SG + q + 1, :] = total - high
    return found


def place_of(row):
    shard, inner = row // SHARD, row % SHARD
    return shard // NX, shard % NX, inner


def grads0_kernel(before, up, slope, kernel, x, out, send, rest, tile):
    found = local_grads(FIRST, before, up, slope, kernel, x, out, tile)
    for row in range(0, len(FIRST) * GS, TILE):
        z, i, inner = place_of(row)
        part = found[row // GS][row % GS : row % GS + TILE, :]
        if z < EARLY:
            at = z * SHARD + inner
            send[i, at : at + TILE, :] = part
        else:
            rest[row - EARLY * PIECE : row - EARLY * PIECE + TILE, :] = part
    for i in range(NX):
        send[i, ROWS0:, :] = tile[...].astype(BF)


def grads0(before, up, slope, kernel, x):
    width = len(FIRST) * GS
    return call(
        grads0_kernel,
        "grads0",
        3 * 10**8,
        6 * 10**6,
        grid=(NY,),
        out_shape=(
            jax.ShapeDtypeStruct((ROWS, NY * width), BF),
            jax.ShapeDtypeStruct((NY * NX, ROWS0 + TILE, GS), BF),
            jax.ShapeDtypeStruct((NY * REST, GS), BF),
        ),
        in_specs=[columns(width)] * 3 + [rows(width), columns(SLAB)],
        out_specs=(
            columns(width),
            pl.BlockSpec((NX, ROWS0 + TILE, GS), lambda i: (i, 0, 0)),
            rows(REST),
        ),
        scratch_shapes=[pltpu.VMEM((TILE, GS), F32)],
    )(before, up, slope, kernel, x)


def grads1_kernel(before, up, slope, kernel, x, rest, out0, out, send, tile):
    start = LAST[0] * GS
    out[:, :start] = out0[...]
    found = local_grads(LAST, before, up, slope, kernel, x, out, tile)
    for row in range(EARLY * PIECE, SLAB, TILE):
        z, i, inner = place_of(row)
        at = (z - EARLY) * SHARD + inner
        if row < start:
            part = rest[row - EARLY * PIECE : row - EARLY * PIECE + TILE, :]
        else:
            part = found[(row - start) // GS][row % GS : row % GS + TILE, :]
        send[i, at : at + TILE, :] = part
    for i in range(NX):
        send[i, ROWS1:, :] = tile[...].astype(BF)


def grads1(before, up, slope, kernel, x, rest, out0):
    width = len(LAST) * GS
    return call(
        grads1_kernel,
        "grads1",
        2 * 10**8,
        4 * 10**6,
        grid=(NY,),
        out_shape=(
            jax.ShapeDtypeStruct((ROWS, D), BF),
            jax.ShapeDtypeStruct((NY * NX, ROWS1 + TILE, GS), BF),
        ),
        in_specs=[columns(width)] * 3
        + [rows(width), columns(SLAB), rows(REST), columns(len(FIRST) * GS)],
        out_specs=(columns(SLAB), pl.BlockSpec((NX, ROWS1 + TILE, GS), lambda i: (i, 0, 0))),
        scratch_shapes=[pltpu.VMEM((TILE, GS), F32)],
    )(before, up, slope, kernel, x, rest, out0)


def add_up(ids, got, total):
    step = pl.program_id(0)

    @pl.when(step == 0)
    def _():
        total[...] = jnp.zeros_like(total)

    for i in range(NX):
        domain = ids[step * NX + i, 0]
        total[domain] += got[i].astype(F32)


def merge0_kernel(ids, got, out, bias, total):
    add_up(ids, got, total)

    @pl.when(pl.program_id(0) == NY - 1)
    def _():
        for k in range(DOMAINS):
            for z in range(EARLY):
                out[z, k * SHARD : (k + 1) * SHARD, :] = total[
                    k, z * SHARD : (z + 1) * SHARD, :
                ].astype(BF)
            bias[k] = total[k, ROWS0:, :]


def whole(shape):
    return pl.BlockSpec(shape, lambda i: (0,) * len(shape))


def merge0(ids, got):
    return call(
        merge0_kernel,
        "merge0",
        10**6,
        10**6,
        grid=(NY,),
        out_shape=(
            jax.ShapeDtypeStruct((EARLY, PIECE, GS), BF),
            jax.ShapeDtypeStruct((DOMAINS, TILE, GS), F32),
        ),
        in_specs=[SMEM, pl.BlockSpec((NX, ROWS0 + TILE, GS), lambda i: (i, 0, 0))],
        out_specs=(whole((EARLY, PIECE, GS)), whole((DOMAINS, TILE, GS))),
        scratch_shapes=[pltpu.VMEM((DOMAINS, ROWS0 + TILE, GS), F32)],
    )(ids, got)


def merge1_kernel(ids, z, got, sums, bias, *refs):
    outs, (total, parts, tile) = refs[:NZ], refs[NZ:]
    add_up(ids, got, total)

    @pl.when(pl.program_id(0) == NY - 1)
    def _():
        tile[...] = jnp.zeros_like(tile)
        parts[:EARLY] = sums[...]
        for k in range(DOMAINS):
            for late in range(NZ - EARLY):
                parts[EARLY + late, k * SHARD : (k + 1) * SHARD, :] = total[
                    k, late * SHARD : (late + 1) * SHARD, :
                ].astype(BF)
            both = total[k, ROWS1:, :] + bias[k]
            tile[k * SG : (k + 1) * SG, :] = both[:SG, :] + both[SG : 2 * SG, :]
        for k in range(NZ):
            outs[k][:PIECE, :] = parts[(z[0] + k) % NZ]
            outs[k][PIECE:, :] = tile[...].astype(BF)


def merge1(ids, z, got, sums, bias):
    return call(
        merge1_kernel,
        "merge1",
        10**6,
        2 * 10**6,
        grid=(NY,),
        out_shape=(jax.ShapeDtypeStruct((BLOCK, GS), BF),) * NZ,
        in_specs=[
            SMEM,
            SMEM,
            pl.BlockSpec((NX, ROWS1 + TILE, GS), lambda i: (i, 0, 0)),
            whole((EARLY, PIECE, GS)),
            whole((DOMAINS, TILE, GS)),
        ],
        out_specs=(whole((BLOCK, GS)),) * NZ,
        scratch_shapes=[
            pltpu.VMEM((DOMAINS, ROWS1 + TILE, GS), F32),
            pltpu.VMEM((NZ, PIECE, GS), BF),
            pltpu.VMEM((TILE, GS), F32),
        ],
    )(ids, z, got, sums, bias)


def finish_kernel(at, *refs):
    got, (sw, dw, d_shared, d_domain, b_shared, b_domain, wide) = refs[:NZ], refs[NZ:]
    shared = sw[...].astype(F32)
    summed = jnp.zeros((SHARD, GS), F32)
    for k in range(DOMAINS):
        part = slice(k * SHARD, (k + 1) * SHARD)
        share = got[0][part, :].astype(F32)
        for z in range(1, NZ):
            share = share + got[z][part, :].astype(F32)
        summed = summed + share * dw[k].astype(F32)
        d_domain[k] = share * shared
    d_shared[...] = summed
    tile = got[0][PIECE:, :].astype(F32)
    for z in range(1, NZ):
        tile = tile + got[z][PIECE:, :].astype(F32)
    wide[...] = jnp.zeros_like(wide)
    for k in range(DOMAINS):
        for q in range(SG):
            row = k * SG + q
            wide[k : k + 1, q * GS : (q + 1) * GS] = tile[row : row + 1, :]
    placed = pltpu.roll(wide[...], SLAB - at[0], 1)
    b_domain[...] = placed[:DOMAINS, :SHARD]
    b_shared[...] = jnp.sum(placed[:DOMAINS, :SHARD], axis=0, keepdims=True)


def finish(at, got, sw, dw):
    return call(
        finish_kernel,
        "finish",
        10**6,
        10**6,
        out_shape=(
            jax.ShapeDtypeStruct((SHARD, GS), F32),
            jax.ShapeDtypeStruct((DOMAINS, SHARD, GS), F32),
            jax.ShapeDtypeStruct((1, SHARD), F32),
            jax.ShapeDtypeStruct((DOMAINS, SHARD), F32),
        ),
        in_specs=[SMEM] + [VMEM] * (NZ + 2),
        out_specs=(VMEM,) * 4,
        scratch_shapes=[pltpu.VMEM((8, SLAB), F32)],
    )(at, *got, sw, dw)


def exchange(block, axes):
    return lax.all_to_all(block, axes, 0, 0, tiled=True)


def turned(block, k):
    return lax.ppermute(block, "zlo", [(i, (i + k) % NZ) for i in range(NZ)])


def after(first, *then):
    return lax.optimization_barrier((first, *then))[1:]


def body(stash, cotangent, domain_ids, shared_weight, domain_weight, shared_bias, domain_bias):
    x = stash[0]
    sw, dw = shared_weight[0], domain_weight[0]
    section = jnp.reshape(2 * lax.axis_index("zhi") + lax.axis_index("core"), (1,))
    z = jnp.reshape(lax.axis_index("zlo"), (1,))
    at = PIECE * z + SHARD * lax.axis_index("x")

    own = prep(at, sw, dw, shared_bias, domain_bias[0])
    held = [own] + [turned(own, k) for k in range(1, NZ)]
    (ids,) = after(own, domain_ids)
    plane_ids = exchange(
        jnp.broadcast_to(ids[0], (NY * NX, 1, 128)), ("y", "x")
    ).reshape(NY * NX, 128)
    got = exchange(pick(plane_ids, z, held), ("y", "x"))
    slope0, slope1, kernel0, kernel1 = slopes(domain_ids, got, x)

    def hop(block, turn):
        return lax.ppermute(block, ("zhi", "core"), [(3 - turn, 2 - turn)])

    out0, kept0 = chain(FIRST, section, cotangent, slope0, kernel0, first=True)
    (slope1,) = after(out0, slope1)
    out1, kept1 = chain(LAST, section, cotangent, slope1, kernel1, first=True)
    for turn in range(3):
        up0 = hop(out0, turn)
        if turn == 1:
            (out1,) = after(up0, out1)
        up1 = hop(out1, turn)
        if turn < 2:
            out0, kept0 = chain(FIRST, kept0, up0, slope0, kernel0)
            out1, kept1 = chain(LAST, kept1, up1, slope1, kernel1)
    d_in0, send0, rest = grads0(kept0, up0, slope0, kernel0, x)
    got0 = exchange(send0, ("y", "x"))
    d_inputs, send1 = grads1(kept1, up1, slope1, kernel1, x, rest, d_in0)
    sums0, bias0 = merge0(plane_ids, got0)
    (send1,) = after(got0, send1)
    got1 = exchange(send1, ("y", "x"))
    merged = merge1(plane_ids, z, got1, sums0, bias0)
    final = [merged[0]] + [turned(merged[k], k) for k in range(1, NZ)]
    d_shared, d_domain, b_shared, b_domain = finish(at, final, sw, dw)
    return (d_inputs[None], d_shared[None], d_domain[None], b_shared, b_domain[None])


def solution(mesh):
    fine = Mesh(mesh.devices.reshape(2, 2, NY, NZ, NX), ("zhi", "core", "y", "zlo", "x"))
    section, dp = ("zhi", "core"), ("y", "zlo", "x")
    in_specs = (
        P(section, dp, None),
        P(dp, None),
        P(dp),
        P(section, dp, None),
        P(section, None, dp, None),
        P(section, dp),
        P(section, None, dp),
    )
    out_specs = (
        P(section, dp, None),
        P(section, dp, None),
        P(section, None, dp, None),
        P(section, dp),
        P(section, None, dp),
    )
    return jax.shard_map(
        body, mesh=fine, in_specs=in_specs, out_specs=out_specs, check_vma=False
    )
```

```python
import jax
import jax.numpy as jnp
from jax import lax
from jax.experimental import pallas as pl
from jax.experimental.pallas import tpu as pltpu
from jax.sharding import Mesh, PartitionSpec as P

D = 3072
GS = 256
DOMAINS = 4
ROWS = 128
NY, NZ, NX = 4, 4, 4
SHARD = 48
SLAB = D // NY
SG = SLAB // GS
WIDE = D // 2
SLABS = NY // 2
PIECE = NZ * SHARD
TILE = 16
BLOCK = PIECE + TILE
VMEM = pl.BlockSpec(memory_space=pltpu.VMEM)
SMEM = pl.BlockSpec(memory_space=pltpu.SMEM)
BF = jnp.bfloat16
F32 = jnp.float32
HEAVY = 10**11


def call(kernel, name, limit=48, weight=HEAVY, **rest):
    return pl.pallas_call(
        kernel,
        name=name,
        compiler_params=pltpu.CompilerParams(vmem_limit_bytes=limit * 1024 * 1024),
        cost_estimate=pl.CostEstimate(
            flops=weight, bytes_accessed=weight // 100, transcendentals=0
        ),
        **rest,
    )


def prep_kernel(at, sw, dw, sb, db, out, wide, tile):
    shared = sw[...].astype(F32)
    for k in range(DOMAINS):
        out[k * SHARD : (k + 1) * SHARD, :] = (shared * dw[k].astype(F32)).astype(BF)
    wide[...] = jnp.zeros_like(wide)
    wide[0:1, :SHARD] = sb[...].astype(F32)
    wide[1 : 1 + DOMAINS, :SHARD] = db[...].astype(F32)
    placed = pltpu.roll(wide[...], at[0], 1)
    tile[...] = jnp.zeros_like(tile)
    for k in range(1 + DOMAINS):
        for q in range(SG):
            row = k * SG + q
            tile[row : row + 1, :] = placed[k : k + 1, q * GS : (q + 1) * GS]
    out[PIECE:, :] = tile[...].astype(BF)


def prep(at, sw, dw, sb, db):
    return call(
        prep_kernel,
        "prep",
        limit=58,
        out_shape=jax.ShapeDtypeStruct((BLOCK, GS), BF),
        in_specs=[SMEM, VMEM, VMEM, VMEM, VMEM],
        out_specs=VMEM,
        scratch_shapes=[pltpu.VMEM((8, SLAB), F32), pltpu.VMEM((TILE, GS), F32)],
    )(at, sw, dw, sb, db)


def pick_kernel(ids, z, *refs):
    held, out = refs[:NZ], refs[NZ]
    step = pl.program_id(0)
    tile = held[0][PIECE:, :].astype(F32)
    for k in range(1, NZ):
        tile = tile + held[k][PIECE:, :].astype(F32)
    tile = tile.astype(BF)
    for i in range(NX):
        start = pl.multiple_of(ids[step * NX + i, 0] * SHARD, TILE)
        for k in range(NZ):
            to = pl.multiple_of(((z[0] + NZ - k) % NZ) * SHARD, TILE)
            out[i, pl.ds(to, SHARD), :] = held[k][pl.ds(start, SHARD), :]
        out[i, PIECE:, :] = tile


def pick(ids, z, held):
    return call(
        pick_kernel,
        "pick",
        grid=(NY,),
        out_shape=jax.ShapeDtypeStruct((NY * NX, BLOCK, GS), BF),
        in_specs=[SMEM, SMEM] + [pl.BlockSpec((BLOCK, GS), lambda i: (0, 0))] * NZ,
        out_specs=pl.BlockSpec((NX, BLOCK, GS), lambda i: (i, 0, 0)),
    )(ids, z, *held)


def gather_kernel(core, own, other, cotangent, x, up):
    even = core[0] == 0
    x[0] = jnp.where(even, own[:, :WIDE], other[...])
    x[1] = jnp.where(even, other[...], own[:, WIDE:])
    up[...] = jnp.where(even, cotangent[:, :WIDE], cotangent[:, WIDE:])


def gather(core, own, other, cotangent):
    return call(
        gather_kernel,
        "gather",
        out_shape=(
            jax.ShapeDtypeStruct((2, ROWS, WIDE), BF),
            jax.ShapeDtypeStruct((ROWS, WIDE), BF),
        ),
        in_specs=[SMEM, VMEM, VMEM, VMEM],
        out_specs=(VMEM, VMEM),
    )(core, own, other, cotangent)


def slope_kernel(own, got, x, slope, kernel, offsets):
    domain = own[0]
    tile = got[0, PIECE:, :].astype(F32)
    for i in range(1, NX):
        tile = tile + got[i, PIECE:, :].astype(F32)
    offsets[...] = tile
    for z in range(NZ):
        for i in range(NX):
            at = (z * NX + i) * SHARD
            kernel[0, at : at + SHARD, :] = got[i, z * SHARD : (z + 1) * SHARD, :]
    for q in range(SG):
        lanes = slice(q * GS, (q + 1) * GS)
        offset = offsets[q : q + 1, :] + offsets[pl.ds((1 + domain) * SG + q, 1), :]
        pre = jnp.dot(x[0, :, lanes], kernel[0, lanes, :], preferred_element_type=F32) + offset
        sigma = jax.nn.sigmoid(pre)
        slope[0, :, lanes] = sigma * (1.0 + pre * (1.0 - sigma))


def slopes(own, got, x):
    return call(
        slope_kernel,
        "slopes",
        grid=(2, SLABS),
        out_shape=(
            jax.ShapeDtypeStruct((2, ROWS, WIDE), F32),
            jax.ShapeDtypeStruct((2, WIDE, GS), BF),
        ),
        in_specs=[
            SMEM,
            pl.BlockSpec((NX, BLOCK, GS), lambda p, h: (SLABS * p + h, 0, 0)),
            pl.BlockSpec((1, ROWS, SLAB), lambda p, h: (p, 0, h)),
        ],
        out_specs=(
            pl.BlockSpec((1, ROWS, SLAB), lambda p, h: (p, 0, h)),
            pl.BlockSpec((1, SLAB, GS), lambda p, h: (p, h, 0)),
        ),
        scratch_shapes=[pltpu.VMEM((TILE, GS), F32)],
    )(own, got, x)


def layer(above, slope, kernel):
    signal = (above * slope).astype(BF)
    back = lax.dot_general(signal, kernel, (((1,), (1,)), ((), ())), preferred_element_type=F32)
    return signal, (above + back).astype(BF)


COLUMNS = pl.BlockSpec((ROWS, SLAB), lambda h: (0, h))
BOTH_COLUMNS = pl.BlockSpec((2, ROWS, SLAB), lambda h: (0, 0, h))
BOTH_ROWS = pl.BlockSpec((2, SLAB, GS), lambda h: (0, h, 0))


def pair_kernel(up, slope, kernel, out):
    for q in range(SG):
        lanes = slice(q * GS, (q + 1) * GS)
        above = up[:, lanes].astype(F32)
        _, middle = layer(above, slope[1, :, lanes], kernel[1, lanes, :])
        _, out[:, lanes] = layer(middle.astype(F32), slope[0, :, lanes], kernel[0, lanes, :])


def pair(up, slope, kernel):
    return call(
        pair_kernel,
        "pair",
        grid=(SLABS,),
        out_shape=jax.ShapeDtypeStruct((ROWS, WIDE), BF),
        in_specs=[COLUMNS, BOTH_COLUMNS, BOTH_ROWS],
        out_specs=COLUMNS,
    )(up, slope, kernel)


def grads_kernel(place, top, hop, slope, kernel, x, keep, give, send, tile):
    even = place[0] == 0
    last = place[1] == 1
    for q in range(SG):
        lanes = slice(q * GS, (q + 1) * GS)
        above = jnp.where(last, top[:, lanes], hop[:, lanes]).astype(F32)
        outs = [None, None]
        for p in (1, 0):
            signal, outs[p] = layer(above, slope[p, :, lanes], kernel[p, lanes, :])
            above = outs[p].astype(F32)
            grad = lax.dot_general(
                x[p, :, lanes], signal, (((0,), (0,)), ((), ())), preferred_element_type=F32
            ).astype(BF)
            for row in range(q * GS, (q + 1) * GS, TILE):
                shard, inner = row // SHARD, row % SHARD
                at = shard // NX * SHARD + inner
                send[p, 0, shard % NX, at : at + TILE, :] = grad[row - q * GS : row - q * GS + TILE]
            total = jnp.sum(signal.astype(F32), axis=0, keepdims=True)
            high = total.astype(BF).astype(F32)
            tile[p, q : q + 1, :] = high
            tile[p, SG + q : SG + q + 1, :] = total - high
        keep[:, lanes] = jnp.where(even, outs[0], outs[1])
        give[:, lanes] = jnp.where(even, outs[1], outs[0])
    tile[:, 2 * SG :, :] = jnp.zeros((2, TILE - 2 * SG, GS), F32)
    for p in range(2):
        for i in range(NX):
            send[p, 0, i, PIECE:, :] = tile[p].astype(BF)


def grads(place, top, hop, slope, kernel, x):
    half = jax.ShapeDtypeStruct((ROWS, WIDE), BF)
    return call(
        grads_kernel,
        "grads",
        grid=(SLABS,),
        out_shape=(half, half, jax.ShapeDtypeStruct((2, SLABS, NX, BLOCK, GS), BF)),
        in_specs=[SMEM, COLUMNS, COLUMNS, BOTH_COLUMNS, BOTH_ROWS, BOTH_COLUMNS],
        out_specs=(
            COLUMNS,
            COLUMNS,
            pl.BlockSpec((2, 1, NX, BLOCK, GS), lambda h: (0, h, 0, 0, 0)),
        ),
        scratch_shapes=[pltpu.VMEM((2, TILE, GS), F32)],
    )(place, top, hop, slope, kernel, x)


def join_kernel(core, keep, other, out):
    even = core[0] == 0
    out[:, :WIDE] = jnp.where(even, keep[...], other[...])
    out[:, WIDE:] = jnp.where(even, other[...], keep[...])


def join(core, keep, other):
    return call(
        join_kernel,
        "join",
        out_shape=jax.ShapeDtypeStruct((ROWS, D), BF),
        in_specs=[SMEM, VMEM, VMEM],
        out_specs=VMEM,
    )(core, keep, other)


def merge_kernel(ids, z, got, *refs):
    outs, (total, parts, tile) = refs[:NZ], refs[NZ:]
    step = pl.program_id(0)

    @pl.when(step == 0)
    def _():
        total[...] = jnp.zeros_like(total)

    for i in range(NX):
        domain = ids[step * NX + i, 0]
        total[domain] += got[i].astype(F32)

    @pl.when(step == NY - 1)
    def _():
        tile[...] = jnp.zeros_like(tile)
        for k in range(DOMAINS):
            for to in range(NZ):
                parts[to, k * SHARD : (k + 1) * SHARD, :] = total[
                    k, to * SHARD : (to + 1) * SHARD, :
                ].astype(BF)
            tile[k * SG : (k + 1) * SG, :] = (
                total[k, PIECE : PIECE + SG, :] + total[k, PIECE + SG : PIECE + 2 * SG, :]
            )
        for k in range(NZ):
            outs[k][:PIECE, :] = parts[(z[0] + k) % NZ]
            outs[k][PIECE:, :] = tile[...].astype(BF)


def merge(ids, z, got):
    return call(
        merge_kernel,
        "merge",
        grid=(NY,),
        out_shape=(jax.ShapeDtypeStruct((BLOCK, GS), BF),) * NZ,
        in_specs=[SMEM, SMEM, pl.BlockSpec((NX, BLOCK, GS), lambda i: (i, 0, 0))],
        out_specs=(pl.BlockSpec((BLOCK, GS), lambda i: (0, 0)),) * NZ,
        scratch_shapes=[
            pltpu.VMEM((DOMAINS, BLOCK, GS), F32),
            pltpu.VMEM((NZ, PIECE, GS), BF),
            pltpu.VMEM((TILE, GS), F32),
        ],
    )(ids, z, got)


def finish_kernel(at, *refs):
    got, (sw, dw, d_shared, d_domain, b_shared, b_domain, wide) = refs[:NZ], refs[NZ:]
    shared = sw[...].astype(F32)
    summed = jnp.zeros((SHARD, GS), F32)
    for k in range(DOMAINS):
        part = slice(k * SHARD, (k + 1) * SHARD)
        share = got[0][part, :].astype(F32)
        for z in range(1, NZ):
            share = share + got[z][part, :].astype(F32)
        summed = summed + share * dw[k].astype(F32)
        d_domain[k] = share * shared
    d_shared[...] = summed
    tile = got[0][PIECE:, :].astype(F32)
    for z in range(1, NZ):
        tile = tile + got[z][PIECE:, :].astype(F32)
    wide[...] = jnp.zeros_like(wide)
    for k in range(DOMAINS):
        for q in range(SG):
            row = k * SG + q
            wide[k : k + 1, q * GS : (q + 1) * GS] = tile[row : row + 1, :]
    placed = pltpu.roll(wide[...], SLAB - at[0], 1)
    b_domain[...] = placed[:DOMAINS, :SHARD]
    b_shared[...] = jnp.sum(placed[:DOMAINS, :SHARD], axis=0, keepdims=True)


def finish(at, got, sw, dw):
    return call(
        finish_kernel,
        "finish",
        out_shape=(
            jax.ShapeDtypeStruct((SHARD, GS), F32),
            jax.ShapeDtypeStruct((DOMAINS, SHARD, GS), F32),
            jax.ShapeDtypeStruct((1, SHARD), F32),
            jax.ShapeDtypeStruct((DOMAINS, SHARD), F32),
        ),
        in_specs=[SMEM] + [VMEM] * (NZ + 2),
        out_specs=(VMEM,) * 4,
        scratch_shapes=[pltpu.VMEM((8, SLAB), F32)],
    )(at, *got, sw, dw)


def exchange(block, axes):
    return lax.all_to_all(block, axes, 0, 0, tiled=True)


def turned(block, k):
    pairs = []
    for core in range(2):
        for y in range(NY):
            for z in range(NZ):
                to = (y // SLABS * NY + core * SLABS + y % SLABS) * NZ + (z + k) % NZ
                pairs.append(((core * NY + y) * NZ + z, to))
    return lax.ppermute(block, ("core", "y", "zlo"), pairs)


def swapped(block):
    return lax.ppermute(block, "core", [(0, 1), (1, 0)])


def after(first, *then):
    return lax.optimization_barrier((first, *then))[1:]


def body(stash, cotangent, domain_ids, shared_weight, domain_weight, shared_bias, domain_bias):
    own = stash[0]
    sw, dw = shared_weight[0], domain_weight[0]
    core = lax.axis_index("core")
    place = jnp.stack([core, lax.axis_index("zhi")])
    z = jnp.reshape(lax.axis_index("zlo"), (1,))
    at = PIECE * z + SHARD * lax.axis_index("x")

    mine = prep(at, sw, dw, shared_bias, domain_bias[0])
    held = [turned(mine, k) for k in range(NZ)]
    (ids,) = after(mine, domain_ids)
    plane_ids = exchange(
        jnp.broadcast_to(ids[0], (NY * NX, 1, 128)), ("y", "x")
    ).reshape(NY * NX, 128)
    (own,) = after(plane_ids, own)
    other = swapped(lax.dynamic_slice(own, (0, (1 - core) * WIDE), (ROWS, WIDE)))
    got = exchange(pick(plane_ids, z, held), ("y", "x"))
    x, top = gather(place, own, other, cotangent)

    slope, kernel = slopes(domain_ids, got, x)
    out = pair(top, slope, kernel)
    hop = lax.ppermute(out, "zhi", [(1, 0)])
    keep, give, send = grads(place, top, hop, slope, kernel, x)
    got = exchange(send.reshape(NY * NX, BLOCK, GS), ("y", "x"))
    d_inputs = join(place, keep, swapped(give))
    merged = merge(plane_ids, z, got)
    final = [turned(merged[k], k) for k in range(NZ)]
    d_shared, d_domain, b_shared, b_domain = finish(at, final, sw, dw)
    return (d_inputs[None], d_shared[None], d_domain[None], b_shared, b_domain[None])


def solution(mesh):
    fine = Mesh(mesh.devices.reshape(2, 2, NY, NZ, NX), ("zhi", "core", "y", "zlo", "x"))
    section, dp = ("zhi", "core"), ("y", "zlo", "x")
    in_specs = (
        P(section, dp, None),
        P(dp, None),
        P(dp),
        P(section, dp, None),
        P(section, None, dp, None),
        P(section, dp),
        P(section, None, dp),
    )
    out_specs = (
        P(section, dp, None),
        P(section, dp, None),
        P(section, None, dp, None),
        P(section, dp),
        P(section, None, dp),
    )
    return jax.shard_map(
        body, mesh=fine, in_specs=in_specs, out_specs=out_specs, check_vma=False
    )
```

```python
import jax
import jax.numpy as jnp
from jax import lax
from jax.experimental import pallas as pl
from jax.experimental.pallas import tpu as pltpu
from jax.sharding import Mesh, PartitionSpec as P

D = 3072
GS = 256
DOMAINS = 4
ROWS = 128
NY, NZ, NX = 4, 4, 4
SHARD = 48
SLAB = D // NY
SG = SLAB // GS
SECTIONS = 4
PIECE = NZ * SHARD
TILE = 16
BLOCK = PIECE + TILE
VMEM = pl.BlockSpec(memory_space=pltpu.VMEM)
SMEM = pl.BlockSpec(memory_space=pltpu.SMEM)
BF = jnp.bfloat16
F32 = jnp.float32
HEAVY = 10**11


def call(kernel, name, limit=48, weight=HEAVY, **rest):
    return pl.pallas_call(
        kernel,
        name=name,
        compiler_params=pltpu.CompilerParams(vmem_limit_bytes=limit * 1024 * 1024),
        cost_estimate=pl.CostEstimate(
            flops=weight, bytes_accessed=weight // 100, transcendentals=0
        ),
        **rest,
    )


def prep_kernel(at, sw, dw, sb, db, out, wide, tile):
    shared = sw[...].astype(F32)
    for k in range(DOMAINS):
        out[k * SHARD : (k + 1) * SHARD, :] = (shared * dw[k].astype(F32)).astype(BF)
    wide[...] = jnp.zeros_like(wide)
    wide[0:1, :SHARD] = sb[...].astype(F32)
    wide[1 : 1 + DOMAINS, :SHARD] = db[...].astype(F32)
    placed = pltpu.roll(wide[...], at[0], 1)
    tile[...] = jnp.zeros_like(tile)
    for k in range(1 + DOMAINS):
        for q in range(SG):
            row = k * SG + q
            tile[row : row + 1, :] = placed[k : k + 1, q * GS : (q + 1) * GS]
    out[PIECE:, :] = tile[...].astype(BF)


def prep(at, sw, dw, sb, db):
    return call(
        prep_kernel,
        "prep",
        limit=58,
        out_shape=jax.ShapeDtypeStruct((BLOCK, GS), BF),
        in_specs=[SMEM, VMEM, VMEM, VMEM, VMEM],
        out_specs=VMEM,
        scratch_shapes=[pltpu.VMEM((8, SLAB), F32), pltpu.VMEM((TILE, GS), F32)],
    )(at, sw, dw, sb, db)


def pick_kernel(ids, z, *refs):
    held, out = refs[:NZ], refs[NZ]
    step = pl.program_id(0)
    tile = held[0][PIECE:, :].astype(F32)
    for k in range(1, NZ):
        tile = tile + held[k][PIECE:, :].astype(F32)
    tile = tile.astype(BF)
    for i in range(NX):
        start = pl.multiple_of(ids[step * NX + i, 0] * SHARD, TILE)
        for k in range(NZ):
            to = pl.multiple_of(((z[0] + NZ - k) % NZ) * SHARD, TILE)
            out[i, pl.ds(to, SHARD), :] = held[k][pl.ds(start, SHARD), :]
        out[i, PIECE:, :] = tile


def pick(ids, z, held):
    return call(
        pick_kernel,
        "pick",
        grid=(NY,),
        out_shape=jax.ShapeDtypeStruct((NY * NX, BLOCK, GS), BF),
        in_specs=[SMEM, SMEM] + [pl.BlockSpec((BLOCK, GS), lambda i: (0, 0))] * NZ,
        out_specs=pl.BlockSpec((NX, BLOCK, GS), lambda i: (i, 0, 0)),
    )(ids, z, *held)


def fixed(shape):
    return pl.BlockSpec(shape, lambda i, s: (0,) * len(shape))


def slab_of(k):
    return pl.BlockSpec((ROWS, SLAB), lambda i, s: (0, s[0] ^ k))


def cut_kernel(s, *refs):
    for k in range(1, SECTIONS):
        refs[SECTIONS - 2 + k][...] = refs[k - 1][...]


def cut(section, stash):
    quarter = jax.ShapeDtypeStruct((ROWS, SLAB), BF)
    return call(
        cut_kernel,
        "cut",
        out_shape=(quarter,) * (SECTIONS - 1),
        grid_spec=pltpu.PrefetchScalarGridSpec(
            num_scalar_prefetch=1,
            grid=(1,),
            in_specs=[slab_of(k) for k in range(1, SECTIONS)],
            out_specs=[fixed((ROWS, SLAB))] * (SECTIONS - 1),
        ),
    )(section, stash, stash, stash)


def gather_kernel(s, own, other1, other2, other3, cotangent, x, top):
    for k, part in enumerate((own, other1, other2, other3)):
        x[s[0] ^ k] = part[...]
    top[...] = cotangent[...]


def gather(section, stash, others, cotangent):
    return call(
        gather_kernel,
        "gather",
        out_shape=(
            jax.ShapeDtypeStruct((SECTIONS, ROWS, SLAB), BF),
            jax.ShapeDtypeStruct((ROWS, SLAB), BF),
        ),
        grid_spec=pltpu.PrefetchScalarGridSpec(
            num_scalar_prefetch=1,
            grid=(1,),
            in_specs=[slab_of(0)] + [fixed((ROWS, SLAB))] * (SECTIONS - 1) + [slab_of(0)],
            out_specs=[fixed((SECTIONS, ROWS, SLAB)), fixed((ROWS, SLAB))],
        ),
    )(section, stash, *others, cotangent)


def slope_kernel(own, got, x, slope, kernel, offsets):
    domain = own[0]
    tile = got[0, PIECE:, :].astype(F32)
    for i in range(1, NX):
        tile = tile + got[i, PIECE:, :].astype(F32)
    offsets[...] = tile
    for z in range(NZ):
        for i in range(NX):
            at = (z * NX + i) * SHARD
            kernel[0, at : at + SHARD, :] = got[i, z * SHARD : (z + 1) * SHARD, :]
    for q in range(SG):
        lanes = slice(q * GS, (q + 1) * GS)
        offset = offsets[q : q + 1, :] + offsets[pl.ds((1 + domain) * SG + q, 1), :]
        pre = jnp.dot(x[0, :, lanes], kernel[0, lanes, :], preferred_element_type=F32) + offset
        sigma = jax.nn.sigmoid(pre)
        slope[0, :, lanes] = sigma * (1.0 + pre * (1.0 - sigma))


def slopes(own, got, x):
    tokens = pl.BlockSpec((1, ROWS, SLAB), lambda i: (i, 0, 0))
    return call(
        slope_kernel,
        "slopes",
        grid=(SECTIONS,),
        out_shape=(
            jax.ShapeDtypeStruct((SECTIONS, ROWS, SLAB), F32),
            jax.ShapeDtypeStruct((SECTIONS, SLAB, GS), BF),
        ),
        in_specs=[SMEM, pl.BlockSpec((NX, BLOCK, GS), lambda i: (i, 0, 0)), tokens],
        out_specs=(tokens, pl.BlockSpec((1, SLAB, GS), lambda i: (i, 0, 0))),
        scratch_shapes=[pltpu.VMEM((TILE, GS), F32)],
    )(own, got, x)


def grads_kernel(s, top, slope, kernel, x, out, send, above, tile):
    @pl.when(pl.program_id(0) == 0)
    def _():
        above[...] = top[...]

    tile[...] = jnp.zeros_like(tile)
    for q in range(SG):
        lanes = slice(q * GS, (q + 1) * GS)
        incoming = above[:, lanes].astype(F32)
        signal = (incoming * slope[0, :, lanes]).astype(BF)
        back = lax.dot_general(
            signal, kernel[0, lanes, :], (((1,), (1,)), ((), ())), preferred_element_type=F32
        )
        outgoing = (incoming + back).astype(BF)
        out[0, :, lanes] = outgoing
        above[:, lanes] = outgoing
        grad = lax.dot_general(
            x[0, :, lanes], signal, (((0,), (0,)), ((), ())), preferred_element_type=F32
        ).astype(BF)
        for row in range(q * GS, (q + 1) * GS, TILE):
            shard, inner = row // SHARD, row % SHARD
            at = shard // NX * SHARD + inner
            send[shard % NX, at : at + TILE, :] = grad[row - q * GS : row - q * GS + TILE]
        total = jnp.sum(signal.astype(F32), axis=0, keepdims=True)
        high = total.astype(BF).astype(F32)
        tile[q : q + 1, :] = high
        tile[SG + q : SG + q + 1, :] = total - high
    for i in range(NX):
        send[i, PIECE:, :] = tile[...].astype(BF)


def grads(section, top, slope, kernel, x):
    last = SECTIONS - 1
    tokens = pl.BlockSpec((1, ROWS, SLAB), lambda i, s: (last - i, 0, 0))
    return call(
        grads_kernel,
        "grads",
        out_shape=(
            jax.ShapeDtypeStruct((SECTIONS, ROWS, SLAB), BF),
            jax.ShapeDtypeStruct((SECTIONS * NX, BLOCK, GS), BF),
        ),
        grid_spec=pltpu.PrefetchScalarGridSpec(
            num_scalar_prefetch=1,
            grid=(SECTIONS,),
            in_specs=[
                fixed((ROWS, SLAB)),
                tokens,
                pl.BlockSpec((1, SLAB, GS), lambda i, s: (last - i, 0, 0)),
                tokens,
            ],
            out_specs=[
                pl.BlockSpec((1, ROWS, SLAB), lambda i, s: ((last - i) ^ s[0], 0, 0)),
                pl.BlockSpec((NX, BLOCK, GS), lambda i, s: (last - i, 0, 0)),
            ],
            scratch_shapes=[pltpu.VMEM((ROWS, SLAB), BF), pltpu.VMEM((TILE, GS), F32)],
        ),
    )(section, top, slope, kernel, x)


def join_kernel(s, own, other1, other2, other3, out):
    for k, part in enumerate((own, other1, other2, other3)):

        @pl.when(pl.program_id(0) == k)
        def _(part=part):
            out[...] = part[...]


def join(section, own, others):
    return call(
        join_kernel,
        "join",
        out_shape=jax.ShapeDtypeStruct((ROWS, D), BF),
        grid_spec=pltpu.PrefetchScalarGridSpec(
            num_scalar_prefetch=1,
            grid=(SECTIONS,),
            in_specs=[fixed((ROWS, SLAB))] * SECTIONS,
            out_specs=pl.BlockSpec((ROWS, SLAB), lambda i, s: (0, i ^ s[0])),
        ),
    )(section, own, *others)


def merge_kernel(ids, z, got, *refs):
    outs, (total, parts, tile) = refs[:NZ], refs[NZ:]
    step = pl.program_id(0)

    @pl.when(step == 0)
    def _():
        total[...] = jnp.zeros_like(total)

    for i in range(NX):
        domain = ids[step * NX + i, 0]
        total[domain] += got[i].astype(F32)

    @pl.when(step == NY - 1)
    def _():
        tile[...] = jnp.zeros_like(tile)
        for k in range(DOMAINS):
            for to in range(NZ):
                parts[to, k * SHARD : (k + 1) * SHARD, :] = total[
                    k, to * SHARD : (to + 1) * SHARD, :
                ].astype(BF)
            tile[k * SG : (k + 1) * SG, :] = (
                total[k, PIECE : PIECE + SG, :] + total[k, PIECE + SG : PIECE + 2 * SG, :]
            )
        for k in range(NZ):
            outs[k][:PIECE, :] = parts[(z[0] + k) % NZ]
            outs[k][PIECE:, :] = tile[...].astype(BF)


def merge(ids, z, got):
    return call(
        merge_kernel,
        "merge",
        grid=(NY,),
        out_shape=(jax.ShapeDtypeStruct((BLOCK, GS), BF),) * NZ,
        in_specs=[SMEM, SMEM, pl.BlockSpec((NX, BLOCK, GS), lambda i: (i, 0, 0))],
        out_specs=(pl.BlockSpec((BLOCK, GS), lambda i: (0, 0)),) * NZ,
        scratch_shapes=[
            pltpu.VMEM((DOMAINS, BLOCK, GS), F32),
            pltpu.VMEM((NZ, PIECE, GS), BF),
            pltpu.VMEM((TILE, GS), F32),
        ],
    )(ids, z, got)


def finish_kernel(at, *refs):
    got, (sw, dw, d_shared, d_domain, b_shared, b_domain, wide) = refs[:NZ], refs[NZ:]
    shared = sw[...].astype(F32)
    summed = jnp.zeros((SHARD, GS), F32)
    for k in range(DOMAINS):
        part = slice(k * SHARD, (k + 1) * SHARD)
        share = got[0][part, :].astype(F32)
        for z in range(1, NZ):
            share = share + got[z][part, :].astype(F32)
        summed = summed + share * dw[k].astype(F32)
        d_domain[k] = share * shared
    d_shared[...] = summed
    tile = got[0][PIECE:, :].astype(F32)
    for z in range(1, NZ):
        tile = tile + got[z][PIECE:, :].astype(F32)
    wide[...] = jnp.zeros_like(wide)
    for k in range(DOMAINS):
        for q in range(SG):
            row = k * SG + q
            wide[k : k + 1, q * GS : (q + 1) * GS] = tile[row : row + 1, :]
    placed = pltpu.roll(wide[...], SLAB - at[0], 1)
    b_domain[...] = placed[:DOMAINS, :SHARD]
    b_shared[...] = jnp.sum(placed[:DOMAINS, :SHARD], axis=0, keepdims=True)


def finish(at, got, sw, dw):
    return call(
        finish_kernel,
        "finish",
        out_shape=(
            jax.ShapeDtypeStruct((SHARD, GS), F32),
            jax.ShapeDtypeStruct((DOMAINS, SHARD, GS), F32),
            jax.ShapeDtypeStruct((1, SHARD), F32),
            jax.ShapeDtypeStruct((DOMAINS, SHARD), F32),
        ),
        in_specs=[SMEM] + [VMEM] * (NZ + 2),
        out_specs=(VMEM,) * 4,
        scratch_shapes=[pltpu.VMEM((8, SLAB), F32)],
    )(at, *got, sw, dw)


def exchange(block, axes):
    return lax.all_to_all(block, axes, 0, 0, tiled=True)


def turned(block, k):
    pairs = []
    for section in range(SECTIONS):
        for y in range(NY):
            for z in range(NZ):
                to = (y * NY + section) * NZ + (z + k) % NZ
                pairs.append(((section * NY + y) * NZ + z, to))
    return lax.ppermute(block, ("zhi", "core", "y", "zlo"), pairs)


def swapped(block, k):
    pairs = [(section, section ^ k) for section in range(SECTIONS)]
    return lax.ppermute(block, ("zhi", "core"), pairs)


def after(first, *then):
    return lax.optimization_barrier((first, *then))[1:]


def body(stash, cotangent, domain_ids, shared_weight, domain_weight, shared_bias, domain_bias):
    stash = stash[0]
    sw, dw = shared_weight[0], domain_weight[0]
    section = jnp.reshape(2 * lax.axis_index("zhi") + lax.axis_index("core"), (1,))
    z = jnp.reshape(lax.axis_index("zlo"), (1,))
    at = PIECE * z + SHARD * lax.axis_index("x")

    plane_ids = exchange(
        jnp.broadcast_to(domain_ids[0], (NY * NX, 1, 128)), ("y", "x")
    ).reshape(NY * NX, 128)
    mine = prep(at, sw, dw, shared_bias, domain_bias[0])
    held = [turned(mine, k) for k in range(NZ)]
    picked = pick(plane_ids, z, held)
    got = exchange(picked, ("y", "x"))
    (late,) = after(picked, stash)
    parts = cut(section, late)
    others = [swapped(parts[k - 1], k) for k in range(1, SECTIONS)]
    x, top = gather(section, late, others, cotangent)

    slope, kernel = slopes(domain_ids, got, x)
    out, send = grads(section, top, slope, kernel, x)
    got = exchange(send, ("y", "x"))
    d_inputs = join(section, out[0], [swapped(out[k], k) for k in range(1, SECTIONS)])
    merged = merge(plane_ids, z, got)
    final = [turned(merged[k], k) for k in range(NZ)]
    d_shared, d_domain, b_shared, b_domain = finish(at, final, sw, dw)
    return (d_inputs[None], d_shared[None], d_domain[None], b_shared, b_domain[None])


def solution(mesh):
    fine = Mesh(mesh.devices.reshape(2, 2, NY, NZ, NX), ("zhi", "core", "y", "zlo", "x"))
    section, dp = ("zhi", "core"), ("y", "zlo", "x")
    in_specs = (
        P(section, dp, None),
        P(dp, None),
        P(dp),
        P(section, dp, None),
        P(section, None, dp, None),
        P(section, dp),
        P(section, None, dp),
    )
    out_specs = (
        P(section, dp, None),
        P(section, dp, None),
        P(section, None, dp, None),
        P(section, dp),
        P(section, None, dp),
    )
    return jax.shard_map(
        body, mesh=fine, in_specs=in_specs, out_specs=out_specs, check_vma=False
    )
```

```python
import jax
import jax.numpy as jnp
from jax import lax
from jax.experimental import pallas as pl
from jax.experimental.pallas import tpu as pltpu
from jax.sharding import Mesh, PartitionSpec as P

D = 3072
GS = 256
DOMAINS = 4
ROWS = 128
NY, NZ, NX = 4, 4, 4
SHARD = 48
SLAB = D // NY
SG = SLAB // GS
SECTIONS = 4
PIECE = NZ * SHARD
TILE = 16
BLOCK = PIECE + TILE
VMEM = pl.BlockSpec(memory_space=pltpu.VMEM)
SMEM = pl.BlockSpec(memory_space=pltpu.SMEM)
BF = jnp.bfloat16
F32 = jnp.float32
HEAVY = 10**11


def call(kernel, name, limit=48, weight=HEAVY, **rest):
    return pl.pallas_call(
        kernel,
        name=name,
        compiler_params=pltpu.CompilerParams(vmem_limit_bytes=limit * 1024 * 1024),
        cost_estimate=pl.CostEstimate(
            flops=weight, bytes_accessed=weight // 100, transcendentals=0
        ),
        **rest,
    )


def prep_kernel(at, sw, dw, sb, db, out, wide, tile):
    shared = sw[...].astype(F32)
    for k in range(DOMAINS):
        out[k * SHARD : (k + 1) * SHARD, :] = (shared * dw[k].astype(F32)).astype(BF)
    wide[...] = jnp.zeros_like(wide)
    wide[0:1, :SHARD] = sb[...].astype(F32)
    wide[1 : 1 + DOMAINS, :SHARD] = db[...].astype(F32)
    placed = pltpu.roll(wide[...], at[0], 1)
    tile[...] = jnp.zeros_like(tile)
    for k in range(1 + DOMAINS):
        for q in range(SG):
            row = k * SG + q
            tile[row : row + 1, :] = placed[k : k + 1, q * GS : (q + 1) * GS]
    out[PIECE:, :] = tile[...].astype(BF)


def prep(at, sw, dw, sb, db):
    return call(
        prep_kernel,
        "prep",
        limit=58,
        out_shape=jax.ShapeDtypeStruct((BLOCK, GS), BF),
        in_specs=[SMEM, VMEM, VMEM, VMEM, VMEM],
        out_specs=VMEM,
        scratch_shapes=[pltpu.VMEM((8, SLAB), F32), pltpu.VMEM((TILE, GS), F32)],
    )(at, sw, dw, sb, db)


def pick_kernel(ids, z, *refs):
    held, out = refs[:NZ], refs[NZ]
    step = pl.program_id(0)
    tile = held[0][PIECE:, :].astype(F32)
    for k in range(1, NZ):
        tile = tile + held[k][PIECE:, :].astype(F32)
    tile = tile.astype(BF)
    for i in range(out.shape[0]):
        start = pl.multiple_of(ids[step * out.shape[0] + i, 0] * SHARD, TILE)
        for k in range(NZ):
            to = pl.multiple_of(((z[0] + NZ - k) % NZ) * SHARD, TILE)
            out[i, pl.ds(to, SHARD), :] = held[k][pl.ds(start, SHARD), :]
        out[i, PIECE:, :] = tile


def pick(ids, z, held):
    return call(
        pick_kernel,
        "pick",
        grid=(2,),
        out_shape=jax.ShapeDtypeStruct((NY * NX, BLOCK, GS), BF),
        in_specs=[SMEM, SMEM] + [pl.BlockSpec((BLOCK, GS), lambda i: (0, 0))] * NZ,
        out_specs=pl.BlockSpec((NY * NX // 2, BLOCK, GS), lambda i: (i, 0, 0)),
    )(ids, z, *held)


def fixed(shape):
    return pl.BlockSpec(shape, lambda i, s: (0,) * len(shape))


def slab_of(k):
    return pl.BlockSpec((ROWS, SLAB), lambda i, s: (0, s[0] ^ k))


def cut_kernel(s, *refs):
    for k in range(1, SECTIONS):
        refs[SECTIONS - 2 + k][...] = refs[k - 1][...]


def cut(section, stash):
    quarter = jax.ShapeDtypeStruct((ROWS, SLAB), BF)
    return call(
        cut_kernel,
        "cut",
        out_shape=(quarter,) * (SECTIONS - 1),
        grid_spec=pltpu.PrefetchScalarGridSpec(
            num_scalar_prefetch=1,
            grid=(1,),
            in_specs=[slab_of(k) for k in range(1, SECTIONS)],
            out_specs=[fixed((ROWS, SLAB))] * (SECTIONS - 1),
        ),
    )(section, stash, stash, stash)


def gather_kernel(s, own, other1, other2, other3, cotangent, x, top):
    for k, part in enumerate((own, other1, other2, other3)):
        x[s[0] ^ k] = part[...]
    top[...] = cotangent[...]


def gather(section, stash, others, cotangent):
    return call(
        gather_kernel,
        "gather",
        weight=0,
        out_shape=(
            jax.ShapeDtypeStruct((SECTIONS, ROWS, SLAB), BF),
            jax.ShapeDtypeStruct((ROWS, SLAB), BF),
        ),
        grid_spec=pltpu.PrefetchScalarGridSpec(
            num_scalar_prefetch=1,
            grid=(1,),
            in_specs=[slab_of(0)] + [fixed((ROWS, SLAB))] * (SECTIONS - 1) + [slab_of(0)],
            out_specs=[fixed((SECTIONS, ROWS, SLAB)), fixed((ROWS, SLAB))],
        ),
    )(section, stash, *others, cotangent)


def slope_kernel(own, got, x, slope, kernel, offsets):
    domain = own[0]
    tile = got[0, PIECE:, :].astype(F32)
    for i in range(1, NX):
        tile = tile + got[i, PIECE:, :].astype(F32)
    offsets[...] = tile
    for z in range(NZ):
        for i in range(NX):
            at = (z * NX + i) * SHARD
            kernel[0, at : at + SHARD, :] = got[i, z * SHARD : (z + 1) * SHARD, :]
    for q in range(SG):
        lanes = slice(q * GS, (q + 1) * GS)
        offset = offsets[q : q + 1, :] + offsets[pl.ds((1 + domain) * SG + q, 1), :]
        pre = jnp.dot(x[0, :, lanes], kernel[0, lanes, :], preferred_element_type=F32) + offset
        sigma = jax.nn.sigmoid(pre)
        slope[0, :, lanes] = sigma * (1.0 + pre * (1.0 - sigma))


def slopes(own, got, x):
    tokens = pl.BlockSpec((1, ROWS, SLAB), lambda i: (i, 0, 0))
    return call(
        slope_kernel,
        "slopes",
        grid=(SECTIONS,),
        out_shape=(
            jax.ShapeDtypeStruct((SECTIONS, ROWS, SLAB), F32),
            jax.ShapeDtypeStruct((SECTIONS, SLAB, GS), BF),
        ),
        in_specs=[SMEM, pl.BlockSpec((NX, BLOCK, GS), lambda i: (i, 0, 0)), tokens],
        out_specs=(tokens, pl.BlockSpec((1, SLAB, GS), lambda i: (i, 0, 0))),
        scratch_shapes=[pltpu.VMEM((TILE, GS), F32)],
    )(own, got, x)


def grads_kernel(s, top, slope, kernel, x, out, send, above, tile):
    @pl.when(pl.program_id(0) == 0)
    def _():
        above[...] = top[...]

    tile[...] = jnp.zeros_like(tile)
    for q in range(SG):
        lanes = slice(q * GS, (q + 1) * GS)
        incoming = above[:, lanes].astype(F32)
        signal = (incoming * slope[0, :, lanes]).astype(BF)
        back = lax.dot_general(
            signal, kernel[0, lanes, :], (((1,), (1,)), ((), ())), preferred_element_type=F32
        )
        outgoing = (incoming + back).astype(BF)
        out[0, :, lanes] = outgoing
        above[:, lanes] = outgoing
        grad = lax.dot_general(
            x[0, :, lanes], signal, (((0,), (0,)), ((), ())), preferred_element_type=F32
        ).astype(BF)
        for row in range(q * GS, (q + 1) * GS, TILE):
            shard, inner = row // SHARD, row % SHARD
            at = shard // NX * SHARD + inner
            send[shard % NX, at : at + TILE, :] = grad[row - q * GS : row - q * GS + TILE]
        total = jnp.sum(signal.astype(F32), axis=0, keepdims=True)
        high = total.astype(BF).astype(F32)
        tile[q : q + 1, :] = high
        tile[SG + q : SG + q + 1, :] = total - high
    for i in range(NX):
        send[i, PIECE:, :] = tile[...].astype(BF)


def grads(section, top, slope, kernel, x):
    last = SECTIONS - 1
    tokens = pl.BlockSpec((1, ROWS, SLAB), lambda i, s: (last - i, 0, 0))
    return call(
        grads_kernel,
        "grads",
        out_shape=(
            jax.ShapeDtypeStruct((SECTIONS, ROWS, SLAB), BF),
            jax.ShapeDtypeStruct((SECTIONS * NX, BLOCK, GS), BF),
        ),
        grid_spec=pltpu.PrefetchScalarGridSpec(
            num_scalar_prefetch=1,
            grid=(SECTIONS,),
            in_specs=[
                fixed((ROWS, SLAB)),
                tokens,
                pl.BlockSpec((1, SLAB, GS), lambda i, s: (last - i, 0, 0)),
                tokens,
            ],
            out_specs=[
                pl.BlockSpec((1, ROWS, SLAB), lambda i, s: ((last - i) ^ s[0], 0, 0)),
                pl.BlockSpec((NX, BLOCK, GS), lambda i, s: (last - i, 0, 0)),
            ],
            scratch_shapes=[pltpu.VMEM((ROWS, SLAB), BF), pltpu.VMEM((TILE, GS), F32)],
        ),
    )(section, top, slope, kernel, x)


def join_kernel(s, own, other1, other2, other3, out):
    for k, part in enumerate((own, other1, other2, other3)):

        @pl.when(pl.program_id(0) == k)
        def _(part=part):
            out[...] = part[...]


def join(section, own, others):
    return call(
        join_kernel,
        "join",
        out_shape=jax.ShapeDtypeStruct((ROWS, D), BF),
        grid_spec=pltpu.PrefetchScalarGridSpec(
            num_scalar_prefetch=1,
            grid=(SECTIONS,),
            in_specs=[fixed((ROWS, SLAB))] * SECTIONS,
            out_specs=pl.BlockSpec((ROWS, SLAB), lambda i, s: (0, i ^ s[0])),
        ),
    )(section, own, *others)


def merge_kernel(ids, z, got, *refs):
    outs, (total, parts, tile) = refs[:NZ], refs[NZ:]
    step = pl.program_id(0)

    @pl.when(step == 0)
    def _():
        total[...] = jnp.zeros_like(total)

    for i in range(NX):
        domain = ids[step * NX + i, 0]
        total[domain] += got[i].astype(F32)

    @pl.when(step == NY - 1)
    def _():
        tile[...] = jnp.zeros_like(tile)
        for k in range(DOMAINS):
            for to in range(NZ):
                parts[to, k * SHARD : (k + 1) * SHARD, :] = total[
                    k, to * SHARD : (to + 1) * SHARD, :
                ].astype(BF)
            tile[k * SG : (k + 1) * SG, :] = (
                total[k, PIECE : PIECE + SG, :] + total[k, PIECE + SG : PIECE + 2 * SG, :]
            )
        for k in range(NZ):
            outs[k][:PIECE, :] = parts[(z[0] + k) % NZ]
            outs[k][PIECE:, :] = tile[...].astype(BF)


def merge(ids, z, got):
    return call(
        merge_kernel,
        "merge",
        grid=(NY,),
        out_shape=(jax.ShapeDtypeStruct((BLOCK, GS), BF),) * NZ,
        in_specs=[SMEM, SMEM, pl.BlockSpec((NX, BLOCK, GS), lambda i: (i, 0, 0))],
        out_specs=(pl.BlockSpec((BLOCK, GS), lambda i: (0, 0)),) * NZ,
        scratch_shapes=[
            pltpu.VMEM((DOMAINS, BLOCK, GS), F32),
            pltpu.VMEM((NZ, PIECE, GS), BF),
            pltpu.VMEM((TILE, GS), F32),
        ],
    )(ids, z, got)


def finish_kernel(at, *refs):
    got, (sw, dw, d_shared, d_domain, b_shared, b_domain, wide) = refs[:NZ], refs[NZ:]
    shared = sw[...].astype(F32)
    summed = jnp.zeros((SHARD, GS), F32)
    for k in range(DOMAINS):
        part = slice(k * SHARD, (k + 1) * SHARD)
        share = got[0][part, :].astype(F32)
        for z in range(1, NZ):
            share = share + got[z][part, :].astype(F32)
        summed = summed + share * dw[k].astype(F32)
        d_domain[k] = share * shared
    d_shared[...] = summed
    tile = got[0][PIECE:, :].astype(F32)
    for z in range(1, NZ):
        tile = tile + got[z][PIECE:, :].astype(F32)
    wide[...] = jnp.zeros_like(wide)
    for k in range(DOMAINS):
        for q in range(SG):
            row = k * SG + q
            wide[k : k + 1, q * GS : (q + 1) * GS] = tile[row : row + 1, :]
    placed = pltpu.roll(wide[...], SLAB - at[0], 1)
    b_domain[...] = placed[:DOMAINS, :SHARD]
    b_shared[...] = jnp.sum(placed[:DOMAINS, :SHARD], axis=0, keepdims=True)


def finish(at, got, sw, dw):
    return call(
        finish_kernel,
        "finish",
        out_shape=(
            jax.ShapeDtypeStruct((SHARD, GS), F32),
            jax.ShapeDtypeStruct((DOMAINS, SHARD, GS), F32),
            jax.ShapeDtypeStruct((1, SHARD), F32),
            jax.ShapeDtypeStruct((DOMAINS, SHARD), F32),
        ),
        in_specs=[SMEM] + [VMEM] * (NZ + 2),
        out_specs=(VMEM,) * 4,
        scratch_shapes=[pltpu.VMEM((8, SLAB), F32)],
    )(at, *got, sw, dw)


def exchange(block, axes):
    return lax.all_to_all(block, axes, 0, 0, tiled=True)


def turned(block, k):
    pairs = []
    for section in range(SECTIONS):
        for y in range(NY):
            for z in range(NZ):
                to = (y * NY + section) * NZ + (z + k) % NZ
                pairs.append(((section * NY + y) * NZ + z, to))
    return lax.ppermute(block, ("zhi", "core", "y", "zlo"), pairs)


def swapped(block, k):
    pairs = [(section, section ^ k) for section in range(SECTIONS)]
    return lax.ppermute(block, ("zhi", "core"), pairs)


def after(first, *then):
    return lax.optimization_barrier((first, *then))[1:]


def body(stash, cotangent, domain_ids, shared_weight, domain_weight, shared_bias, domain_bias):
    stash = stash[0]
    sw, dw = shared_weight[0], domain_weight[0]
    section = jnp.reshape(2 * lax.axis_index("zhi") + lax.axis_index("core"), (1,))
    z = jnp.reshape(lax.axis_index("zlo"), (1,))
    at = PIECE * z + SHARD * lax.axis_index("x")

    plane_ids = exchange(
        jnp.broadcast_to(domain_ids[0], (NY * NX, 1, 128)), ("y", "x")
    ).reshape(NY * NX, 128)
    mine = prep(at, sw, dw, shared_bias, domain_bias[0])
    (mine,) = after(plane_ids, mine)
    held = [turned(mine, k) for k in range(NZ)]
    picked = pick(plane_ids, z, held)
    got = exchange(picked, ("y", "x"))
    (late,) = after(picked, stash)
    parts = cut(section, late)
    others = [swapped(parts[k - 1], k) for k in range(1, SECTIONS)]
    x, top = gather(section, late, others, cotangent)

    slope, kernel = slopes(domain_ids, got, x)
    out, send = grads(section, top, slope, kernel, x)
    got = exchange(send, ("y", "x"))
    d_inputs = join(section, out[0], [swapped(out[k], k) for k in range(1, SECTIONS)])
    merged = merge(plane_ids, z, got)
    final = [turned(merged[k], k) for k in range(NZ)]
    d_shared, d_domain, b_shared, b_domain = finish(at, final, sw, dw)
    return (d_inputs[None], d_shared[None], d_domain[None], b_shared, b_domain[None])


def solution(mesh):
    fine = Mesh(mesh.devices.reshape(2, 2, NY, NZ, NX), ("zhi", "core", "y", "zlo", "x"))
    section, dp = ("zhi", "core"), ("y", "zlo", "x")
    in_specs = (
        P(section, dp, None),
        P(dp, None),
        P(dp),
        P(section, dp, None),
        P(section, None, dp, None),
        P(section, dp),
        P(section, None, dp),
    )
    out_specs = (
        P(section, dp, None),
        P(section, dp, None),
        P(section, None, dp, None),
        P(section, dp),
        P(section, None, dp),
    )
    return jax.shard_map(
        body, mesh=fine, in_specs=in_specs, out_specs=out_specs, check_vma=False
    )
```

```python
import jax
import jax.numpy as jnp
from jax import lax
from jax.experimental import pallas as pl
from jax.experimental.pallas import tpu as pltpu
from jax.sharding import Mesh, PartitionSpec as P

D = 3072
GS = 256
DOMAINS = 4
ROWS = 128
NY, NZ, NX = 4, 4, 4
SHARD = 48
SLAB = D // NY
SG = SLAB // GS
SECTIONS = 4
PIECE = NZ * SHARD
TILE = 16
BLOCK = PIECE + TILE
VMEM = pl.BlockSpec(memory_space=pltpu.VMEM)
SMEM = pl.BlockSpec(memory_space=pltpu.SMEM)
BF = jnp.bfloat16
F32 = jnp.float32
HEAVY = 10**11


def call(kernel, name, limit=48, weight=HEAVY, **rest):
    return pl.pallas_call(
        kernel,
        name=name,
        compiler_params=pltpu.CompilerParams(vmem_limit_bytes=limit * 1024 * 1024),
        cost_estimate=pl.CostEstimate(
            flops=weight, bytes_accessed=weight // 100, transcendentals=0
        ),
        **rest,
    )


def prep_kernel(at, sw, dw, sb, db, out, wide, tile):
    shared = sw[...].astype(F32)
    for k in range(DOMAINS):
        out[k * SHARD : (k + 1) * SHARD, :] = (shared * dw[k].astype(F32)).astype(BF)
    wide[...] = jnp.zeros_like(wide)
    wide[0:1, :SHARD] = sb[...].astype(F32)
    wide[1 : 1 + DOMAINS, :SHARD] = db[...].astype(F32)
    placed = pltpu.roll(wide[...], at[0], 1)
    tile[...] = jnp.zeros_like(tile)
    for k in range(1 + DOMAINS):
        for q in range(SG):
            row = k * SG + q
            tile[row : row + 1, :] = placed[k : k + 1, q * GS : (q + 1) * GS]
    out[PIECE:, :] = tile[...].astype(BF)


def prep(at, sw, dw, sb, db):
    return call(
        prep_kernel,
        "prep",
        limit=58,
        out_shape=jax.ShapeDtypeStruct((BLOCK, GS), BF),
        in_specs=[SMEM, VMEM, VMEM, VMEM, VMEM],
        out_specs=VMEM,
        scratch_shapes=[pltpu.VMEM((8, SLAB), F32), pltpu.VMEM((TILE, GS), F32)],
    )(at, sw, dw, sb, db)


def pick_kernel(ids, z, *refs):
    held, out = refs[:NZ], refs[NZ]
    step = pl.program_id(0)
    tile = held[0][PIECE:, :].astype(F32)
    for k in range(1, NZ):
        tile = tile + held[k][PIECE:, :].astype(F32)
    tile = tile.astype(BF)
    for i in range(out.shape[0]):
        start = pl.multiple_of(ids[step * out.shape[0] + i, 0] * SHARD, TILE)
        for k in range(NZ):
            to = pl.multiple_of(((z[0] + NZ - k) % NZ) * SHARD, TILE)
            out[i, pl.ds(to, SHARD), :] = held[k][pl.ds(start, SHARD), :]
        out[i, PIECE:, :] = tile


def pick(ids, z, held):
    return call(
        pick_kernel,
        "pick",
        grid=(2,),
        out_shape=jax.ShapeDtypeStruct((NY * NX, BLOCK, GS), BF),
        in_specs=[SMEM, SMEM] + [pl.BlockSpec((BLOCK, GS), lambda i: (0, 0))] * NZ,
        out_specs=pl.BlockSpec((NY * NX // 2, BLOCK, GS), lambda i: (i, 0, 0)),
    )(ids, z, *held)


def fixed(shape):
    return pl.BlockSpec(shape, lambda i, s: (0,) * len(shape))


def slab_of(k):
    return pl.BlockSpec((ROWS, SLAB), lambda i, s: (0, s[0] ^ k))


def cut_kernel(s, *refs):
    for k in range(1, SECTIONS):
        refs[SECTIONS - 2 + k][...] = refs[k - 1][...]


def cut(section, stash):
    quarter = jax.ShapeDtypeStruct((ROWS, SLAB), BF)
    return call(
        cut_kernel,
        "cut",
        out_shape=(quarter,) * (SECTIONS - 1),
        grid_spec=pltpu.PrefetchScalarGridSpec(
            num_scalar_prefetch=1,
            grid=(1,),
            in_specs=[slab_of(k) for k in range(1, SECTIONS)],
            out_specs=[fixed((ROWS, SLAB))] * (SECTIONS - 1),
        ),
    )(section, stash, stash, stash)


def gather_kernel(s, own, other1, other2, other3, cotangent, x, top):
    for k, part in enumerate((own, other1, other2, other3)):
        x[s[0] ^ k] = part[...]
    top[...] = cotangent[...]


def gather(section, stash, others, cotangent):
    return call(
        gather_kernel,
        "gather",
        weight=0,
        out_shape=(
            jax.ShapeDtypeStruct((SECTIONS, ROWS, SLAB), BF),
            jax.ShapeDtypeStruct((ROWS, SLAB), BF),
        ),
        grid_spec=pltpu.PrefetchScalarGridSpec(
            num_scalar_prefetch=1,
            grid=(1,),
            in_specs=[slab_of(0)] + [fixed((ROWS, SLAB))] * (SECTIONS - 1) + [slab_of(0)],
            out_specs=[fixed((SECTIONS, ROWS, SLAB)), fixed((ROWS, SLAB))],
        ),
    )(section, stash, *others, cotangent)


def slope_kernel(own, got, x, slope, kernel, offsets):
    domain = own[0]
    tile = got[0, PIECE:, :].astype(F32)
    for i in range(1, NX):
        tile = tile + got[i, PIECE:, :].astype(F32)
    offsets[...] = tile
    for z in range(NZ):
        for i in range(NX):
            at = (z * NX + i) * SHARD
            kernel[0, at : at + SHARD, :] = got[i, z * SHARD : (z + 1) * SHARD, :]
    for q in range(SG):
        lanes = slice(q * GS, (q + 1) * GS)
        offset = offsets[q : q + 1, :] + offsets[pl.ds((1 + domain) * SG + q, 1), :]
        pre = jnp.dot(x[0, :, lanes], kernel[0, lanes, :], preferred_element_type=F32) + offset
        sigma = jax.nn.sigmoid(pre)
        slope[0, :, lanes] = sigma * (1.0 + pre * (1.0 - sigma))


def slopes(own, got, x):
    tokens = pl.BlockSpec((1, ROWS, SLAB), lambda i: (i, 0, 0))
    return call(
        slope_kernel,
        "slopes",
        grid=(SECTIONS,),
        out_shape=(
            jax.ShapeDtypeStruct((SECTIONS, ROWS, SLAB), F32),
            jax.ShapeDtypeStruct((SECTIONS, SLAB, GS), BF),
        ),
        in_specs=[SMEM, pl.BlockSpec((NX, BLOCK, GS), lambda i: (i, 0, 0)), tokens],
        out_specs=(tokens, pl.BlockSpec((1, SLAB, GS), lambda i: (i, 0, 0))),
        scratch_shapes=[pltpu.VMEM((TILE, GS), F32)],
    )(own, got, x)


def grads_kernel(s, top, slope, kernel, x, out, send, above, tile):
    @pl.when(pl.program_id(0) == 0)
    def _():
        above[...] = top[...]

    tile[...] = jnp.zeros_like(tile)
    for q in range(SG):
        lanes = slice(q * GS, (q + 1) * GS)
        incoming = above[:, lanes].astype(F32)
        signal = (incoming * slope[0, :, lanes]).astype(BF)
        back = lax.dot_general(
            signal, kernel[0, lanes, :], (((1,), (1,)), ((), ())), preferred_element_type=F32
        )
        outgoing = (incoming + back).astype(BF)
        out[0, :, lanes] = outgoing
        above[:, lanes] = outgoing
        grad = lax.dot_general(
            x[0, :, lanes], signal, (((0,), (0,)), ((), ())), preferred_element_type=F32
        ).astype(BF)
        for row in range(q * GS, (q + 1) * GS, TILE):
            shard, inner = row // SHARD, row % SHARD
            at = shard // NX * SHARD + inner
            send[shard % NX, at : at + TILE, :] = grad[row - q * GS : row - q * GS + TILE]
        total = jnp.sum(signal.astype(F32), axis=0, keepdims=True)
        high = total.astype(BF).astype(F32)
        tile[q : q + 1, :] = high
        tile[SG + q : SG + q + 1, :] = total - high
    for i in range(NX):
        send[i, PIECE:, :] = tile[...].astype(BF)


def grads(section, top, slope, kernel, x):
    last = SECTIONS - 1
    tokens = pl.BlockSpec((1, ROWS, SLAB), lambda i, s: (last - i, 0, 0))
    return call(
        grads_kernel,
        "grads",
        out_shape=(
            pltpu.HBM((SECTIONS, ROWS, SLAB), BF),
            jax.ShapeDtypeStruct((SECTIONS * NX, BLOCK, GS), BF),
        ),
        grid_spec=pltpu.PrefetchScalarGridSpec(
            num_scalar_prefetch=1,
            grid=(SECTIONS,),
            in_specs=[
                fixed((ROWS, SLAB)),
                tokens,
                pl.BlockSpec((1, SLAB, GS), lambda i, s: (last - i, 0, 0)),
                tokens,
            ],
            out_specs=[
                pl.BlockSpec((1, ROWS, SLAB), lambda i, s: ((last - i) ^ s[0], 0, 0)),
                pl.BlockSpec((NX, BLOCK, GS), lambda i, s: (last - i, 0, 0)),
            ],
            scratch_shapes=[pltpu.VMEM((ROWS, SLAB), BF), pltpu.VMEM((TILE, GS), F32)],
        ),
    )(section, top, slope, kernel, x)


def split_kernel(out, *parts):
    for k in range(SECTIONS):
        parts[k][...] = out[k]


def split(out):
    return call(
        split_kernel,
        "split",
        out_shape=(jax.ShapeDtypeStruct((ROWS, SLAB), BF),) * SECTIONS,
        in_specs=[VMEM],
        out_specs=(VMEM,) * SECTIONS,
    )(out)


def join_kernel(s, own, other1, other2, other3, out):
    for k, part in enumerate((own, other1, other2, other3)):

        @pl.when(pl.program_id(0) == k)
        def _(part=part):
            out[...] = part[...]


def join(section, own, others):
    return call(
        join_kernel,
        "join",
        weight=0,
        out_shape=jax.ShapeDtypeStruct((ROWS, D), BF),
        grid_spec=pltpu.PrefetchScalarGridSpec(
            num_scalar_prefetch=1,
            grid=(SECTIONS,),
            in_specs=[fixed((ROWS, SLAB))] * SECTIONS,
            out_specs=pl.BlockSpec((ROWS, SLAB), lambda i, s: (0, i ^ s[0])),
        ),
    )(section, own, *others)


def merge_kernel(ids, z, got, *refs):
    outs, (total, parts, tile) = refs[:NZ], refs[NZ:]
    step = pl.program_id(0)

    @pl.when(step == 0)
    def _():
        total[...] = jnp.zeros_like(total)

    for i in range(NX):
        domain = ids[step * NX + i, 0]
        total[domain] += got[i].astype(F32)

    @pl.when(step == NY - 1)
    def _():
        tile[...] = jnp.zeros_like(tile)
        for k in range(DOMAINS):
            for to in range(NZ):
                parts[to, k * SHARD : (k + 1) * SHARD, :] = total[
                    k, to * SHARD : (to + 1) * SHARD, :
                ].astype(BF)
            tile[k * SG : (k + 1) * SG, :] = (
                total[k, PIECE : PIECE + SG, :] + total[k, PIECE + SG : PIECE + 2 * SG, :]
            )
        for k in range(NZ):
            outs[k][:PIECE, :] = parts[(z[0] + k) % NZ]
            outs[k][PIECE:, :] = tile[...].astype(BF)


def merge(ids, z, got):
    return call(
        merge_kernel,
        "merge",
        grid=(NY,),
        out_shape=(jax.ShapeDtypeStruct((BLOCK, GS), BF),) * NZ,
        in_specs=[SMEM, SMEM, pl.BlockSpec((NX, BLOCK, GS), lambda i: (i, 0, 0))],
        out_specs=(pl.BlockSpec((BLOCK, GS), lambda i: (0, 0)),) * NZ,
        scratch_shapes=[
            pltpu.VMEM((DOMAINS, BLOCK, GS), F32),
            pltpu.VMEM((NZ, PIECE, GS), BF),
            pltpu.VMEM((TILE, GS), F32),
        ],
    )(ids, z, got)


def total_kernel(a, b, c, d, out):
    both = a[...].astype(F32) + b[...].astype(F32)
    out[...] = (both + c[...].astype(F32) + d[...].astype(F32)).astype(BF)


def total(got):
    return call(
        total_kernel,
        "total",
        out_shape=jax.ShapeDtypeStruct((BLOCK, GS), BF),
        in_specs=[VMEM] * NZ,
        out_specs=VMEM,
    )(*got)


def finish_kernel(at, got, sw, dw, d_shared, d_domain, b_shared, b_domain, wide):
    shared = sw[...].astype(F32)
    summed = jnp.zeros((SHARD, GS), F32)
    for k in range(DOMAINS):
        share = got[k * SHARD : (k + 1) * SHARD, :].astype(F32)
        summed = summed + share * dw[k].astype(F32)
        d_domain[k] = share * shared
    d_shared[...] = summed
    tile = got[PIECE:, :].astype(F32)
    wide[...] = jnp.zeros_like(wide)
    for k in range(DOMAINS):
        for q in range(SG):
            row = k * SG + q
            wide[k : k + 1, q * GS : (q + 1) * GS] = tile[row : row + 1, :]
    placed = pltpu.roll(wide[...], SLAB - at[0], 1)
    b_domain[...] = placed[:DOMAINS, :SHARD]
    b_shared[...] = jnp.sum(placed[:DOMAINS, :SHARD], axis=0, keepdims=True)


def finish(at, got, sw, dw):
    return call(
        finish_kernel,
        "finish",
        out_shape=(
            jax.ShapeDtypeStruct((SHARD, GS), F32),
            jax.ShapeDtypeStruct((DOMAINS, SHARD, GS), F32),
            jax.ShapeDtypeStruct((1, SHARD), F32),
            jax.ShapeDtypeStruct((DOMAINS, SHARD), F32),
        ),
        in_specs=[SMEM, VMEM, VMEM, VMEM],
        out_specs=(VMEM,) * 4,
        scratch_shapes=[pltpu.VMEM((8, SLAB), F32)],
    )(at, got, sw, dw)


def exchange(block, axes):
    return lax.all_to_all(block, axes, 0, 0, tiled=True)


def turned(block, k):
    return lax.ppermute(block, "zlo", [(z, (z + k) % NZ) for z in range(NZ)])


def crossed(block):
    pairs = [(a * NY + b, b * NY + a) for a in range(SECTIONS) for b in range(NY)]
    return lax.ppermute(block, ("zhi", "core", "y"), pairs)


def swapped(block, k):
    pairs = [(section, section ^ k) for section in range(SECTIONS)]
    return lax.ppermute(block, ("zhi", "core"), pairs)


def after(first, *then):
    return lax.optimization_barrier((first, *then))[1:]


def body(stash, cotangent, domain_ids, shared_weight, domain_weight, shared_bias, domain_bias):
    stash = stash[0]
    sw, dw = shared_weight[0], domain_weight[0]
    section = jnp.reshape(2 * lax.axis_index("zhi") + lax.axis_index("core"), (1,))
    z = jnp.reshape(lax.axis_index("zlo"), (1,))
    at = PIECE * z + SHARD * lax.axis_index("x")

    mine = prep(at, sw, dw, shared_bias, domain_bias[0])
    (ids,) = after(mine, domain_ids)
    plane_ids = exchange(
        jnp.broadcast_to(ids[0], (NY * NX, 1, 128)), ("y", "x")
    ).reshape(NY * NX, 128)
    (mine,) = after(plane_ids, crossed(mine))
    held = [mine] + [turned(mine, k) for k in range(1, NZ)]
    picked = pick(plane_ids, z, held)
    got = exchange(picked, ("y", "x"))
    (late,) = after(picked, stash)
    parts = cut(section, late)
    others = [swapped(parts[k - 1], k) for k in range(1, SECTIONS)]
    x, top = gather(section, late, others, cotangent)

    slope, kernel = slopes(domain_ids, got, x)
    out, send = grads(section, top, slope, kernel, x)
    got = exchange(send, ("y", "x"))
    parts = split(out)
    d_inputs = join(section, parts[0], [swapped(parts[k], k) for k in range(1, SECTIONS)])
    (got,) = after(d_inputs, got)
    merged = merge(plane_ids, z, got)
    final = crossed(total([merged[0]] + [turned(merged[k], k) for k in range(1, NZ)]))
    d_shared, d_domain, b_shared, b_domain = finish(at, final, sw, dw)
    return (d_inputs[None], d_shared[None], d_domain[None], b_shared, b_domain[None])


def solution(mesh):
    fine = Mesh(mesh.devices.reshape(2, 2, NY, NZ, NX), ("zhi", "core", "y", "zlo", "x"))
    section, dp = ("zhi", "core"), ("y", "zlo", "x")
    in_specs = (
        P(section, dp, None),
        P(dp, None),
        P(dp),
        P(section, dp, None),
        P(section, None, dp, None),
        P(section, dp),
        P(section, None, dp),
    )
    out_specs = (
        P(section, dp, None),
        P(section, dp, None),
        P(section, None, dp, None),
        P(section, dp),
        P(section, None, dp),
    )
    return jax.shard_map(
        body, mesh=fine, in_specs=in_specs, out_specs=out_specs, check_vma=False
    )
```

```python
import jax
import jax.numpy as jnp
from jax import lax
from jax.experimental import pallas as pl
from jax.experimental.pallas import tpu as pltpu
from jax.sharding import Mesh, PartitionSpec as P

D = 3072
GS = 256
DOMAINS = 4
ROWS = 128
NY, NZ, NX = 4, 4, 4
SHARD = 48
SLAB = D // NY
SG = SLAB // GS
SECTIONS = 4
PIECE = NZ * SHARD
TILE = 16
BLOCK = PIECE + TILE
VMEM = pl.BlockSpec(memory_space=pltpu.VMEM)
SMEM = pl.BlockSpec(memory_space=pltpu.SMEM)
BF = jnp.bfloat16
F32 = jnp.float32
HEAVY = 10**11


def call(kernel, name, limit=48, weight=HEAVY, **rest):
    return pl.pallas_call(
        kernel,
        name=name,
        compiler_params=pltpu.CompilerParams(vmem_limit_bytes=limit * 1024 * 1024),
        cost_estimate=pl.CostEstimate(
            flops=weight, bytes_accessed=weight // 100, transcendentals=0
        ),
        **rest,
    )


def prep_kernel(at, own, sw, dw, sb, db, out, ids, wide, tile):
    ids[...] = jnp.full(ids.shape, own[0], jnp.int32)
    shared = sw[...].astype(F32)
    for k in range(DOMAINS):
        out[k * SHARD : (k + 1) * SHARD, :] = (shared * dw[k].astype(F32)).astype(BF)
    wide[...] = jnp.zeros_like(wide)
    wide[0:1, :SHARD] = sb[...].astype(F32)
    wide[1 : 1 + DOMAINS, :SHARD] = db[...].astype(F32)
    placed = pltpu.roll(wide[...], at[0], 1)
    tile[...] = jnp.zeros_like(tile)
    for k in range(1 + DOMAINS):
        for q in range(SG):
            row = k * SG + q
            tile[row : row + 1, :] = placed[k : k + 1, q * GS : (q + 1) * GS]
    out[PIECE:, :] = tile[...].astype(BF)


def prep(at, own, sw, dw, sb, db):
    return call(
        prep_kernel,
        "prep",
        limit=58,
        out_shape=(
            jax.ShapeDtypeStruct((BLOCK, GS), BF),
            jax.ShapeDtypeStruct((NY * NX, 1, 128), jnp.int32),
        ),
        in_specs=[SMEM, SMEM, VMEM, VMEM, VMEM, VMEM],
        out_specs=(VMEM, VMEM),
        scratch_shapes=[pltpu.VMEM((8, SLAB), F32), pltpu.VMEM((TILE, GS), F32)],
    )(at, own, sw, dw, sb, db)


def pick_kernel(ids, z, *refs):
    held, out = refs[:NZ], refs[NZ]
    step = pl.program_id(0)
    tile = held[0][PIECE:, :].astype(F32)
    for k in range(1, NZ):
        tile = tile + held[k][PIECE:, :].astype(F32)
    tile = tile.astype(BF)
    for i in range(out.shape[0]):
        start = pl.multiple_of(ids[step * out.shape[0] + i, 0] * SHARD, TILE)
        for k in range(NZ):
            to = pl.multiple_of(((z[0] + NZ - k) % NZ) * SHARD, TILE)
            out[i, pl.ds(to, SHARD), :] = held[k][pl.ds(start, SHARD), :]
        out[i, PIECE:, :] = tile


def pick(ids, z, held):
    return call(
        pick_kernel,
        "pick",
        grid=(2,),
        out_shape=jax.ShapeDtypeStruct((NY * NX, BLOCK, GS), BF),
        in_specs=[SMEM, SMEM] + [pl.BlockSpec((BLOCK, GS), lambda i: (0, 0))] * NZ,
        out_specs=pl.BlockSpec((NY * NX // 2, BLOCK, GS), lambda i: (i, 0, 0)),
    )(ids, z, *held)


def fixed(shape):
    return pl.BlockSpec(shape, lambda i, s: (0,) * len(shape))


def slab_of(k):
    return pl.BlockSpec((ROWS, SLAB), lambda i, s: (0, s[1] ^ k))


def cut_kernel(s, *refs):
    for k in range(1, SECTIONS):
        refs[SECTIONS - 2 + k][...] = refs[k - 1][...]


def cut(section, stash):
    quarter = jax.ShapeDtypeStruct((ROWS, SLAB), BF)
    return call(
        cut_kernel,
        "cut",
        out_shape=(quarter,) * (SECTIONS - 1),
        grid_spec=pltpu.PrefetchScalarGridSpec(
            num_scalar_prefetch=1,
            grid=(1,),
            in_specs=[slab_of(k) for k in range(1, SECTIONS)],
            out_specs=[fixed((ROWS, SLAB))] * (SECTIONS - 1),
        ),
    )(section, stash, stash, stash)


def gather_kernel(s, own, other1, other2, other3, cotangent, x, top):
    for k, part in enumerate((own, other1, other2, other3)):
        x[s[0] ^ k] = part[...]
    top[...] = cotangent[...]


def gather(section, stash, others, cotangent):
    return call(
        gather_kernel,
        "gather",
        weight=0,
        out_shape=(
            jax.ShapeDtypeStruct((SECTIONS, ROWS, SLAB), BF),
            jax.ShapeDtypeStruct((ROWS, SLAB), BF),
        ),
        grid_spec=pltpu.PrefetchScalarGridSpec(
            num_scalar_prefetch=1,
            grid=(1,),
            in_specs=[slab_of(0)] + [fixed((ROWS, SLAB))] * (SECTIONS - 1) + [slab_of(0)],
            out_specs=[fixed((SECTIONS, ROWS, SLAB)), fixed((ROWS, SLAB))],
        ),
    )(section, stash, *others, cotangent)


def layers_kernel(s, own, top, got, x, out, send, above, kernel, offsets, tile):
    @pl.when(pl.program_id(0) == 0)
    def _():
        above[...] = top[...]

    domain = own[0]
    biases = got[0, PIECE:, :].astype(F32)
    for i in range(1, NX):
        biases = biases + got[i, PIECE:, :].astype(F32)
    offsets[...] = biases
    for z in range(NZ):
        for i in range(NX):
            at = (z * NX + i) * SHARD
            kernel[at : at + SHARD, :] = got[i, z * SHARD : (z + 1) * SHARD, :]
    tile[...] = jnp.zeros_like(tile)
    for q in range(SG):
        lanes = slice(q * GS, (q + 1) * GS)
        inputs, weights = x[0, :, lanes], kernel[lanes, :]
        offset = offsets[q : q + 1, :] + offsets[pl.ds((1 + domain) * SG + q, 1), :]
        pre = jnp.dot(inputs, weights, preferred_element_type=F32) + offset
        sigma = jax.nn.sigmoid(pre)
        slope = sigma * (1.0 + pre * (1.0 - sigma))
        incoming = above[:, lanes].astype(F32)
        signal = (incoming * slope).astype(BF)
        back = lax.dot_general(
            signal, weights, (((1,), (1,)), ((), ())), preferred_element_type=F32
        )
        outgoing = (incoming + back).astype(BF)
        out[0, :, lanes] = outgoing
        above[:, lanes] = outgoing
        grad = lax.dot_general(
            inputs, signal, (((0,), (0,)), ((), ())), preferred_element_type=F32
        ).astype(BF)
        for row in range(q * GS, (q + 1) * GS, TILE):
            shard, inner = row // SHARD, row % SHARD
            at = shard // NX * SHARD + inner
            send[shard % NX, at : at + TILE, :] = grad[row - q * GS : row - q * GS + TILE]
        total = jnp.sum(signal.astype(F32), axis=0, keepdims=True)
        high = total.astype(BF).astype(F32)
        tile[q : q + 1, :] = high
        tile[SG + q : SG + q + 1, :] = total - high
    for i in range(NX):
        send[i, PIECE:, :] = tile[...].astype(BF)


def layers(section, own, top, got, x):
    last = SECTIONS - 1
    block = pl.BlockSpec((NX, BLOCK, GS), lambda i, s, d: (last - i, 0, 0))
    return call(
        layers_kernel,
        "layers",
        out_shape=(
            pltpu.HBM((SECTIONS, ROWS, SLAB), BF),
            jax.ShapeDtypeStruct((SECTIONS * NX, BLOCK, GS), BF),
        ),
        grid_spec=pltpu.PrefetchScalarGridSpec(
            num_scalar_prefetch=2,
            grid=(SECTIONS,),
            in_specs=[
                pl.BlockSpec((ROWS, SLAB), lambda i, s, d: (0, 0)),
                block,
                pl.BlockSpec((1, ROWS, SLAB), lambda i, s, d: (last - i, 0, 0)),
            ],
            out_specs=[
                pl.BlockSpec((1, ROWS, SLAB), lambda i, s, d: ((last - i) ^ s[0], 0, 0)),
                block,
            ],
            scratch_shapes=[
                pltpu.VMEM((ROWS, SLAB), BF),
                pltpu.VMEM((SLAB, GS), BF),
                pltpu.VMEM((TILE, GS), F32),
                pltpu.VMEM((TILE, GS), F32),
            ],
        ),
    )(section, own, top, got, x)


def split_kernel(out, *parts):
    for k in range(SECTIONS):
        parts[k][...] = out[k]


def split(out):
    return call(
        split_kernel,
        "split",
        out_shape=(jax.ShapeDtypeStruct((ROWS, SLAB), BF),) * SECTIONS,
        in_specs=[VMEM],
        out_specs=(VMEM,) * SECTIONS,
    )(out)


def join_kernel(s, own, other1, other2, other3, out):
    for k, part in enumerate((own, other1, other2, other3)):

        @pl.when(pl.program_id(0) == k)
        def _(part=part):
            out[...] = part[...]


def join(section, own, others):
    return call(
        join_kernel,
        "join",
        weight=0,
        out_shape=jax.ShapeDtypeStruct((ROWS, D), BF),
        grid_spec=pltpu.PrefetchScalarGridSpec(
            num_scalar_prefetch=1,
            grid=(SECTIONS,),
            in_specs=[fixed((ROWS, SLAB))] * SECTIONS,
            out_specs=pl.BlockSpec((ROWS, SLAB), lambda i, s: (0, i ^ s[1])),
        ),
    )(section, own, *others)


def merge_kernel(ids, z, got, *refs):
    outs, (total, parts, tile) = refs[:NZ], refs[NZ:]
    step = pl.program_id(0)

    @pl.when(step == 0)
    def _():
        total[...] = jnp.zeros_like(total)

    for i in range(got.shape[0]):
        domain = ids[step * got.shape[0] + i, 0]
        total[domain] += got[i].astype(F32)

    @pl.when(step == 1)
    def _():
        tile[...] = jnp.zeros_like(tile)
        for k in range(DOMAINS):
            for to in range(NZ):
                parts[to, k * SHARD : (k + 1) * SHARD, :] = total[
                    k, to * SHARD : (to + 1) * SHARD, :
                ].astype(BF)
            tile[k * SG : (k + 1) * SG, :] = (
                total[k, PIECE : PIECE + SG, :] + total[k, PIECE + SG : PIECE + 2 * SG, :]
            )
        for k in range(NZ):
            outs[k][:PIECE, :] = parts[(z[0] + k) % NZ]
            outs[k][PIECE:, :] = tile[...].astype(BF)


def merge(ids, z, got):
    return call(
        merge_kernel,
        "merge",
        grid=(2,),
        out_shape=(jax.ShapeDtypeStruct((BLOCK, GS), BF),) * NZ,
        in_specs=[SMEM, SMEM, pl.BlockSpec((NY * NX // 2, BLOCK, GS), lambda i: (i, 0, 0))],
        out_specs=(pl.BlockSpec((BLOCK, GS), lambda i: (0, 0)),) * NZ,
        scratch_shapes=[
            pltpu.VMEM((DOMAINS, BLOCK, GS), F32),
            pltpu.VMEM((NZ, PIECE, GS), BF),
            pltpu.VMEM((TILE, GS), F32),
        ],
    )(ids, z, got)


def finish_kernel(at, *refs):
    got, (sw, dw, d_shared, d_domain, b_shared, b_domain, wide) = refs[:NZ], refs[NZ:]
    shared = sw[...].astype(F32)
    summed = jnp.zeros((SHARD, GS), F32)
    for k in range(DOMAINS):
        part = slice(k * SHARD, (k + 1) * SHARD)
        share = got[0][part, :].astype(F32)
        for z in range(1, NZ):
            share = share + got[z][part, :].astype(F32)
        summed = summed + share * dw[k].astype(F32)
        d_domain[k] = share * shared
    d_shared[...] = summed
    tile = got[0][PIECE:, :].astype(F32)
    for z in range(1, NZ):
        tile = tile + got[z][PIECE:, :].astype(F32)
    wide[...] = jnp.zeros_like(wide)
    for k in range(DOMAINS):
        for q in range(SG):
            row = k * SG + q
            wide[k : k + 1, q * GS : (q + 1) * GS] = tile[row : row + 1, :]
    placed = pltpu.roll(wide[...], SLAB - at[0], 1)
    b_domain[...] = placed[:DOMAINS, :SHARD]
    b_shared[...] = jnp.sum(placed[:DOMAINS, :SHARD], axis=0, keepdims=True)


def finish(at, got, sw, dw):
    return call(
        finish_kernel,
        "finish",
        out_shape=(
            jax.ShapeDtypeStruct((SHARD, GS), F32),
            jax.ShapeDtypeStruct((DOMAINS, SHARD, GS), F32),
            jax.ShapeDtypeStruct((1, SHARD), F32),
            jax.ShapeDtypeStruct((DOMAINS, SHARD), F32),
        ),
        in_specs=[SMEM] + [VMEM] * (NZ + 2),
        out_specs=(VMEM,) * 4,
        scratch_shapes=[pltpu.VMEM((8, SLAB), F32)],
    )(at, *got, sw, dw)


def exchange(block, axes):
    return lax.all_to_all(block, axes, 0, 0, tiled=True)


def flip(z):
    return z % 2 * 2


def turned(block, k, home):
    pairs = []
    for a in range(SECTIONS):
        for b in range(NY):
            for z in range(NZ):
                later = (z + k) % NZ
                to = (b, a ^ flip(z)) if home else (b ^ flip(later), a)
                pairs.append(((a * NY + b) * NZ + z, (to[0] * NY + to[1]) * NZ + later))
    return lax.ppermute(block, ("zhi", "core", "y", "zlo"), pairs)


def swapped(block, k):
    pairs = [(section, section ^ k) for section in range(SECTIONS)]
    return lax.ppermute(block, ("zhi", "core"), pairs)


def after(first, *then):
    return lax.optimization_barrier((first, *then))[1:]


def body(stash, cotangent, domain_ids, shared_weight, domain_weight, shared_bias, domain_bias):
    stash = stash[0]
    sw, dw = shared_weight[0], domain_weight[0]
    section = 2 * lax.axis_index("zhi") + lax.axis_index("core")
    section = jnp.stack([section, section ^ flip(lax.axis_index("zlo"))])
    z = jnp.reshape(lax.axis_index("zlo"), (1,))
    at = PIECE * z + SHARD * lax.axis_index("x")

    mine, ids = prep(at, domain_ids, sw, dw, shared_bias, domain_bias[0])
    plane_ids = exchange(ids, ("y", "x")).reshape(NY * NX, 128)
    held = [turned(mine, k, False) for k in range(NZ)]
    picked = pick(plane_ids, z, held)
    got = exchange(picked, ("y", "x"))
    (late,) = after(picked, stash)
    parts = cut(section, late)
    others = [swapped(parts[k - 1], k) for k in range(1, SECTIONS)]
    x, top = gather(section, late, others, cotangent)

    out, send = layers(section, domain_ids, top, got, x)
    got = exchange(send, ("y", "x"))
    parts = split(out)
    d_inputs = join(section, parts[0], [swapped(parts[k], k) for k in range(1, SECTIONS)])
    (got,) = after(d_inputs, got)
    merged = merge(plane_ids, z, got)
    final = [turned(merged[k], k, True) for k in range(NZ)]
    d_shared, d_domain, b_shared, b_domain = finish(at, final, sw, dw)
    return (d_inputs[None], d_shared[None], d_domain[None], b_shared, b_domain[None])


def solution(mesh):
    fine = Mesh(mesh.devices.reshape(2, 2, NY, NZ, NX), ("zhi", "core", "y", "zlo", "x"))
    section, dp = ("zhi", "core"), ("y", "zlo", "x")
    in_specs = (
        P(section, dp, None),
        P(dp, None),
        P(dp),
        P(section, dp, None),
        P(section, None, dp, None),
        P(section, dp),
        P(section, None, dp),
    )
    out_specs = (
        P(section, dp, None),
        P(section, dp, None),
        P(section, None, dp, None),
        P(section, dp),
        P(section, None, dp),
    )
    return jax.shard_map(
        body, mesh=fine, in_specs=in_specs, out_specs=out_specs, check_vma=False
    )
```

```python
import jax
import jax.numpy as jnp
from jax import lax
from jax.experimental import pallas as pl
from jax.experimental.pallas import tpu as pltpu
from jax.sharding import Mesh, PartitionSpec as P

D = 3072
GS = 256
DOMAINS = 4
ROWS = 128
NY, NZ, NX = 4, 4, 4
SHARD = 48
SLAB = D // NY
SG = SLAB // GS
SECTIONS = 4
PIECE = NZ * SHARD
TILE = 16
BLOCK = PIECE + TILE
VMEM = pl.BlockSpec(memory_space=pltpu.VMEM)
SMEM = pl.BlockSpec(memory_space=pltpu.SMEM)
BF = jnp.bfloat16
F32 = jnp.float32
HEAVY = 10**11


def call(kernel, name, limit=48, weight=HEAVY, **rest):
    return pl.pallas_call(
        kernel,
        name=name,
        compiler_params=pltpu.CompilerParams(vmem_limit_bytes=limit * 1024 * 1024),
        cost_estimate=pl.CostEstimate(
            flops=weight, bytes_accessed=weight // 100, transcendentals=0
        ),
        **rest,
    )


def prep_kernel(at, own, sw, dw, sb, db, out, ids, wide, tile):
    ids[...] = jnp.full(ids.shape, own[0], jnp.int32)
    shared = sw[...].astype(F32)
    for k in range(DOMAINS):
        out[k * SHARD : (k + 1) * SHARD, :] = (shared * dw[k].astype(F32)).astype(BF)
    wide[...] = jnp.zeros_like(wide)
    wide[0:1, :SHARD] = sb[...].astype(F32)
    wide[1 : 1 + DOMAINS, :SHARD] = db[...].astype(F32)
    placed = pltpu.roll(wide[...], at[0], 1)
    tile[...] = jnp.zeros_like(tile)
    for k in range(1 + DOMAINS):
        for q in range(SG):
            row = k * SG + q
            tile[row : row + 1, :] = placed[k : k + 1, q * GS : (q + 1) * GS]
    out[PIECE:, :] = tile[...].astype(BF)


def prep(at, own, sw, dw, sb, db):
    return call(
        prep_kernel,
        "prep",
        limit=58,
        out_shape=(
            jax.ShapeDtypeStruct((BLOCK, GS), BF),
            jax.ShapeDtypeStruct((NY * NX, 1, 128), jnp.int32),
        ),
        in_specs=[SMEM, SMEM, VMEM, VMEM, VMEM, VMEM],
        out_specs=(VMEM, VMEM),
        scratch_shapes=[pltpu.VMEM((8, SLAB), F32), pltpu.VMEM((TILE, GS), F32)],
    )(at, own, sw, dw, sb, db)


def pick_kernel(ids, z, *refs):
    held, out = [refs[0], refs[1], refs[3], refs[2]], refs[NZ]
    step = pl.program_id(0)
    tile = held[0][PIECE:, :].astype(F32)
    for k in range(1, NZ):
        tile = tile + held[k][PIECE:, :].astype(F32)
    tile = tile.astype(BF)
    for i in range(out.shape[0]):
        start = pl.multiple_of(ids[step * out.shape[0] + i, 0] * SHARD, TILE)
        for k in range(NZ):
            to = pl.multiple_of(((z[0] + NZ - k) % NZ) * SHARD, TILE)
            out[i, pl.ds(to, SHARD), :] = held[k][pl.ds(start, SHARD), :]
        out[i, PIECE:, :] = tile


def pick(ids, z, held):
    return call(
        pick_kernel,
        "pick",
        grid=(2,),
        out_shape=jax.ShapeDtypeStruct((NY * NX, BLOCK, GS), BF),
        in_specs=[SMEM, SMEM] + [pl.BlockSpec((BLOCK, GS), lambda i: (0, 0))] * NZ,
        out_specs=pl.BlockSpec((NY * NX // 2, BLOCK, GS), lambda i: (i, 0, 0)),
    )(ids, z, held[0], held[1], held[3], held[2])


def fixed(shape):
    return pl.BlockSpec(shape, lambda i, s: (0,) * len(shape))


def slab_of(k):
    return pl.BlockSpec((ROWS, SLAB), lambda i, s: (0, s[1] ^ k))


def cut_kernel(s, *refs):
    for k in range(1, SECTIONS):
        refs[SECTIONS - 2 + k][...] = refs[k - 1][...]


def cut(section, stash):
    quarter = jax.ShapeDtypeStruct((ROWS, SLAB), BF)
    return call(
        cut_kernel,
        "cut",
        out_shape=(quarter,) * (SECTIONS - 1),
        grid_spec=pltpu.PrefetchScalarGridSpec(
            num_scalar_prefetch=1,
            grid=(1,),
            in_specs=[slab_of(k) for k in range(1, SECTIONS)],
            out_specs=[fixed((ROWS, SLAB))] * (SECTIONS - 1),
        ),
    )(section, stash, stash, stash)


def gather_kernel(s, other3, other2, other1, own, cotangent, x, top):
    for k, part in enumerate((own, other1, other2, other3)):
        x[s[0] ^ k] = part[...]
    top[...] = cotangent[...]


def gather(section, stash, others, cotangent):
    return call(
        gather_kernel,
        "gather",
        weight=0,
        out_shape=(
            jax.ShapeDtypeStruct((SECTIONS, ROWS, SLAB), BF),
            jax.ShapeDtypeStruct((ROWS, SLAB), BF),
        ),
        grid_spec=pltpu.PrefetchScalarGridSpec(
            num_scalar_prefetch=1,
            grid=(1,),
            in_specs=[fixed((ROWS, SLAB))] * (SECTIONS - 1) + [slab_of(0)] * 2,
            out_specs=[fixed((SECTIONS, ROWS, SLAB)), fixed((ROWS, SLAB))],
        ),
    )(section, *others[::-1], stash, cotangent)


def layers_kernel(s, own, top, got, x, out, send, above, kernel, offsets, tile):
    @pl.when(pl.program_id(0) == 0)
    def _():
        above[...] = top[...]

    domain = own[0]
    biases = got[0, PIECE:, :].astype(F32)
    for i in range(1, NX):
        biases = biases + got[i, PIECE:, :].astype(F32)
    offsets[...] = biases
    for z in range(NZ):
        for i in range(NX):
            at = (z * NX + i) * SHARD
            kernel[at : at + SHARD, :] = got[i, z * SHARD : (z + 1) * SHARD, :]
    tile[...] = jnp.zeros_like(tile)
    for q in range(SG):
        lanes = slice(q * GS, (q + 1) * GS)
        inputs, weights = x[0, :, lanes], kernel[lanes, :]
        offset = offsets[q : q + 1, :] + offsets[pl.ds((1 + domain) * SG + q, 1), :]
        pre = jnp.dot(inputs, weights, preferred_element_type=F32) + offset
        sigma = jax.nn.sigmoid(pre)
        slope = sigma * (1.0 + pre * (1.0 - sigma))
        incoming = above[:, lanes].astype(F32)
        signal = (incoming * slope).astype(BF)
        back = lax.dot_general(
            signal, weights, (((1,), (1,)), ((), ())), preferred_element_type=F32
        )
        outgoing = (incoming + back).astype(BF)
        out[0, :, lanes] = outgoing
        above[:, lanes] = outgoing
        grad = lax.dot_general(
            inputs, signal, (((0,), (0,)), ((), ())), preferred_element_type=F32
        ).astype(BF)
        for row in range(q * GS, (q + 1) * GS, TILE):
            shard, inner = row // SHARD, row % SHARD
            at = shard // NX * SHARD + inner
            send[shard % NX, at : at + TILE, :] = grad[row - q * GS : row - q * GS + TILE]
        total = jnp.sum(signal.astype(F32), axis=0, keepdims=True)
        high = total.astype(BF).astype(F32)
        tile[q : q + 1, :] = high
        tile[SG + q : SG + q + 1, :] = total - high
    for i in range(NX):
        send[i, PIECE:, :] = tile[...].astype(BF)


def layers(section, own, top, got, x):
    last = SECTIONS - 1
    block = pl.BlockSpec((NX, BLOCK, GS), lambda i, s, d: (last - i, 0, 0))
    return call(
        layers_kernel,
        "layers",
        out_shape=(
            pltpu.HBM((SECTIONS, ROWS, SLAB), BF),
            jax.ShapeDtypeStruct((SECTIONS * NX, BLOCK, GS), BF),
        ),
        grid_spec=pltpu.PrefetchScalarGridSpec(
            num_scalar_prefetch=2,
            grid=(SECTIONS,),
            in_specs=[
                pl.BlockSpec((ROWS, SLAB), lambda i, s, d: (0, 0)),
                block,
                pl.BlockSpec((1, ROWS, SLAB), lambda i, s, d: (last - i, 0, 0)),
            ],
            out_specs=[
                pl.BlockSpec((1, ROWS, SLAB), lambda i, s, d: ((last - i) ^ s[0], 0, 0)),
                block,
            ],
            scratch_shapes=[
                pltpu.VMEM((ROWS, SLAB), BF),
                pltpu.VMEM((SLAB, GS), BF),
                pltpu.VMEM((TILE, GS), F32),
                pltpu.VMEM((TILE, GS), F32),
            ],
        ),
    )(section, own, top, got, x)


def split_kernel(out, *parts):
    for k in range(SECTIONS):
        parts[k][...] = out[k]


def split(out):
    return call(
        split_kernel,
        "split",
        out_shape=(jax.ShapeDtypeStruct((ROWS, SLAB), BF),) * SECTIONS,
        in_specs=[VMEM],
        out_specs=(VMEM,) * SECTIONS,
    )(out)


def join_kernel(s, other3, other2, other1, own, out):
    for k, part in enumerate((own, other1, other2, other3)):

        @pl.when(pl.program_id(0) == k)
        def _(part=part):
            out[...] = part[...]


def join(section, own, others):
    return call(
        join_kernel,
        "join",
        weight=0,
        out_shape=jax.ShapeDtypeStruct((ROWS, D), BF),
        grid_spec=pltpu.PrefetchScalarGridSpec(
            num_scalar_prefetch=1,
            grid=(SECTIONS,),
            in_specs=[fixed((ROWS, SLAB))] * SECTIONS,
            out_specs=pl.BlockSpec((ROWS, SLAB), lambda i, s: (0, i ^ s[1])),
        ),
    )(section, *others[::-1], own)


def merge_kernel(ids, z, got, *refs):
    outs, (total, parts, tile) = refs[:NZ], refs[NZ:]
    step = pl.program_id(0)

    @pl.when(step == 0)
    def _():
        total[...] = jnp.zeros_like(total)

    for i in range(got.shape[0]):
        domain = ids[step * got.shape[0] + i, 0]
        total[domain] += got[i].astype(F32)

    @pl.when(step == 1)
    def _():
        tile[...] = jnp.zeros_like(tile)
        for k in range(DOMAINS):
            for to in range(NZ):
                parts[to, k * SHARD : (k + 1) * SHARD, :] = total[
                    k, to * SHARD : (to + 1) * SHARD, :
                ].astype(BF)
            tile[k * SG : (k + 1) * SG, :] = (
                total[k, PIECE : PIECE + SG, :] + total[k, PIECE + SG : PIECE + 2 * SG, :]
            )
        for k in range(NZ):
            outs[k][:PIECE, :] = parts[(z[0] + k) % NZ]
            outs[k][PIECE:, :] = tile[...].astype(BF)


def merge(ids, z, got):
    return call(
        merge_kernel,
        "merge",
        grid=(2,),
        out_shape=(jax.ShapeDtypeStruct((BLOCK, GS), BF),) * NZ,
        in_specs=[SMEM, SMEM, pl.BlockSpec((NY * NX // 2, BLOCK, GS), lambda i: (i, 0, 0))],
        out_specs=(pl.BlockSpec((BLOCK, GS), lambda i: (0, 0)),) * NZ,
        scratch_shapes=[
            pltpu.VMEM((DOMAINS, BLOCK, GS), F32),
            pltpu.VMEM((NZ, PIECE, GS), BF),
            pltpu.VMEM((TILE, GS), F32),
        ],
    )(ids, z, got)


def finish_kernel(at, *refs):
    got, (sw, dw, d_shared, d_domain, b_shared, b_domain, wide) = refs[:NZ], refs[NZ:]
    shared = sw[...].astype(F32)
    summed = jnp.zeros((SHARD, GS), F32)
    for k in range(DOMAINS):
        part = slice(k * SHARD, (k + 1) * SHARD)
        share = got[0][part, :].astype(F32)
        for z in range(1, NZ):
            share = share + got[z][part, :].astype(F32)
        summed = summed + share * dw[k].astype(F32)
        d_domain[k] = share * shared
    d_shared[...] = summed
    tile = got[0][PIECE:, :].astype(F32)
    for z in range(1, NZ):
        tile = tile + got[z][PIECE:, :].astype(F32)
    wide[...] = jnp.zeros_like(wide)
    for k in range(DOMAINS):
        for q in range(SG):
            row = k * SG + q
            wide[k : k + 1, q * GS : (q + 1) * GS] = tile[row : row + 1, :]
    placed = pltpu.roll(wide[...], SLAB - at[0], 1)
    b_domain[...] = placed[:DOMAINS, :SHARD]
    b_shared[...] = jnp.sum(placed[:DOMAINS, :SHARD], axis=0, keepdims=True)


def finish(at, got, sw, dw):
    return call(
        finish_kernel,
        "finish",
        out_shape=(
            jax.ShapeDtypeStruct((SHARD, GS), F32),
            jax.ShapeDtypeStruct((DOMAINS, SHARD, GS), F32),
            jax.ShapeDtypeStruct((1, SHARD), F32),
            jax.ShapeDtypeStruct((DOMAINS, SHARD), F32),
        ),
        in_specs=[SMEM] + [VMEM] * (NZ + 2),
        out_specs=(VMEM,) * 4,
        scratch_shapes=[pltpu.VMEM((8, SLAB), F32)],
    )(at, got[2], got[1], got[3], got[0], sw, dw)


def exchange(block, axes):
    return lax.all_to_all(block, axes, 0, 0, tiled=True)


def flip(z):
    return z % 2 * 2


def turned(block, k, home):
    pairs = []
    for a in range(SECTIONS):
        for b in range(NY):
            for z in range(NZ):
                later = (z + k) % NZ
                to = (b, a ^ flip(z)) if home else (b ^ flip(later), a)
                pairs.append(((a * NY + b) * NZ + z, (to[0] * NY + to[1]) * NZ + later))
    return lax.ppermute(block, ("zhi", "core", "y", "zlo"), pairs)


def swapped(block, k):
    pairs = [(section, section ^ k) for section in range(SECTIONS)]
    return lax.ppermute(block, ("zhi", "core"), pairs)


def after(first, *then):
    return lax.optimization_barrier((first, *then))[1:]


def body(stash, cotangent, domain_ids, shared_weight, domain_weight, shared_bias, domain_bias):
    stash = stash[0]
    sw, dw = shared_weight[0], domain_weight[0]
    section = 2 * lax.axis_index("zhi") + lax.axis_index("core")
    section = jnp.stack([section, section ^ flip(lax.axis_index("zlo"))])
    z = jnp.reshape(lax.axis_index("zlo"), (1,))
    at = PIECE * z + SHARD * lax.axis_index("x")

    mine, ids = prep(at, domain_ids, sw, dw, shared_bias, domain_bias[0])
    plane_ids = exchange(ids, ("y", "x")).reshape(NY * NX, 128)
    held = [turned(mine, k, False) for k in range(NZ)]
    picked = pick(plane_ids, z, held)
    got = exchange(picked, ("y", "x"))
    (late,) = after(picked, stash)
    parts = cut(section, late)
    others = [swapped(parts[k - 1], k) for k in range(1, SECTIONS)]
    x, top = gather(section, late, others, cotangent)

    out, send = layers(section, domain_ids, top, got, x)
    got = exchange(send, ("y", "x"))
    parts = split(out)
    d_inputs = join(section, parts[0], [swapped(parts[k], k) for k in range(1, SECTIONS)])
    (got,) = after(d_inputs, got)
    merged = merge(plane_ids, z, got)
    final = [turned(merged[k], k, True) for k in range(NZ)]
    d_shared, d_domain, b_shared, b_domain = finish(at, final, sw, dw)
    return (d_inputs[None], d_shared[None], d_domain[None], b_shared, b_domain[None])


def solution(mesh):
    fine = Mesh(mesh.devices.reshape(2, 2, NY, NZ, NX), ("zhi", "core", "y", "zlo", "x"))
    section, dp = ("zhi", "core"), ("y", "zlo", "x")
    in_specs = (
        P(section, dp, None),
        P(dp, None),
        P(dp),
        P(section, dp, None),
        P(section, None, dp, None),
        P(section, dp),
        P(section, None, dp),
    )
    out_specs = (
        P(section, dp, None),
        P(section, dp, None),
        P(section, None, dp, None),
        P(section, dp),
        P(section, None, dp),
    )
    return jax.shard_map(
        body, mesh=fine, in_specs=in_specs, out_specs=out_specs, check_vma=False
    )
```

```python
import jax
import jax.numpy as jnp
from jax import lax
from jax.experimental import pallas as pl
from jax.experimental.pallas import tpu as pltpu
from jax.sharding import Mesh, PartitionSpec as P

D = 3072
GS = 256
DOMAINS = 4
ROWS = 128
NY, NZ, NX = 4, 4, 4
SHARD = 48
SLAB = D // NY
SG = SLAB // GS
SECTIONS = 4
PIECE = NZ * SHARD
TILE = 16
BLOCK = PIECE + TILE
VMEM = pl.BlockSpec(memory_space=pltpu.VMEM)
SMEM = pl.BlockSpec(memory_space=pltpu.SMEM)
BF = jnp.bfloat16
F32 = jnp.float32
HEAVY = 10**11


def call(kernel, name, limit=48, weight=HEAVY, **rest):
    return pl.pallas_call(
        kernel,
        name=name,
        compiler_params=pltpu.CompilerParams(vmem_limit_bytes=limit * 1024 * 1024),
        cost_estimate=pl.CostEstimate(
            flops=weight, bytes_accessed=weight // 100, transcendentals=0
        ),
        **rest,
    )


def prep_kernel(at, own, sw, dw, sb, db, out, ids, wide, tile):
    ids[...] = jnp.full(ids.shape, own[0], jnp.int32)
    shared = sw[...].astype(F32)
    for k in range(DOMAINS):
        out[k * SHARD : (k + 1) * SHARD, :] = (shared * dw[k].astype(F32)).astype(BF)
    wide[...] = jnp.zeros_like(wide)
    wide[0:1, :SHARD] = sb[...].astype(F32)
    wide[1 : 1 + DOMAINS, :SHARD] = db[...].astype(F32)
    placed = pltpu.roll(wide[...], at[0], 1)
    tile[...] = jnp.zeros_like(tile)
    for k in range(1 + DOMAINS):
        for q in range(SG):
            row = k * SG + q
            tile[row : row + 1, :] = placed[k : k + 1, q * GS : (q + 1) * GS]
    out[PIECE:, :] = tile[...].astype(BF)


def prep(at, own, sw, dw, sb, db):
    return call(
        prep_kernel,
        "prep",
        limit=58,
        out_shape=(
            jax.ShapeDtypeStruct((BLOCK, GS), BF),
            jax.ShapeDtypeStruct((NY * NX, 1, 128), jnp.int32),
        ),
        in_specs=[SMEM, SMEM, VMEM, VMEM, VMEM, VMEM],
        out_specs=(VMEM, VMEM),
        scratch_shapes=[pltpu.VMEM((8, SLAB), F32), pltpu.VMEM((TILE, GS), F32)],
    )(at, own, sw, dw, sb, db)


def pick_kernel(ids, z, *refs):
    held, out = [refs[0], refs[1], refs[3], refs[2]], refs[NZ]
    step = pl.program_id(0)
    tile = held[0][PIECE:, :].astype(F32)
    for k in range(1, NZ):
        tile = tile + held[k][PIECE:, :].astype(F32)
    tile = tile.astype(BF)
    for i in range(out.shape[0]):
        start = pl.multiple_of(ids[step * out.shape[0] + i, 0] * SHARD, TILE)
        for k in range(NZ):
            to = pl.multiple_of(((z[0] + NZ - k) % NZ) * SHARD, TILE)
            out[i, pl.ds(to, SHARD), :] = held[k][pl.ds(start, SHARD), :]
        out[i, PIECE:, :] = tile


def pick(ids, z, held):
    return call(
        pick_kernel,
        "pick",
        grid=(1,),
        out_shape=jax.ShapeDtypeStruct((NY * NX, BLOCK, GS), BF),
        in_specs=[SMEM, SMEM] + [pl.BlockSpec((BLOCK, GS), lambda i: (0, 0))] * NZ,
        out_specs=pl.BlockSpec((NY * NX, BLOCK, GS), lambda i: (i, 0, 0)),
    )(ids, z, held[0], held[1], held[3], held[2])


def fixed(shape):
    return pl.BlockSpec(shape, lambda i, s: (0,) * len(shape))


def slab_of(k):
    return pl.BlockSpec((ROWS, SLAB), lambda i, s: (0, s[1] ^ k))


def cut_kernel(s, *refs):
    for k in range(1, SECTIONS):
        refs[SECTIONS - 2 + k][...] = refs[k - 1][...]


def cut(section, stash):
    quarter = jax.ShapeDtypeStruct((ROWS, SLAB), BF)
    return call(
        cut_kernel,
        "cut",
        out_shape=(quarter,) * (SECTIONS - 1),
        grid_spec=pltpu.PrefetchScalarGridSpec(
            num_scalar_prefetch=1,
            grid=(1,),
            in_specs=[slab_of(k) for k in range(1, SECTIONS)],
            out_specs=[fixed((ROWS, SLAB))] * (SECTIONS - 1),
        ),
    )(section, stash, stash, stash)


def gather_kernel(s, other3, other2, other1, own, cotangent, x, top):
    for k, part in enumerate((own, other1, other2, other3)):
        x[s[0] ^ k] = part[...]
    top[...] = cotangent[...]


def gather(section, stash, others, cotangent):
    return call(
        gather_kernel,
        "gather",
        weight=0,
        out_shape=(
            jax.ShapeDtypeStruct((SECTIONS, ROWS, SLAB), BF),
            jax.ShapeDtypeStruct((ROWS, SLAB), BF),
        ),
        grid_spec=pltpu.PrefetchScalarGridSpec(
            num_scalar_prefetch=1,
            grid=(1,),
            in_specs=[fixed((ROWS, SLAB))] * (SECTIONS - 1) + [slab_of(0)] * 2,
            out_specs=[fixed((SECTIONS, ROWS, SLAB)), fixed((ROWS, SLAB))],
        ),
    )(section, *others[::-1], stash, cotangent)


def layers_kernel(s, own, top, got, x, out, send, above, kernel, offsets, tile):
    @pl.when(pl.program_id(0) == 0)
    def _():
        above[...] = top[...]

    domain = own[0]
    biases = got[0, PIECE:, :].astype(F32)
    for i in range(1, NX):
        biases = biases + got[i, PIECE:, :].astype(F32)
    offsets[...] = biases
    for z in range(NZ):
        for i in range(NX):
            at = (z * NX + i) * SHARD
            kernel[at : at + SHARD, :] = got[i, z * SHARD : (z + 1) * SHARD, :]
    tile[...] = jnp.zeros_like(tile)
    for q in range(SG):
        lanes = slice(q * GS, (q + 1) * GS)
        inputs, weights = x[0, :, lanes], kernel[lanes, :]
        offset = offsets[q : q + 1, :] + offsets[pl.ds((1 + domain) * SG + q, 1), :]
        pre = jnp.dot(inputs, weights, preferred_element_type=F32) + offset
        sigma = jax.nn.sigmoid(pre)
        slope = sigma * (1.0 + pre * (1.0 - sigma))
        incoming = above[:, lanes].astype(F32)
        signal = (incoming * slope).astype(BF)
        back = lax.dot_general(
            signal, weights, (((1,), (1,)), ((), ())), preferred_element_type=F32
        )
        outgoing = (incoming + back).astype(BF)
        out[0, :, lanes] = outgoing
        above[:, lanes] = outgoing
        grad = lax.dot_general(
            inputs, signal, (((0,), (0,)), ((), ())), preferred_element_type=F32
        ).astype(BF)
        for row in range(q * GS, (q + 1) * GS, TILE):
            shard, inner = row // SHARD, row % SHARD
            at = shard // NX * SHARD + inner
            send[shard % NX, at : at + TILE, :] = grad[row - q * GS : row - q * GS + TILE]
        total = jnp.sum(signal.astype(F32), axis=0, keepdims=True)
        high = total.astype(BF).astype(F32)
        tile[q : q + 1, :] = high
        tile[SG + q : SG + q + 1, :] = total - high
    for i in range(NX):
        send[i, PIECE:, :] = tile[...].astype(BF)


def layers(section, own, top, got, x):
    last = SECTIONS - 1
    block = pl.BlockSpec((NX, BLOCK, GS), lambda i, s, d: (last - i, 0, 0))
    return call(
        layers_kernel,
        "layers",
        out_shape=(
            pltpu.HBM((SECTIONS, ROWS, SLAB), BF),
            jax.ShapeDtypeStruct((SECTIONS * NX, BLOCK, GS), BF),
        ),
        grid_spec=pltpu.PrefetchScalarGridSpec(
            num_scalar_prefetch=2,
            grid=(SECTIONS,),
            in_specs=[
                pl.BlockSpec((ROWS, SLAB), lambda i, s, d: (0, 0)),
                block,
                pl.BlockSpec((1, ROWS, SLAB), lambda i, s, d: (last - i, 0, 0)),
            ],
            out_specs=[
                pl.BlockSpec((1, ROWS, SLAB), lambda i, s, d: ((last - i) ^ s[0], 0, 0)),
                block,
            ],
            scratch_shapes=[
                pltpu.VMEM((ROWS, SLAB), BF),
                pltpu.VMEM((SLAB, GS), BF),
                pltpu.VMEM((TILE, GS), F32),
                pltpu.VMEM((TILE, GS), F32),
            ],
        ),
    )(section, own, top, got, x)


def split_kernel(out, *parts):
    for k in range(SECTIONS):
        parts[k][...] = out[k]


def split(out):
    return call(
        split_kernel,
        "split",
        out_shape=(jax.ShapeDtypeStruct((ROWS, SLAB), BF),) * SECTIONS,
        in_specs=[VMEM],
        out_specs=(VMEM,) * SECTIONS,
    )(out)


def join_kernel(s, other3, other2, other1, own, out):
    for k, part in enumerate((own, other1, other2, other3)):

        @pl.when(pl.program_id(0) == k)
        def _(part=part):
            out[...] = part[...]


def join(section, own, others):
    return call(
        join_kernel,
        "join",
        weight=0,
        out_shape=jax.ShapeDtypeStruct((ROWS, D), BF),
        grid_spec=pltpu.PrefetchScalarGridSpec(
            num_scalar_prefetch=1,
            grid=(SECTIONS,),
            in_specs=[fixed((ROWS, SLAB))] * SECTIONS,
            out_specs=pl.BlockSpec((ROWS, SLAB), lambda i, s: (0, i ^ s[1])),
        ),
    )(section, *others[::-1], own)


def merge_kernel(ids, z, got, *refs):
    outs, (total, parts, tile) = refs[:NZ], refs[NZ:]
    step = pl.program_id(0)

    @pl.when(step == 0)
    def _():
        total[...] = jnp.zeros_like(total)

    for i in range(got.shape[0]):
        domain = ids[step * got.shape[0] + i, 0]
        total[domain] += got[i].astype(F32)

    @pl.when(step == 0)
    def _():
        tile[...] = jnp.zeros_like(tile)
        for k in range(DOMAINS):
            for to in range(NZ):
                parts[to, k * SHARD : (k + 1) * SHARD, :] = total[
                    k, to * SHARD : (to + 1) * SHARD, :
                ].astype(BF)
            tile[k * SG : (k + 1) * SG, :] = (
                total[k, PIECE : PIECE + SG, :] + total[k, PIECE + SG : PIECE + 2 * SG, :]
            )
        for k in range(NZ):
            outs[k][:PIECE, :] = parts[(z[0] + k) % NZ]
            outs[k][PIECE:, :] = tile[...].astype(BF)


def merge(ids, z, got):
    return call(
        merge_kernel,
        "merge",
        grid=(1,),
        out_shape=(jax.ShapeDtypeStruct((BLOCK, GS), BF),) * NZ,
        in_specs=[SMEM, SMEM, pl.BlockSpec((NY * NX, BLOCK, GS), lambda i: (i, 0, 0))],
        out_specs=(pl.BlockSpec((BLOCK, GS), lambda i: (0, 0)),) * NZ,
        scratch_shapes=[
            pltpu.VMEM((DOMAINS, BLOCK, GS), F32),
            pltpu.VMEM((NZ, PIECE, GS), BF),
            pltpu.VMEM((TILE, GS), F32),
        ],
    )(ids, z, got)


def finish_kernel(at, *refs):
    got, (sw, dw, d_shared, d_domain, b_shared, b_domain, wide) = refs[:NZ], refs[NZ:]
    shared = sw[...].astype(F32)
    summed = jnp.zeros((SHARD, GS), F32)
    for k in range(DOMAINS):
        part = slice(k * SHARD, (k + 1) * SHARD)
        share = got[0][part, :].astype(F32)
        for z in range(1, NZ):
            share = share + got[z][part, :].astype(F32)
        summed = summed + share * dw[k].astype(F32)
        d_domain[k] = share * shared
    d_shared[...] = summed
    tile = got[0][PIECE:, :].astype(F32)
    for z in range(1, NZ):
        tile = tile + got[z][PIECE:, :].astype(F32)
    wide[...] = jnp.zeros_like(wide)
    for k in range(DOMAINS):
        for q in range(SG):
            row = k * SG + q
            wide[k : k + 1, q * GS : (q + 1) * GS] = tile[row : row + 1, :]
    placed = pltpu.roll(wide[...], SLAB - at[0], 1)
    b_domain[...] = placed[:DOMAINS, :SHARD]
    b_shared[...] = jnp.sum(placed[:DOMAINS, :SHARD], axis=0, keepdims=True)


def finish(at, got, sw, dw):
    return call(
        finish_kernel,
        "finish",
        out_shape=(
            jax.ShapeDtypeStruct((SHARD, GS), F32),
            jax.ShapeDtypeStruct((DOMAINS, SHARD, GS), F32),
            jax.ShapeDtypeStruct((1, SHARD), F32),
            jax.ShapeDtypeStruct((DOMAINS, SHARD), F32),
        ),
        in_specs=[SMEM] + [VMEM] * (NZ + 2),
        out_specs=(VMEM,) * 4,
        scratch_shapes=[pltpu.VMEM((8, SLAB), F32)],
    )(at, got[2], got[1], got[3], got[0], sw, dw)


def exchange(block, axes):
    return lax.all_to_all(block, axes, 0, 0, tiled=True)


def flip(z):
    return z % 2 * 2


def turned(block, k, home):
    pairs = []
    for a in range(SECTIONS):
        for b in range(NY):
            for z in range(NZ):
                later = (z + k) % NZ
                to = (b, a ^ flip(z)) if home else (b ^ flip(later), a)
                pairs.append(((a * NY + b) * NZ + z, (to[0] * NY + to[1]) * NZ + later))
    return lax.ppermute(block, ("zhi", "core", "y", "zlo"), pairs)


def swapped(block, k):
    pairs = [(section, section ^ k) for section in range(SECTIONS)]
    return lax.ppermute(block, ("zhi", "core"), pairs)


def after(first, *then):
    return lax.optimization_barrier((first, *then))[1:]


def body(stash, cotangent, domain_ids, shared_weight, domain_weight, shared_bias, domain_bias):
    stash = stash[0]
    sw, dw = shared_weight[0], domain_weight[0]
    section = 2 * lax.axis_index("zhi") + lax.axis_index("core")
    section = jnp.stack([section, section ^ flip(lax.axis_index("zlo"))])
    z = jnp.reshape(lax.axis_index("zlo"), (1,))
    at = PIECE * z + SHARD * lax.axis_index("x")

    mine, ids = prep(at, domain_ids, sw, dw, shared_bias, domain_bias[0])
    plane_ids = exchange(ids, ("y", "x")).reshape(NY * NX, 128)
    held = [turned(mine, k, False) for k in range(NZ)]
    picked = pick(plane_ids, z, held)
    got = exchange(picked, ("y", "x"))
    (late,) = after(picked, stash)
    parts = cut(section, late)
    others = [swapped(parts[k - 1], k) for k in range(1, SECTIONS)]
    x, top = gather(section, late, others, cotangent)

    out, send = layers(section, domain_ids, top, got, x)
    got = exchange(send, ("y", "x"))
    parts = split(out)
    d_inputs = join(section, parts[0], [swapped(parts[k], k) for k in range(1, SECTIONS)])
    (got,) = after(d_inputs, got)
    merged = merge(plane_ids, z, got)
    final = [turned(merged[k], k, True) for k in range(NZ)]
    d_shared, d_domain, b_shared, b_domain = finish(at, final, sw, dw)
    return (d_inputs[None], d_shared[None], d_domain[None], b_shared, b_domain[None])


def solution(mesh):
    fine = Mesh(mesh.devices.reshape(2, 2, NY, NZ, NX), ("zhi", "core", "y", "zlo", "x"))
    section, dp = ("zhi", "core"), ("y", "zlo", "x")
    in_specs = (
        P(section, dp, None),
        P(dp, None),
        P(dp),
        P(section, dp, None),
        P(section, None, dp, None),
        P(section, dp),
        P(section, None, dp),
    )
    out_specs = (
        P(section, dp, None),
        P(section, dp, None),
        P(section, None, dp, None),
        P(section, dp),
        P(section, None, dp),
    )
    return jax.shard_map(
        body, mesh=fine, in_specs=in_specs, out_specs=out_specs, check_vma=False
    )
```

```python
import jax
import jax.numpy as jnp
from jax import lax
from jax.experimental import pallas as pl
from jax.experimental.pallas import tpu as pltpu
from jax.sharding import Mesh, PartitionSpec as P

D = 3072
GS = 256
DOMAINS = 4
ROWS = 128
NY, NZ, NX = 4, 4, 4
SHARD = 48
SLAB = D // NY
SG = SLAB // GS
SECTIONS = 4
PIECE = NZ * SHARD
TILE = 16
BLOCK = PIECE + TILE
VMEM = pl.BlockSpec(memory_space=pltpu.VMEM)
SMEM = pl.BlockSpec(memory_space=pltpu.SMEM)
BF = jnp.bfloat16
F32 = jnp.float32
HEAVY = 10**11


def call(kernel, name, limit=48, weight=HEAVY, **rest):
    return pl.pallas_call(
        kernel,
        name=name,
        compiler_params=pltpu.CompilerParams(vmem_limit_bytes=limit * 1024 * 1024),
        cost_estimate=pl.CostEstimate(
            flops=weight, bytes_accessed=weight // 100, transcendentals=0
        ),
        **rest,
    )


def prep_kernel(at, own, sw, dw, sb, db, out, ids, wide, tile):
    ids[...] = jnp.full(ids.shape, own[0], jnp.int32)
    shared = sw[...].astype(F32)
    for k in range(DOMAINS):
        out[k * SHARD : (k + 1) * SHARD, :] = (shared * dw[k].astype(F32)).astype(BF)
    wide[...] = jnp.zeros_like(wide)
    wide[0:1, :SHARD] = sb[...].astype(F32)
    wide[1 : 1 + DOMAINS, :SHARD] = db[...].astype(F32)
    placed = pltpu.roll(wide[...], at[0], 1)
    tile[...] = jnp.zeros_like(tile)
    for k in range(1 + DOMAINS):
        for q in range(SG):
            row = k * SG + q
            tile[row : row + 1, :] = placed[k : k + 1, q * GS : (q + 1) * GS]
    out[PIECE:, :] = tile[...].astype(BF)


def prep(at, own, sw, dw, sb, db):
    return call(
        prep_kernel,
        "prep",
        limit=58,
        out_shape=(
            jax.ShapeDtypeStruct((BLOCK, GS), BF),
            jax.ShapeDtypeStruct((NY * NX, 1, 128), jnp.int32),
        ),
        in_specs=[SMEM, SMEM, VMEM, VMEM, VMEM, VMEM],
        out_specs=(VMEM, VMEM),
        scratch_shapes=[pltpu.VMEM((8, SLAB), F32), pltpu.VMEM((TILE, GS), F32)],
    )(at, own, sw, dw, sb, db)


def pick_kernel(ids, z, *refs):
    held, out, ready = [refs[0], refs[1], refs[3], refs[2]], refs[NZ], refs[NZ + 1]
    step = pl.program_id(0)
    tile = held[0][PIECE:, :].astype(F32)
    for k in range(1, NZ):
        tile = tile + held[k][PIECE:, :].astype(F32)
    tile = tile.astype(BF)
    for k in range(NZ):
        to = pl.multiple_of(((z[0] + NZ - k) % NZ) * SHARD, TILE)
        for d in range(DOMAINS):
            ready[d, pl.ds(to, SHARD), :] = held[k][d * SHARD : (d + 1) * SHARD, :]
    for d in range(DOMAINS):
        ready[d, PIECE:, :] = tile
    for i in range(out.shape[0]):
        out[i] = ready[ids[step * out.shape[0] + i, 0]]


def pick(ids, z, held):
    return call(
        pick_kernel,
        "pick",
        grid=(1,),
        out_shape=jax.ShapeDtypeStruct((NY * NX, BLOCK, GS), BF),
        in_specs=[SMEM, SMEM] + [pl.BlockSpec((BLOCK, GS), lambda i: (0, 0))] * NZ,
        out_specs=pl.BlockSpec((NY * NX, BLOCK, GS), lambda i: (i, 0, 0)),
        scratch_shapes=[pltpu.VMEM((DOMAINS, BLOCK, GS), BF)],
    )(ids, z, held[0], held[1], held[3], held[2])


def fixed(shape):
    return pl.BlockSpec(shape, lambda i, s: (0,) * len(shape))


def slab_of(k):
    return pl.BlockSpec((ROWS, SLAB), lambda i, s: (0, s[1] ^ k))


def cut_kernel(s, *refs):
    for k in range(1, SECTIONS):
        refs[SECTIONS - 2 + k][...] = refs[k - 1][...]


def cut(section, stash):
    quarter = jax.ShapeDtypeStruct((ROWS, SLAB), BF)
    return call(
        cut_kernel,
        "cut",
        out_shape=(quarter,) * (SECTIONS - 1),
        grid_spec=pltpu.PrefetchScalarGridSpec(
            num_scalar_prefetch=1,
            grid=(1,),
            in_specs=[slab_of(k) for k in range(1, SECTIONS)],
            out_specs=[fixed((ROWS, SLAB))] * (SECTIONS - 1),
        ),
    )(section, stash, stash, stash)


def gather_kernel(s, other3, other2, other1, own, cotangent, x, top):
    for k, part in enumerate((own, other1, other2, other3)):
        x[s[0] ^ k] = part[...]
    top[...] = cotangent[...]


def gather(section, stash, others, cotangent):
    return call(
        gather_kernel,
        "gather",
        weight=0,
        out_shape=(
            jax.ShapeDtypeStruct((SECTIONS, ROWS, SLAB), BF),
            jax.ShapeDtypeStruct((ROWS, SLAB), BF),
        ),
        grid_spec=pltpu.PrefetchScalarGridSpec(
            num_scalar_prefetch=1,
            grid=(1,),
            in_specs=[fixed((ROWS, SLAB))] * (SECTIONS - 1) + [slab_of(0)] * 2,
            out_specs=[fixed((SECTIONS, ROWS, SLAB)), fixed((ROWS, SLAB))],
        ),
    )(section, *others[::-1], stash, cotangent)


def layers_kernel(s, own, top, got, x, out, send, above, kernel, offsets, tile):
    @pl.when(pl.program_id(0) == 0)
    def _():
        above[...] = top[...]

    domain = own[0]
    biases = got[0, PIECE:, :].astype(F32)
    for i in range(1, NX):
        biases = biases + got[i, PIECE:, :].astype(F32)
    offsets[...] = biases
    for z in range(NZ):
        for i in range(NX):
            at = (z * NX + i) * SHARD
            kernel[at : at + SHARD, :] = got[i, z * SHARD : (z + 1) * SHARD, :]
    tile[...] = jnp.zeros_like(tile)
    for q in range(SG):
        lanes = slice(q * GS, (q + 1) * GS)
        inputs, weights = x[0, :, lanes], kernel[lanes, :]
        offset = offsets[q : q + 1, :] + offsets[pl.ds((1 + domain) * SG + q, 1), :]
        pre = jnp.dot(inputs, weights, preferred_element_type=F32) + offset
        sigma = jax.nn.sigmoid(pre)
        slope = sigma * (1.0 + pre * (1.0 - sigma))
        incoming = above[:, lanes].astype(F32)
        signal = (incoming * slope).astype(BF)
        back = lax.dot_general(
            signal, weights, (((1,), (1,)), ((), ())), preferred_element_type=F32
        )
        outgoing = (incoming + back).astype(BF)
        out[0, :, lanes] = outgoing
        above[:, lanes] = outgoing
        grad = lax.dot_general(
            inputs, signal, (((0,), (0,)), ((), ())), preferred_element_type=F32
        ).astype(BF)
        for row in range(q * GS, (q + 1) * GS, TILE):
            shard, inner = row // SHARD, row % SHARD
            at = shard // NX * SHARD + inner
            send[shard % NX, at : at + TILE, :] = grad[row - q * GS : row - q * GS + TILE]
        total = jnp.sum(signal.astype(F32), axis=0, keepdims=True)
        high = total.astype(BF).astype(F32)
        tile[q : q + 1, :] = high
        tile[SG + q : SG + q + 1, :] = total - high
    for i in range(NX):
        send[i, PIECE:, :] = tile[...].astype(BF)


def layers(section, own, top, got, x):
    last = SECTIONS - 1
    block = pl.BlockSpec((NX, BLOCK, GS), lambda i, s, d: (last - i, 0, 0))
    return call(
        layers_kernel,
        "layers",
        out_shape=(
            pltpu.HBM((SECTIONS, ROWS, SLAB), BF),
            jax.ShapeDtypeStruct((SECTIONS * NX, BLOCK, GS), BF),
        ),
        grid_spec=pltpu.PrefetchScalarGridSpec(
            num_scalar_prefetch=2,
            grid=(SECTIONS,),
            in_specs=[
                pl.BlockSpec((ROWS, SLAB), lambda i, s, d: (0, 0)),
                block,
                pl.BlockSpec((1, ROWS, SLAB), lambda i, s, d: (last - i, 0, 0)),
            ],
            out_specs=[
                pl.BlockSpec((1, ROWS, SLAB), lambda i, s, d: ((last - i) ^ s[0], 0, 0)),
                block,
            ],
            scratch_shapes=[
                pltpu.VMEM((ROWS, SLAB), BF),
                pltpu.VMEM((SLAB, GS), BF),
                pltpu.VMEM((TILE, GS), F32),
                pltpu.VMEM((TILE, GS), F32),
            ],
        ),
    )(section, own, top, got, x)


def split_kernel(out, *parts):
    for k in range(SECTIONS):
        parts[k][...] = out[k]


def split(out):
    return call(
        split_kernel,
        "split",
        out_shape=(jax.ShapeDtypeStruct((ROWS, SLAB), BF),) * SECTIONS,
        in_specs=[VMEM],
        out_specs=(VMEM,) * SECTIONS,
    )(out)


def join_kernel(s, other3, other2, other1, own, out):
    for k, part in enumerate((own, other1, other2, other3)):

        @pl.when(pl.program_id(0) == k)
        def _(part=part):
            out[...] = part[...]


def join(section, own, others):
    return call(
        join_kernel,
        "join",
        weight=0,
        out_shape=jax.ShapeDtypeStruct((ROWS, D), BF),
        grid_spec=pltpu.PrefetchScalarGridSpec(
            num_scalar_prefetch=1,
            grid=(SECTIONS,),
            in_specs=[fixed((ROWS, SLAB))] * SECTIONS,
            out_specs=pl.BlockSpec((ROWS, SLAB), lambda i, s: (0, i ^ s[1])),
        ),
    )(section, *others[::-1], own)


def merge_kernel(ids, z, got, *refs):
    outs, (total, parts, tile) = refs[:NZ], refs[NZ:]
    step = pl.program_id(0)

    @pl.when(step == 0)
    def _():
        total[...] = jnp.zeros_like(total)

    for i in range(got.shape[0]):
        domain = ids[step * got.shape[0] + i, 0]
        total[domain] += got[i].astype(F32)

    @pl.when(step == 0)
    def _():
        tile[...] = jnp.zeros_like(tile)
        for k in range(DOMAINS):
            for to in range(NZ):
                parts[to, k * SHARD : (k + 1) * SHARD, :] = total[
                    k, to * SHARD : (to + 1) * SHARD, :
                ].astype(BF)
            tile[k * SG : (k + 1) * SG, :] = (
                total[k, PIECE : PIECE + SG, :] + total[k, PIECE + SG : PIECE + 2 * SG, :]
            )
        for k in range(NZ):
            outs[k][:PIECE, :] = parts[(z[0] + k) % NZ]
            outs[k][PIECE:, :] = tile[...].astype(BF)


def merge(ids, z, got):
    return call(
        merge_kernel,
        "merge",
        grid=(1,),
        out_shape=(jax.ShapeDtypeStruct((BLOCK, GS), BF),) * NZ,
        in_specs=[SMEM, SMEM, pl.BlockSpec((NY * NX, BLOCK, GS), lambda i: (i, 0, 0))],
        out_specs=(pl.BlockSpec((BLOCK, GS), lambda i: (0, 0)),) * NZ,
        scratch_shapes=[
            pltpu.VMEM((DOMAINS, BLOCK, GS), F32),
            pltpu.VMEM((NZ, PIECE, GS), BF),
            pltpu.VMEM((TILE, GS), F32),
        ],
    )(ids, z, got)


def finish_kernel(at, *refs):
    got, (sw, dw, d_shared, d_domain, b_shared, b_domain, wide) = refs[:NZ], refs[NZ:]
    shared = sw[...].astype(F32)
    summed = jnp.zeros((SHARD, GS), F32)
    for k in range(DOMAINS):
        part = slice(k * SHARD, (k + 1) * SHARD)
        share = got[0][part, :].astype(F32)
        for z in range(1, NZ):
            share = share + got[z][part, :].astype(F32)
        summed = summed + share * dw[k].astype(F32)
        d_domain[k] = share * shared
    d_shared[...] = summed
    tile = got[0][PIECE:, :].astype(F32)
    for z in range(1, NZ):
        tile = tile + got[z][PIECE:, :].astype(F32)
    wide[...] = jnp.zeros_like(wide)
    for k in range(DOMAINS):
        for q in range(SG):
            row = k * SG + q
            wide[k : k + 1, q * GS : (q + 1) * GS] = tile[row : row + 1, :]
    placed = pltpu.roll(wide[...], SLAB - at[0], 1)
    b_domain[...] = placed[:DOMAINS, :SHARD]
    b_shared[...] = jnp.sum(placed[:DOMAINS, :SHARD], axis=0, keepdims=True)


def finish(at, got, sw, dw):
    return call(
        finish_kernel,
        "finish",
        out_shape=(
            jax.ShapeDtypeStruct((SHARD, GS), F32),
            jax.ShapeDtypeStruct((DOMAINS, SHARD, GS), F32),
            jax.ShapeDtypeStruct((1, SHARD), F32),
            jax.ShapeDtypeStruct((DOMAINS, SHARD), F32),
        ),
        in_specs=[SMEM] + [VMEM] * (NZ + 2),
        out_specs=(VMEM,) * 4,
        scratch_shapes=[pltpu.VMEM((8, SLAB), F32)],
    )(at, got[2], got[1], got[3], got[0], sw, dw)


def exchange(block, axes):
    return lax.all_to_all(block, axes, 0, 0, tiled=True)


def flip(z):
    return z % 2 * 2


def turned(block, k, home):
    pairs = []
    for a in range(SECTIONS):
        for b in range(NY):
            for z in range(NZ):
                later = (z + k) % NZ
                to = (b, a ^ flip(z)) if home else (b ^ flip(later), a)
                pairs.append(((a * NY + b) * NZ + z, (to[0] * NY + to[1]) * NZ + later))
    return lax.ppermute(block, ("zhi", "core", "y", "zlo"), pairs)


def swapped(block, k):
    pairs = [(section, section ^ k) for section in range(SECTIONS)]
    return lax.ppermute(block, ("zhi", "core"), pairs)


def after(first, *then):
    return lax.optimization_barrier((first, *then))[1:]


def body(stash, cotangent, domain_ids, shared_weight, domain_weight, shared_bias, domain_bias):
    stash = stash[0]
    sw, dw = shared_weight[0], domain_weight[0]
    section = 2 * lax.axis_index("zhi") + lax.axis_index("core")
    section = jnp.stack([section, section ^ flip(lax.axis_index("zlo"))])
    z = jnp.reshape(lax.axis_index("zlo"), (1,))
    at = PIECE * z + SHARD * lax.axis_index("x")

    mine, ids = prep(at, domain_ids, sw, dw, shared_bias, domain_bias[0])
    plane_ids = exchange(ids, ("y", "x")).reshape(NY * NX, 128)
    held = [turned(mine, k, False) for k in range(NZ)]
    picked = pick(plane_ids, z, held)
    got = exchange(picked, ("y", "x"))
    (late,) = after(picked, stash)
    parts = cut(section, late)
    others = [swapped(parts[k - 1], k) for k in range(1, SECTIONS)]
    x, top = gather(section, late, others, cotangent)

    out, send = layers(section, domain_ids, top, got, x)
    got = exchange(send, ("y", "x"))
    parts = split(out)
    d_inputs = join(section, parts[0], [swapped(parts[k], k) for k in range(1, SECTIONS)])
    (got,) = after(d_inputs, got)
    merged = merge(plane_ids, z, got)
    final = [turned(merged[k], k, True) for k in range(NZ)]
    d_shared, d_domain, b_shared, b_domain = finish(at, final, sw, dw)
    return (d_inputs[None], d_shared[None], d_domain[None], b_shared, b_domain[None])


def solution(mesh):
    fine = Mesh(mesh.devices.reshape(2, 2, NY, NZ, NX), ("zhi", "core", "y", "zlo", "x"))
    section, dp = ("zhi", "core"), ("y", "zlo", "x")
    in_specs = (
        P(section, dp, None),
        P(dp, None),
        P(dp),
        P(section, dp, None),
        P(section, None, dp, None),
        P(section, dp),
        P(section, None, dp),
    )
    out_specs = (
        P(section, dp, None),
        P(section, dp, None),
        P(section, None, dp, None),
        P(section, dp),
        P(section, None, dp),
    )
    return jax.shard_map(
        body, mesh=fine, in_specs=in_specs, out_specs=out_specs, check_vma=False
    )
```
